32 devices in a mesh: dp: 8 (over z, y), head: 4 (over x, core).
Axes of the slice: x: 2, y: 2, z: 4, core: 2. Of those that a mesh axis runs over, the one named last changes fastest.
Arguments:
- tokens: bfloat16 [8, 2048, 512], P('dp', 'head'), may hold values from -6 to 6
- memory: bfloat16 [8, 1024, 512], P('dp', 'head'), may hold values from -6 to 6
- lengths: int32 [8], P('dp'), may hold values from 256 to 2048, as said below
- self_qkv: bfloat16 [512, 1536], replicated, may hold values from -0.25 to 0.25
- self_out: bfloat16 [512, 512], replicated, may hold values from -6 to 6
- cross_q: bfloat16 [512, 512], replicated, may hold values from -0.25 to 0.25
- cross_kv: bfloat16 [512, 1024], replicated, may hold values from -0.25 to 0.25
- cross_out: bfloat16 [512, 512], replicated, may hold values from -6 to 6
- ffn_in: bfloat16 [512, 2048], replicated, may hold values from -0.25 to 0.25
- ffn_in_bias: bfloat16 [2048], replicated, may hold values from -3 to 3
- ffn_out: bfloat16 [2048, 512], replicated, may hold values from -0.125 to 0.125
- ffn_out_bias: bfloat16 [512], replicated, may hold values from -3 to 3
- slot_weight: bfloat16 [1024, 512], replicated, may hold values from -0.1875 to 0.1875
- slot_bias: bfloat16 [512], replicated, may hold values from -3 to 3
- norm_gain: float32 [3, 512], replicated, may hold values from 0.5 to 1.5
- norm_shift: float32 [3, 512], replicated, may hold values from -3 to 3
- cotangent: bfloat16 [8, 2048, 512], P('dp', 'head'), may hold values from -6 to 6
Outputs:
- slots: bfloat16 [8, 2048, 512], P('dp', 'head')
- token_grad: bfloat16 [8, 2048, 512], P('dp', 'head')
- memory_grad: bfloat16 [8, 1024, 512], P('dp', 'head')
- self_qkv_grad: float32 [512, 1536], replicated
- self_out_grad: float32 [512, 512], replicated
- cross_q_grad: float32 [512, 512], replicated
- cross_kv_grad: float32 [512, 1024], replicated
- cross_out_grad: float32 [512, 512], replicated
- ffn_in_grad: float32 [512, 2048], replicated
- ffn_in_bias_grad: float32 [2048], replicated
- ffn_out_grad: float32 [2048, 512], replicated
- ffn_out_bias_grad: float32 [512], replicated
- slot_weight_grad: float32 [1024, 512], replicated
- slot_bias_grad: float32 [512], replicated
- norm_gain_grad: float32 [3, 512], replicated
- norm_shift_grad: float32 [3, 512], replicated
The draws below stay inside these ranges and needn't reach their ends.
Inputs may be any that keep to these rules, and one draw needn't show every extreme that they name: `lengths`: some canvas has exactly 2048 live tokens, and another exactly 256.
All inputs are finite; a program needn't handle non-finite values.
Results may differ from the reference program's by a relative error of at most 0.025.
Values may be sent and summed in bfloat16 or wider, within the bound.
No kernel may reach another device: no remote copies, remote signals or barrier semaphores. Data moves between devices by JAX's collectives and lax.ppermute only.
A program may use at most 128 MiB of HBM per device.

```python
import jax
import jax.numpy as jnp
from jax import lax

D = 512
HEADS = 8
HEAD_DIM = 64
FF = 2048
LEN = 2048
SRC = 1024
CANV = 8


def draw_lengths(key, part):
    key = jax.random.fold_in(key, 11)
    key_base, key_widest, key_offset = jax.random.split(key, 3)
    drawn = jax.random.randint(key_base, (CANV,), LEN // 8, LEN + 1)
    widest = jax.random.randint(key_widest, (), 0, CANV)
    offset = jax.random.randint(key_offset, (), 1, CANV)
    shortest = (widest + offset) % CANV
    indices = jnp.arange(CANV, dtype=jnp.int32)
    result = jnp.where(indices == widest, LEN, drawn)
    result = jnp.where(indices == shortest, LEN // 8, result)
    return result.astype(jnp.int32)


def level_of(stream_key, extent, cuts, least, high):
    level = 1.0
    for dim, shards_of in cuts:
        draws = jax.random.uniform(jax.random.fold_in(jax.random.fold_in(stream_key, 6), dim), (shards_of,), jnp.float32, least / len(cuts), high / len(cuts))
        level = level * jnp.repeat(jnp.exp(draws), extent[dim] // shards_of).reshape((-1,) + (1,) * (len(extent) - 1 - dim))
    return level


def bell_draw(stream_key, extent, scale, most, shards=(), held_as=jnp.bfloat16):
    loudness = level_of(stream_key, extent, shards, -0.22, 0.18) if shards else 1.0
    values = jax.random.normal(stream_key, extent, jnp.float32) * scale * loudness
    return jnp.minimum(jnp.maximum(values, -most), most).astype(held_as)


def setup_inputs(seed: int = 0) -> dict:
    splits = jax.random.split(jax.random.key(seed), 18)
    tokens = bell_draw(splits[0], (CANV, LEN, D), 1.0, 6.0, ((0, 8), (1, 4)))
    memory = bell_draw(splits[1], (CANV, SRC, D), 1.0, 6.0, ((0, 8), (1, 4)))
    lengths = draw_lengths(jax.random.fold_in(splits[17], 71), 0)
    self_qkv = bell_draw(splits[3], (D, 3 * D), D ** -0.5, 0.25)
    self_out = bell_draw(splits[4], (D, D), (max(1, 2 * D // LEN)) ** -0.5, 6.0)
    cross_q = bell_draw(splits[5], (D, D), D ** -0.5, 0.25)
    cross_kv = bell_draw(splits[6], (D, 2 * D), D ** -0.5, 0.25)
    cross_out = bell_draw(splits[7], (D, D), (max(1, 2 * D // SRC)) ** -0.5, 6.0)
    ffn_in = bell_draw(splits[8], (D, FF), D ** -0.5, 0.25)
    ffn_in_bias = bell_draw(splits[9], (FF,), 0.3, 3.0)
    ffn_out = bell_draw(splits[10], (FF, D), FF ** -0.5, 0.125)
    ffn_out_bias = bell_draw(splits[11], (D,), 0.3, 3.0)
    slot_weight = bell_draw(splits[12], (2 * D, D), (2 * D) ** -0.5, 0.1875)
    slot_bias = bell_draw(splits[13], (D,), 0.3, 3.0)
    norm_gain = jnp.clip(1.0 + 0.1 * jax.random.normal(splits[14], (3, D), jnp.float32), 0.5, 1.5)
    norm_shift = bell_draw(splits[15], (3, D), 0.3, 3.0, (), jnp.float32)
    cotangent = bell_draw(splits[16], (CANV, LEN, D), 1.0, 6.0, ((0, 8), (1, 4)))
    return {"tokens": tokens, "memory": memory, "lengths": lengths, "self_qkv": self_qkv, "self_out": self_out, "cross_q": cross_q, "cross_kv": cross_kv, "cross_out": cross_out, "ffn_in": ffn_in, "ffn_in_bias": ffn_in_bias, "ffn_out": ffn_out, "ffn_out_bias": ffn_out_bias, "slot_weight": slot_weight, "slot_bias": slot_bias, "norm_gain": norm_gain, "norm_shift": norm_shift, "cotangent": cotangent}


@jax.custom_vjp
def low(v):
    return lax.optimization_barrier(v.astype(jnp.bfloat16)).astype(jnp.float32)

@jax.custom_vjp
def low_back(v):
    return v

def low_keep(v):
    return (low(v), None)

def low_pass(kept, grad):
    return (grad,)

def back_keep(v):
    return (v, None)

def back_low(kept, grad):
    return (low(grad),)
low.defvjp(low_keep, low_pass)
low_back.defvjp(back_keep, back_low)
epsilon = 1e-05
masked_score = -1e+30

def product(operand, matrix):
    return jnp.matmul(operand, matrix, precision=lax.Precision.HIGHEST)

def layer_norm(values, gain, shift):
    centred = values - lax.optimization_barrier(jnp.mean(values, axis=-1, keepdims=True))
    spread = lax.optimization_barrier(jnp.mean(centred * centred, axis=-1, keepdims=True))
    return centred * lax.rsqrt(spread + epsilon) * gain + shift

def attend_canvas(queries, key_rows, value_rows, live_keys):
    row_count = queries.shape[0]
    block_rows = min(512, row_count)
    query_blocks = queries.reshape(row_count // block_rows, block_rows, HEADS, HEAD_DIM)

    def one_block(query_block):
        scores = jnp.einsum('qhe,khe->hqk', query_block, key_rows, precision=lax.Precision.HIGHEST) * HEAD_DIM ** (-0.5)
        scores = jnp.where(live_keys[None, None, :], scores, masked_score)
        scores = low_back(scores)
        attn_prob = jax.nn.softmax(scores, axis=-1)
        return jnp.einsum('hqk,khe->qhe', low(attn_prob), value_rows, precision=lax.Precision.HIGHEST)
    return lax.map(jax.checkpoint(one_block), query_blocks).reshape(row_count, D)

def attention(queries, key_rows, value_rows, live_keys):

    def per_canvas(packed):
        query_part, key_part, value_part, live_part = packed
        return attend_canvas(query_part, key_part.reshape(-1, HEADS, HEAD_DIM), value_part.reshape(-1, HEADS, HEAD_DIM), live_part)
    return lax.map(jax.checkpoint(per_canvas), (queries, key_rows, value_rows, live_keys))

def forward_layer(tokens, memory, self_qkv, self_out, cross_q, cross_kv, cross_out, ffn_in, ffn_in_bias, ffn_out, ffn_out_bias, slot_weight, slot_bias, norm_gain, norm_shift, lengths):
    positions = jnp.arange(LEN, dtype=jnp.int32)
    live_keys = positions[None, :] < lengths[:, None]
    memory_live = jnp.zeros((memory.shape[0], SRC), jnp.int32) == 0
    projected = low_back(low(product(tokens, self_qkv)))
    context = low_back(low(attention(projected[..., :D], projected[..., D:2 * D], projected[..., 2 * D:], live_keys)))
    branch = low_back(product(context, self_out))
    first_norm = layer_norm(tokens + branch, norm_gain[0], norm_shift[0])
    cross_queries = low_back(low(product(low(first_norm), cross_q)))
    memory_proj = low_back(low(product(memory, cross_kv)))
    cross_context = low_back(low(attention(cross_queries, memory_proj[..., :D], memory_proj[..., D:], memory_live)))
    cross_branch = low_back(product(cross_context, cross_out))
    second_norm = layer_norm(first_norm + cross_branch, norm_gain[1], norm_shift[1])
    hidden_pre = low_back(product(low(second_norm), ffn_in) + ffn_in_bias)
    hidden_act = low(jax.nn.gelu(hidden_pre))
    ffn_branch = low_back(product(hidden_act, ffn_out) + ffn_out_bias)
    third_norm = layer_norm(second_norm + ffn_branch, norm_gain[2], norm_shift[2])
    rounded = low(third_norm)
    following = jnp.concatenate([rounded[:, 1:], jnp.zeros_like(rounded[:, :1])], axis=1)
    slot_pre = low_back(product(rounded, slot_weight[:D]) + product(following, slot_weight[D:]) + slot_bias)
    live_slots = positions[None, :] < lengths[:, None] - 1
    return jnp.where(live_slots[..., None], slot_pre, 0.0)

def reference(tokens, memory, lengths, self_qkv, self_out, cross_q, cross_kv, cross_out, ffn_in, ffn_in_bias, ffn_out, ffn_out_bias, slot_weight, slot_bias, norm_gain, norm_shift, cotangent):
    floats = tuple((array_in.astype(jnp.float32) for array_in in (tokens, memory, self_qkv, self_out, cross_q, cross_kv, cross_out, ffn_in, ffn_in_bias, ffn_out, ffn_out_bias, slot_weight, slot_bias, norm_gain, norm_shift)))

    def closed(*inputs):
        return forward_layer(*inputs, lengths)
    slot_values, pullback = jax.vjp(closed, *floats)
    grads = pullback(cotangent.astype(jnp.float32))
    return (slot_values.astype(jnp.bfloat16), grads[0].astype(jnp.bfloat16), grads[1].astype(jnp.bfloat16), grads[2], grads[3], grads[4], grads[5], grads[6], grads[7], grads[8], grads[9], grads[10], grads[11], grads[12], grads[13], grads[14])
```

```python
import jax
import jax.numpy as jnp
import numpy as np
from jax import lax
from jax.experimental import pallas as pl
from jax.experimental.pallas import tpu as pltpu
from jax.sharding import PartitionSpec as P

HEAD_DIM = 64
WIDE = 128
epsilon = 1e-05
masked_score = -1e30
log2_e = 1.4426950408889634
f32 = jnp.float32
bf16 = jnp.bfloat16


def dot(a, b, ca=1, cb=0):
    return lax.dot_general(a, b, (((ca,), (cb,)), ((), ())), preferred_element_type=f32)


def params(mib=56):
    return pltpu.CompilerParams(vmem_limit_bytes=mib * 2**20)


def in_lanes(base, lane, column):
    high = column.astype(bf16).astype(f32)
    rest = column - high
    middle = rest.astype(bf16).astype(f32)
    low = rest - middle
    base = jnp.where(lane == HEAD_DIM + 1, high, base)
    base = jnp.where(lane == HEAD_DIM + 2, middle, base)
    return jnp.where(lane == HEAD_DIM + 3, low, base)


def attend_forward(queries, keys_t, values_t, extra):
    rows, wide = queries.shape
    heads = wide // WIDE
    block = 256
    count = rows // block

    def kernel(q_ref, k_ref, v_ref, e_ref, o_ref, qa_ref):
        def step(i, carry):
            h = i // count
            at = pl.ds(pl.multiple_of((i % count) * block, block), block)
            lanes = pl.ds(pl.multiple_of(h * WIDE, WIDE), WIDE)
            feats = pl.ds(pl.multiple_of(h * HEAD_DIM, HEAD_DIM), HEAD_DIM)
            lane = lax.broadcasted_iota(jnp.int32, (block, WIDE), 1)
            extra_rows = e_ref[...]
            q = q_ref[at, lanes]
            q = jnp.where(lane == HEAD_DIM, 1.0, q.astype(f32))
            scores = dot(q.astype(bf16), jnp.concatenate([k_ref[feats, :], extra_rows], axis=0))
            top = jnp.max(scores, axis=1, keepdims=True)
            p = jnp.exp2(scores - top)
            total = jnp.sum(p, axis=1, keepdims=True)
            o_t = dot(jnp.concatenate([v_ref[feats, :], extra_rows], axis=0), p.astype(bf16), 1, 1)
            o_t = o_t / o_t[HEAD_DIM + 1 : HEAD_DIM + 2, :]
            sub = lax.broadcasted_iota(jnp.int32, o_t.shape, 0)
            o_t = jnp.where(sub < HEAD_DIM, o_t, 0.0)
            o_ref[at, lanes] = o_t.T.astype(bf16)
            qa_ref[at, lanes] = in_lanes(q, lane, -(top + jnp.log2(total))).astype(bf16)
            return carry

        lax.fori_loop(0, heads * count, step, 0)

    return pl.pallas_call(
        kernel,
        out_shape=(
            jax.ShapeDtypeStruct((rows, wide), bf16),
            jax.ShapeDtypeStruct((rows, wide), bf16),
        ),
        compiler_params=params(),
        name="attend_forward",
    )(queries, keys_t, values_t, extra)


def attend_backward(queries, keys_t, values_t, extra, outs, grads):
    rows, wide = queries.shape
    heads = wide // WIDE
    keys = keys_t.shape[1]
    block = 512
    feat = heads * HEAD_DIM

    def kernel(q_ref, k_ref, v_ref, e_ref, o_ref, g_ref, dq_ref, dk_ref, dv_ref, acc):
        def head(h, carry):
            lanes = pl.ds(pl.multiple_of(h * WIDE, WIDE), WIDE)
            feats = pl.ds(pl.multiple_of(h * HEAD_DIM, HEAD_DIM), HEAD_DIM)
            lane = lax.broadcasted_iota(jnp.int32, (rows, WIDE), 1)
            q = q_ref[:, lanes]
            g = g_ref[:, lanes].astype(f32)
            centre = jnp.sum(g * o_ref[:, lanes].astype(f32), axis=1, keepdims=True)
            ga = in_lanes(g, lane, -centre).astype(bf16)
            q_t = q.T[:HEAD_DIM]
            g_t = g_ref[:, lanes].T[:HEAD_DIM]
            acc[...] = jnp.zeros_like(acc)

            def keyblock(j, c):
                at = pl.ds(pl.multiple_of(j * block, block), block)
                extra_rows = e_ref[:, at]
                k = k_ref[feats, at]
                v = v_ref[feats, at]
                p = jnp.exp2(dot(q, jnp.concatenate([k, extra_rows], axis=0)))
                dp = dot(ga, jnp.concatenate([v, extra_rows], axis=0))
                ds = (p * dp).astype(bf16)
                dv_ref[feats, at] = dot(g_t, p.astype(bf16)).astype(bf16)
                dk_ref[feats, at] = (dot(q_t, ds) * (1.0 / log2_e)).astype(bf16)
                acc[...] += dot(k, ds, 1, 1)
                return c

            lax.fori_loop(0, keys // block, keyblock, 0, unroll=True)
            dq_ref[feats, :] = (acc[...] * HEAD_DIM**-0.5).astype(bf16)
            return carry

        lax.fori_loop(0, heads, head, 0)

    return pl.pallas_call(
        kernel,
        out_shape=(
            jax.ShapeDtypeStruct((feat, rows), bf16),
            jax.ShapeDtypeStruct((feat, keys), bf16),
            jax.ShapeDtypeStruct((feat, keys), bf16),
        ),
        scratch_shapes=[pltpu.VMEM((HEAD_DIM, rows), f32)],
        compiler_params=params(),
        name="attend_backward",
    )(queries, keys_t, values_t, extra, outs, grads)


def swap(block, axis, bit):
    devices = range(lax.axis_size(axis))
    return lax.ppermute(block, axis, [(i, i ^ bit) for i in devices])


def has(axis, bit):
    return (lax.axis_index(axis) // bit) % 2


def halve(block, axis, bit):
    half = block.shape[0] // 2
    mine = has(axis, bit)
    sent = lax.dynamic_slice_in_dim(block, (1 - mine) * half, half)
    kept = lax.dynamic_slice_in_dim(block, mine * half, half)
    return kept, swap(sent, axis, bit)


def double(block, other, axis, bit):
    half = block.shape[0]
    mine = has(axis, bit)
    whole = jnp.zeros((2 * half,) + block.shape[1:], block.dtype)
    whole = lax.dynamic_update_slice_in_dim(whole, block, mine * half, 0)
    return lax.dynamic_update_slice_in_dim(whole, other, (1 - mine) * half, 0)


def add(a, b):
    return (a.astype(f32) + b.astype(f32)).astype(a.dtype)


def sum_rows(block):
    bits = []
    size = 1
    while size < lax.axis_size("dp"):
        bits.append(("dp", size))
        size *= 2
    far = []
    size = 2
    while size < lax.axis_size("head"):
        far.append(("head", size))
        size *= 2
    kept, other = halve(block, "head", 1)
    block = add(kept, other)
    rows = block.shape[0] // 2
    parts = [block[:rows], block[rows:]]
    orders = [far + bits, bits[:1] + far + bits[1:]]
    for n in range(len(orders[0])):
        both = [halve(part, *order[n]) for part, order in zip(parts, orders)]
        parts = [add(kept, other) for kept, other in both]
    for n in reversed(range(len(orders[0]))):
        both = [swap(part, *order[n]) for part, order in zip(parts, orders)]
        parts = [double(p, o, *order[n]) for p, o, order in zip(parts, both, orders)]
    block = jnp.concatenate(parts, axis=0)
    return double(block, swap(block, "head", 1), "head", 1)


def sum_small(block):
    size = 1
    while size < lax.axis_size("head"):
        block = block + swap(block, "head", size)
        size *= 2
    size = 1
    while size < lax.axis_size("dp"):
        block = block + swap(block, "dp", size)
        size *= 2
    return block


def gather_head(block):
    block = double(block, swap(block, "head", 2), "head", 2)
    rows = block.shape[0] // 2
    other = swap(block, "head", 1)
    mine = has("head", 1)
    first = jnp.where(mine == 0, block, other)
    second = jnp.where(mine == 0, other, block)
    return jnp.concatenate([first[:rows], second[:rows], first[rows:], second[rows:]], axis=0)


def scatter_head(partial):
    rows = partial.shape[0] // 4
    blocks = partial.reshape(2, 2, rows, -1)
    core = has("head", 1)
    pair = lax.dynamic_index_in_dim(blocks, core, 1, keepdims=False)
    sent = lax.dynamic_index_in_dim(blocks, 1 - core, 1, keepdims=False)
    pair = add(pair, swap(sent, "head", 1))
    side = has("head", 2)
    own = lax.dynamic_index_in_dim(pair, side, 0, keepdims=False)
    sent = lax.dynamic_index_in_dim(pair, 1 - side, 0, keepdims=False)
    return own.astype(f32) + swap(sent, "head", 2).astype(f32)


def shifted(block, axis, distance):
    devices = range(lax.axis_size(axis))
    route = [(i - distance, i) for i in devices if i - distance in devices]
    return lax.ppermute(block, axis, route)


def normed(values):
    centred = values - jnp.mean(values, axis=-1, keepdims=True)
    spread = jnp.mean(centred * centred, axis=-1, keepdims=True)
    scale = lax.rsqrt(spread + epsilon)
    return centred * scale, scale


def norm_backward(xhat, scale, gain, upstream):
    g = upstream * gain
    dv = scale * (
        g - jnp.mean(g, axis=-1, keepdims=True) - xhat * jnp.mean(g * xhat, axis=-1, keepdims=True)
    )
    return dv, jnp.sum(upstream * xhat, axis=0), jnp.sum(upstream, axis=0)


def pad_heads(matrix, axis):
    shape = list(matrix.shape)
    heads = shape[axis] // HEAD_DIM
    split = shape[:axis] + [heads, HEAD_DIM] + shape[axis + 1 :]
    pads = [(0, 0)] * len(split)
    pads[axis + 1] = (0, WIDE - HEAD_DIM)
    joined = shape[:axis] + [heads * WIDE] + shape[axis + 1 :]
    return jnp.pad(matrix.reshape(split), pads).reshape(joined)


def shards(
    tokens,
    memory,
    lengths,
    self_qkv,
    self_out,
    cross_q,
    cross_kv,
    cross_out,
    ffn_in,
    ffn_in_bias,
    ffn_out,
    ffn_out_bias,
    slot_weight,
    slot_bias,
    norm_gain,
    norm_shift,
    cotangent,
):
    tokens, memory, cotangent, length = tokens[0], memory[0], cotangent[0], lengths[0]
    rows, d = tokens.shape
    all_tokens = gather_head(tokens)
    all_memory = gather_head(memory)
    keys = all_tokens.shape[0]
    sources = all_memory.shape[0]
    positions = lax.axis_index("head") * rows + jnp.arange(rows, dtype=jnp.int32)
    live_slots = (positions < length - 1)[:, None]
    scale = HEAD_DIM**-0.5 * log2_e
    extra_index = jnp.arange(HEAD_DIM)[:, None]
    ones_rows = ((extra_index >= 1) & (extra_index <= 3)).astype(f32)
    dead = (jnp.arange(keys, dtype=jnp.int32) >= length)[None, :]
    self_extra = jnp.where((extra_index == 0) & dead, masked_score, ones_rows).astype(bf16)
    cross_extra = jnp.broadcast_to(ones_rows, (HEAD_DIM, sources)).astype(bf16)

    wq_pad = pad_heads(self_qkv[:, :d], 1)
    wout_pad = pad_heads(self_out, 0)
    cq_pad = pad_heads(cross_q, 1)
    cout_pad = pad_heads(cross_out, 0)

    queries = (dot(tokens, wq_pad) * scale).astype(bf16)
    kv_t = dot(self_qkv[:, d:], all_tokens, 0, 1).astype(bf16)
    keys_t, values_t = kv_t[:d], kv_t[d:]
    context, queries = attend_forward(queries, keys_t, values_t, self_extra)
    first_hat, first_scale = normed(tokens.astype(f32) + dot(context, wout_pad))
    first_norm = first_hat * norm_gain[0] + norm_shift[0]
    first_low = first_norm.astype(bf16)

    cross_queries = (dot(first_low, cq_pad) * scale).astype(bf16)
    mem_t = dot(cross_kv, all_memory, 0, 1).astype(bf16)
    mem_keys_t, mem_values_t = mem_t[:d], mem_t[d:]
    cross_context, cross_queries = attend_forward(
        cross_queries, mem_keys_t, mem_values_t, cross_extra
    )
    second_hat, second_scale = normed(first_norm + dot(cross_context, cout_pad))
    second_norm = second_hat * norm_gain[1] + norm_shift[1]
    second_low = second_norm.astype(bf16)
    hidden_pre = dot(second_low, ffn_in) + ffn_in_bias.astype(f32)
    hidden, gelu_pull = jax.vjp(jax.nn.gelu, hidden_pre)
    hidden_low = hidden.astype(bf16)
    third_hat, third_scale = normed(
        second_norm + dot(hidden_low, ffn_out) + ffn_out_bias.astype(f32)
    )
    third_low = (third_hat * norm_gain[2] + norm_shift[2]).astype(bf16)
    arriving = shifted(third_low[:1], "head", -1)
    following = jnp.concatenate([third_low[1:], arriving], axis=0)
    slot_pre = (
        dot(third_low, slot_weight[:d])
        + dot(following, slot_weight[d:])
        + slot_bias.astype(f32)
    )
    slots = jnp.where(live_slots, slot_pre, 0.0).astype(bf16)

    slot_grad = jnp.where(live_slots, cotangent.astype(f32), 0.0).astype(bf16)
    grad_slot_bias = jnp.sum(slot_grad.astype(f32), axis=0)
    following_grad = dot(slot_grad, slot_weight[d:], 1, 1)
    carried = shifted(following_grad[-1:], "head", 1)
    third_grad = dot(slot_grad, slot_weight[:d], 1, 1) + jnp.concatenate(
        [carried, following_grad[:-1]], axis=0
    )
    third_in_grad, gain_late, shift_late = norm_backward(
        third_hat, third_scale, norm_gain[2], third_grad
    )
    ffn_grad = third_in_grad.astype(bf16)
    grad_out_bias = jnp.sum(ffn_grad.astype(f32), axis=0)
    hidden_grad = gelu_pull(dot(ffn_grad, ffn_out, 1, 1))[0].astype(bf16)
    grad_in_bias = jnp.sum(hidden_grad.astype(f32), axis=0)
    late = sum_rows(
        jnp.concatenate(
            [
                dot(third_low, slot_grad, 0, 0).astype(bf16),
                dot(following, slot_grad, 0, 0).astype(bf16),
                dot(hidden_low, ffn_grad, 0, 0).astype(bf16),
                dot(hidden_grad, second_low, 0, 0).astype(bf16),
            ],
            axis=0,
        )
    )
    second_grad = third_in_grad + dot(hidden_grad, ffn_in, 1, 1)
    second_in_grad, gain_middle, shift_middle = norm_backward(
        second_hat, second_scale, norm_gain[1], second_grad
    )
    cross_branch = second_in_grad.astype(bf16)
    cross_dq_t, mem_dk_t, mem_dv_t = attend_backward(
        cross_queries,
        mem_keys_t,
        mem_values_t,
        cross_extra,
        cross_context,
        dot(cross_branch, cout_pad, 1, 1).astype(bf16),
    )
    mem_grad_t = jnp.concatenate([mem_dk_t, mem_dv_t], axis=0)
    memory_grad = scatter_head(dot(mem_grad_t, cross_kv, 0, 1).astype(bf16))
    first_grad = second_in_grad + dot(cross_dq_t, cross_q, 0, 1)
    first_in_grad, gain_early, shift_early = norm_backward(
        first_hat, first_scale, norm_gain[0], first_grad
    )
    self_branch = first_in_grad.astype(bf16)
    cross_out_grad = dot(cross_context, cross_branch, 0, 0).astype(bf16)
    middle = sum_rows(
        jnp.concatenate(
            [
                cross_out_grad.reshape(-1, WIDE, d)[:, :HEAD_DIM].reshape(d, d),
                dot(cross_dq_t, first_low).astype(bf16),
                dot(mem_grad_t, all_memory).astype(bf16),
            ],
            axis=0,
        )
    )
    small = sum_small(
        jnp.concatenate(
            [
                grad_in_bias,
                grad_out_bias,
                grad_slot_bias,
                gain_early,
                gain_middle,
                gain_late,
                shift_early,
                shift_middle,
                shift_late,
            ]
        )
    )
    dq_t, dk_t, dv_t = attend_backward(
        queries,
        keys_t,
        values_t,
        self_extra,
        context,
        dot(self_branch, wout_pad, 1, 1).astype(bf16),
    )
    kv_grad_t = jnp.concatenate([dk_t, dv_t], axis=0)
    token_grad = (
        first_in_grad
        + dot(dq_t, self_qkv[:, :d], 0, 1)
        + scatter_head(dot(kv_grad_t, self_qkv[:, d:], 0, 1).astype(bf16))
    )
    self_out_grad = dot(context, self_branch, 0, 0).astype(bf16)
    early = sum_rows(
        jnp.concatenate(
            [
                self_out_grad.reshape(-1, WIDE, d)[:, :HEAD_DIM].reshape(d, d),
                dot(dq_t, tokens).astype(bf16),
                dot(kv_grad_t, all_tokens).astype(bf16),
            ],
            axis=0,
        )
    )
    ff = ffn_in.shape[1]
    return (
        slots[None],
        token_grad.astype(bf16)[None],
        memory_grad.astype(bf16)[None],
        early[d:].T.astype(f32),
        early[:d].astype(f32),
        middle[d : 2 * d].T.astype(f32),
        middle[2 * d :].T.astype(f32),
        middle[:d].astype(f32),
        late[2 * d + ff :].T.astype(f32),
        small[:ff],
        late[2 * d : 2 * d + ff].astype(f32),
        small[ff : ff + d],
        late[: 2 * d].astype(f32),
        small[ff + d : ff + 2 * d],
        small[ff + 2 * d : ff + 5 * d].reshape(3, d),
        small[ff + 5 * d :].reshape(3, d),
    )


def solution(mesh):
    split = P("dp", "head", None)
    return jax.shard_map(
        shards,
        mesh=mesh,
        in_specs=(split, split, P("dp")) + (P(),) * 13 + (split,),
        out_specs=(split,) * 3 + (P(),) * 13,
        check_vma=False,
    )
```

```python
import jax
import jax.numpy as jnp
from jax import lax
from jax.experimental import pallas as pl
from jax.experimental.pallas import tpu as pltpu
from jax.sharding import PartitionSpec as P

HEAD_DIM = 64
WIDE = 128
PAIR = 16
epsilon = 1e-05
masked_score = -1e30
log2_e = 1.4426950408889634
scale = HEAD_DIM**-0.5 * log2_e
largest_safe = 100.0
f32 = jnp.float32
bf16 = jnp.bfloat16
SMEM = pl.BlockSpec(memory_space=pltpu.SMEM)
VMEM = pl.BlockSpec(memory_space=pltpu.VMEM)
ANY = pl.BlockSpec(memory_space=pl.ANY)


def dot(a, b, ca=1, cb=0):
    return lax.dot_general(a, b, (((ca,), (cb,)), ((), ())), preferred_element_type=f32)


def shape(rows, columns, dtype=bf16):
    return jax.ShapeDtypeStruct((rows, columns), dtype)


def kernel_call(body, name, outs, args, mib, specs=None, out_specs=None, scratch=(), flops=0):
    return pl.pallas_call(
        body,
        out_shape=tuple(outs),
        in_specs=specs or [VMEM] * len(args),
        out_specs=tuple(out_specs or [VMEM] * len(outs)),
        scratch_shapes=list(scratch),
        compiler_params=pltpu.CompilerParams(vmem_limit_bytes=mib * 2**20),
        cost_estimate=pl.CostEstimate(
            flops=int(flops), bytes_accessed=2 * 2**20, transcendentals=0
        ),
        name=name,
    )(*args)


def span(start, size):
    return pl.ds(pl.multiple_of(start, size), size)


def in_lanes(base, lane, column):
    high = column.astype(bf16).astype(f32)
    rest = column - high
    middle = rest.astype(bf16).astype(f32)
    low = rest - middle
    base = jnp.where(lane == HEAD_DIM + 1, high, base)
    base = jnp.where(lane == HEAD_DIM + 2, middle, base)
    return jnp.where(lane == HEAD_DIM + 3, low, base)


def project_keys(weight, first, second):
    depth, features = weight.shape
    rows = first.shape[0]
    half = features // 2

    def body(w_ref, a_ref, b_ref, k_ref, v_ref):
        w_t = w_ref[...].T
        for part, x_ref in enumerate((a_ref, b_ref)):
            at = pl.ds(part * rows, rows)
            k_ref[:, at] = dot(w_t[:half], x_ref[...], 1, 1).astype(bf16)
            v_ref[:, at] = dot(w_t[half:], x_ref[...], 1, 1).astype(bf16)

    out = shape(half, 2 * rows)
    flops = 4 * rows * depth * features
    return kernel_call(body, "project_keys", [out, out], (weight, first, second), 20, flops=flops)


def attend_forward(queries, keys_t, values_t, extra):
    rows, wide = queries.shape
    heads = wide // WIDE
    keys = keys_t.shape[1]
    block = min(1024, keys)
    group = 4

    def body(q_ref, k_ref, v_ref, e_ref, o_ref, qa_ref):
        lane = lax.broadcasted_iota(jnp.int32, (rows, WIDE), 1)
        sub = lax.broadcasted_iota(jnp.int32, (WIDE, rows), 0)

        def feats(h):
            return span(h * HEAD_DIM, HEAD_DIM)

        def queries_of(h):
            q = jnp.where(lane == HEAD_DIM, 1.0, q_ref[:, span(h * WIDE, WIDE)].astype(f32))
            return q, q.astype(bf16).T

        def scores(h, q_t, at):
            return dot(jnp.concatenate([k_ref[feats(h), at], e_ref[:, at]], axis=0), q_t, 0, 0)

        def weighted(h, p, at):
            return dot(
                jnp.concatenate([v_ref[feats(h), at], e_ref[:PAIR, at]], axis=0), p.astype(bf16)
            )

        def finish(h, q, total, top):
            zeros = jnp.zeros((WIDE - total.shape[0], rows), f32)
            total = jnp.concatenate([total, zeros], axis=0)
            if top is not None:
                total = jnp.where(sub == HEAD_DIM + 4, top, total)
            out = total.T
            weight = out[:, HEAD_DIM + 1 : HEAD_DIM + 2]
            logs = out[:, HEAD_DIM + 4 : HEAD_DIM + 5] + jnp.log2(weight)
            lanes = span(h * WIDE, WIDE)
            o_ref[:, lanes] = jnp.where(lane < HEAD_DIM, out / weight, 0.0).astype(bf16)
            qa_ref[:, lanes] = in_lanes(q, lane, -logs).astype(bf16)

        def step(i, carry):
            held = [queries_of(i * group + u) for u in range(group)]
            bound = jnp.zeros((1, 1), f32)
            for u, (q, q_t) in enumerate(held):
                k = k_ref[feats(i * group + u), :].astype(f32)
                q_f = q_t[:HEAD_DIM].astype(f32)
                most_k = jnp.max(jnp.sum(k * k, axis=0, keepdims=True), axis=1, keepdims=True)
                most_q = jnp.max(jnp.sum(q_f * q_f, axis=0, keepdims=True), axis=1, keepdims=True)
                bound = jnp.maximum(bound, most_k * most_q)
            safe = bound[0, 0] < largest_safe**2

            @pl.when(safe)
            def _():
                totals = [None] * group
                for j in range(keys // block):
                    at = pl.ds(j * block, block)
                    for u in range(group):
                        h = i * group + u
                        part = weighted(h, jnp.exp2(scores(h, held[u][1], at)), at)
                        totals[u] = part if j == 0 else totals[u] + part
                for u in range(group):
                    finish(i * group + u, held[u][0], totals[u], None)

            @pl.when(jnp.logical_not(safe))
            def _():
                def slow(u, c):
                    h = i * group + u
                    q, q_t = queries_of(h)
                    top = jnp.full((1, rows), -jnp.inf, f32)
                    for j in range(keys // block):
                        s = scores(h, q_t, pl.ds(j * block, block))
                        top = jnp.maximum(top, jnp.max(s, axis=0, keepdims=True))
                    total = None
                    for j in range(keys // block):
                        at = pl.ds(j * block, block)
                        part = weighted(h, jnp.exp2(scores(h, q_t, at) - top), at)
                        total = part if j == 0 else total + part
                    finish(h, q, total, top)
                    return c

                lax.fori_loop(0, group, slow, 0)

            return carry

        lax.fori_loop(0, heads // group, step, 0)

    out = shape(rows, wide)
    flops = 8 * rows * keys * wide
    return kernel_call(
        body, "attend_forward", [out, out], (queries, keys_t, values_t, extra), 28, flops=flops
    )


def attend_backward(queries, keys_t, values_t, extra, outs, grads):
    rows, wide = queries.shape
    heads = wide // WIDE
    keys = keys_t.shape[1]
    block = min(1024, keys)
    group = 2
    features = heads * HEAD_DIM

    def body(q_ref, k_ref, v_ref, e_ref, o_ref, g_ref, dq_ref, dk_ref, dv_ref):
        lane = lax.broadcasted_iota(jnp.int32, (rows, WIDE), 1)

        def step(i, carry):
            held = []
            for u in range(group):
                lanes = span((i * group + u) * WIDE, WIDE)
                q = q_ref[:, lanes]
                g_low = g_ref[:, lanes]
                g = g_low.astype(f32)
                centre = jnp.sum(g * o_ref[:, lanes].astype(f32), axis=1, keepdims=True)
                g_more = in_lanes(g, lane, -centre).astype(bf16)
                held.append((q, g_more, q.T[:HEAD_DIM], g_low.T[:HEAD_DIM]))
            totals = [None] * group
            for j in range(keys // block):
                at = pl.ds(j * block, block)
                for u, (q, g_more, q_t, g_t) in enumerate(held):
                    feats = span((i * group + u) * HEAD_DIM, HEAD_DIM)
                    k, v, e = k_ref[feats, at], v_ref[feats, at], e_ref[:, at]
                    p = jnp.exp2(dot(q, jnp.concatenate([k, e], axis=0)))
                    dp = dot(g_more, jnp.concatenate([v, e], axis=0))
                    ds = (p * dp).astype(bf16)
                    dv_ref[feats, at] = dot(g_t, p.astype(bf16)).astype(bf16)
                    dk_ref[feats, at] = (dot(q_t, ds) * (1.0 / log2_e)).astype(bf16)
                    part = dot(k, ds, 1, 1)
                    totals[u] = part if j == 0 else totals[u] + part
            for u in range(group):
                feats = span((i * group + u) * HEAD_DIM, HEAD_DIM)
                dq_ref[feats, :] = (totals[u] * HEAD_DIM**-0.5).astype(bf16)
            return carry

        lax.fori_loop(0, heads // group, step, 0)

    flops = 20 * rows * keys * wide
    outs_of = [shape(features, rows), shape(features, keys), shape(features, keys)]
    args = (queries, keys_t, values_t, extra, outs, grads)
    return kernel_call(body, "attend_backward", outs_of, args, 28, flops=flops)


def late_grads(bits, third, slot_grads, hidden, ffn_grad, hidden_grad, second):
    rows, d = third.shape
    half = hidden.shape[1] // 2

    def body(bits_ref, t_ref, s_ref, h_ref, f_ref, g_ref, n_ref, send_ref, keep_ref):
        core = bits_ref[0]
        for side, out_ref in ((1 - core, send_ref), (core, keep_ref)):
            columns = span(side * half, half)
            out_ref[:d] = dot(t_ref[...], s_ref[side], 0, 0).astype(bf16)
            out_ref[d : d + half] = dot(h_ref[:, columns], f_ref[...], 0, 0).astype(bf16)
            out_ref[d + half :] = dot(g_ref[:, columns], n_ref[...], 0, 0).astype(bf16)

    out = shape(d + 2 * half, d)
    args = (bits, third, slot_grads, hidden, ffn_grad, hidden_grad, second)
    flops = 4 * rows * d * (d + 2 * half)
    specs = [SMEM] + [VMEM] * 6
    return kernel_call(body, "late_grads", [out, out], args, 24, specs, flops=flops)


def head_grads(bits, context, branch, dq_t, inputs, dk_t, dv_t, first, second, by_core):
    rows, d = branch.shape
    heads = context.shape[1] // WIDE
    half = d // 2
    pair = first.shape[0]

    def body(bits_ref, c_ref, b_ref, q_ref, x_ref, k_ref, v_ref, a_ref, z_ref, send_ref, keep_ref):
        core = bits_ref[0]
        for side, out_ref in ((1 - core, send_ref), (core, keep_ref)):
            for h in range(heads // 2):
                lanes = span((side * (heads // 2) + h) * WIDE, WIDE)
                part = dot(c_ref[:, lanes], b_ref[...], 0, 0)
                out_ref[h * HEAD_DIM : (h + 1) * HEAD_DIM] = part[:HEAD_DIM].astype(bf16)
            out_ref[half:d] = dot(q_ref[span(side * half, half)], x_ref[...]).astype(bf16)

            def keyed(ref, feats):
                return (
                    dot(ref[feats, :pair], a_ref[...]) + dot(ref[feats, pair:], z_ref[...])
                ).astype(bf16)

            if by_core:
                out_ref[d : d + half] = keyed(k_ref, span(side * half, half))
                out_ref[d + half :] = keyed(v_ref, span(side * half, half))
            else:

                @pl.when(side == 0)
                def _():
                    out_ref[d:] = keyed(k_ref, slice(None))

                @pl.when(side == 1)
                def _():
                    out_ref[d:] = keyed(v_ref, slice(None))

    out = shape(2 * d, d)
    args = (bits, context, branch, dq_t, inputs, dk_t, dv_t, first, second)
    flops = 4 * d * d * (2 * rows + 2 * pair)
    specs = [SMEM] + [VMEM] * 8
    return kernel_call(body, "head_grads", [out, out], args, 24, specs, flops=flops)


def merge(bits, jobs, name):
    outs, sizes = [], []
    for kept, got, cuts in jobs:
        rows, columns = kept.shape
        parts = max(1, len(cuts))
        size = rows // parts
        sizes.append(size)
        for _ in range(parts):
            outs += [shape(size // 2, columns)] * 2 if cuts else [shape(size, columns)]

    def body(bits_ref, *refs):
        ins, results = list(refs[: 2 * len(jobs)]), list(refs[2 * len(jobs) :])
        for (kept, got, cuts), size in zip(jobs, sizes):
            a_ref, b_ref = ins.pop(0), ins.pop(0)

            def total(at):
                return (a_ref[at].astype(f32) + b_ref[at].astype(f32)).astype(bf16)

            if not cuts:
                results.pop(0)[...] = total(slice(None))
            for n, cut in enumerate(cuts):
                half = size // 2
                mine = bits_ref[cut]
                sent, stays = results.pop(0), results.pop(0)
                sent[...] = total(pl.ds(pl.multiple_of(n * size + (1 - mine) * half, PAIR), half))
                stays[...] = total(pl.ds(pl.multiple_of(n * size + mine * half, PAIR), half))

    args = [bits]
    for kept, got, _ in jobs:
        args += [kept, got]
    specs = [SMEM] + [VMEM] * (2 * len(jobs))
    return kernel_call(body, name, outs, args, 20, specs)


def join(bits, jobs, name):
    outs = [shape(2 * own.shape[0], own.shape[1]) for own, _, _ in jobs]

    def body(bits_ref, *refs):
        ins, results = refs[: 2 * len(jobs)], refs[2 * len(jobs) :]
        for n, (own, _, bit) in enumerate(jobs):
            rows = own.shape[0]
            mine = bits_ref[bit]
            results[n][pl.ds(pl.multiple_of(mine * rows, PAIR), rows)] = ins[2 * n][...]
            results[n][pl.ds(pl.multiple_of((1 - mine) * rows, PAIR), rows)] = ins[2 * n + 1][...]

    args = [bits]
    for own, got, _ in jobs:
        args += [own, got]
    specs = [SMEM] + [VMEM] * (2 * len(jobs))
    return kernel_call(body, name, outs, args, 20, specs)


def swap(block, axis, bit):
    devices = range(lax.axis_size(axis))
    return lax.ppermute(block, axis, [(i, i ^ bit) for i in devices])


def axis_bits(axis, first):
    bits = []
    while first < lax.axis_size(axis):
        bits.append((axis, first))
        first *= 2
    return bits


def sum_rows(bits, table, send, keep, name):
    far, near = axis_bits("head", 2), axis_bits("dp", 1)
    orders = [far + near, near[:1] + far + near[1:]]
    got = swap(send, "head", 1)
    rows = keep.shape[0] // 2
    halved = 0
    while halved < len(orders[0]) and (rows >> halved) % (2 * PAIR) == 0:
        halved += 1
    places = [[table.index(step) for step in order] for order in orders]
    flat = merge(bits, [(keep, got, [place[0] for place in places])], name + "_0")
    for n in range(halved):
        got = [swap(flat[2 * p], *orders[p][n]) for p in range(2)]
        jobs = [
            (flat[2 * p + 1], got[p], [places[p][n + 1]] if n + 1 < halved else [])
            for p in range(2)
        ]
        flat = merge(bits, jobs, name + "_m%d" % n)
    for n in range(halved, len(orders[0])):
        got = [swap(flat[p], *orders[p][n]) for p in range(2)]
        flat = merge(bits, [(flat[p], got[p], []) for p in range(2)], name + "_x%d" % n)
    for n in reversed(range(halved)):
        got = [swap(flat[p], *orders[p][n]) for p in range(2)]
        jobs = [(flat[p], got[p], places[p][n]) for p in range(2)]
        flat = join(bits, jobs, name + "_j%d" % n)
    return flat, [swap(part, "head", 1) for part in flat]


def by_core(core, own, got):
    def reader(side):
        def read(part, at):
            return jnp.where(core == side, own[part][at], got[part][at])

        return read

    return [reader(0), reader(1)]


def late_outputs(bits, own, got, d, ff):
    size = d // 2
    half = ff // 2

    def body(bits_ref, a0, a1, b0, b1, slot_out, down_out, up_out, slot, down, up, sems):
        reads = by_core(bits_ref[0], (a0, a1), (b0, b1))
        per_part = a0.shape[0] // size
        copies = []

        def send(src, dst):
            copies.append(pltpu.make_async_copy(src, dst, sems.at[len(copies)]))
            copies[-1].start()

        for side, read in enumerate(reads):
            for n in range(2 * per_part):
                part, row = divmod(n, per_part)
                block = read(part, pl.ds(row * size, size))
                at = n * size
                if at < d:
                    rows = pl.ds(side * d + at, size)
                    slot[rows] = block.astype(f32)
                    send(slot.at[rows], slot_out.at[rows])
                elif at < d + half:
                    rows = pl.ds(side * half + at - d, size)
                    down[rows] = block.astype(f32)
                    send(down.at[rows], down_out.at[rows])
                else:
                    columns = pl.ds(side * half + at - d - half, size)
                    up[:, columns] = block.T.astype(f32)
                    send(up.at[:, columns], up_out.at[:, columns])
        for copy in copies:
            copy.wait()

    shapes = [shape(2 * d, d, f32), shape(ff, d, f32), shape(d, ff, f32)]
    count = 4 * own[0].shape[0] // size
    scratch = [pltpu.VMEM(s.shape, f32) for s in shapes] + [pltpu.SemaphoreType.DMA((count,))]
    args = (bits, *own, *got)
    specs = [SMEM] + [VMEM] * 4
    return kernel_call(body, "late_outputs", shapes, args, 24, specs, [ANY] * 3, scratch)


def head_outputs(bits, own, got, d, split):
    half = d // 2

    def body(bits_ref, a0, a1, b0, b1, out_out, *rest):
        reads = by_core(bits_ref[0], (a0, a1), (b0, b1))
        if split:
            q_out, kv_out, out, q, kv, sems = rest
        else:
            kv_out, out, kv, sems = rest
            q_out, q = kv_out, kv
        copies = []

        def send(src, dst):
            copies.append(pltpu.make_async_copy(src, dst, sems.at[len(copies)]))
            copies[-1].start()

        for side, read in enumerate(reads):
            rows = pl.ds(side * half, half)
            out[rows] = read(0, pl.ds(0, half)).astype(f32)
            send(out.at[rows], out_out.at[rows])
            columns = pl.ds(side * half, half)
            q[:, columns] = read(0, pl.ds(half, half)).T.astype(f32)
            send(q.at[:, columns], q_out.at[:, columns])
            for n in range(2):
                start = side * d + n * half if split else d + n * d + side * half
                columns = pl.ds(start, half)
                kv[:, columns] = read(1, pl.ds(n * half, half)).T.astype(f32)
                send(kv.at[:, columns], kv_out.at[:, columns])
        for copy in copies:
            copy.wait()

    widths = [d, d, 2 * d] if split else [d, 3 * d]
    shapes = [shape(d, width, f32) for width in widths]
    scratch = [pltpu.VMEM(s.shape, f32) for s in shapes] + [pltpu.SemaphoreType.DMA((8,))]
    args = (bits, *own, *got)
    specs = [SMEM] + [VMEM] * 4
    outs = [ANY] * len(shapes)
    return kernel_call(body, "head_outputs", shapes, args, 24, specs, outs, scratch)


def sum_small(block):
    for axis, first in (("head", 1), ("dp", 1)):
        for axis, bit in axis_bits(axis, first):
            block = block + swap(block, axis, bit)
    return block


def gather_pairs(block):
    pair = jnp.concatenate([block, swap(block, "head", 2)], axis=0)
    return pair, swap(pair, "head", 1)


def scatter_pairs(partial):
    half = partial.shape[0] // 2
    pair = partial[:half].astype(f32) + swap(partial[half:], "head", 1).astype(f32)
    return pair[: half // 2] + swap(pair[half // 2 :].astype(bf16), "head", 2).astype(f32)


def shifted(block, axis, distance):
    devices = range(lax.axis_size(axis))
    route = [(i - distance, i) for i in devices if i - distance in devices]
    return lax.ppermute(block, axis, route)


def normed(values):
    centred = values - jnp.mean(values, axis=-1, keepdims=True)
    spread = jnp.mean(centred * centred, axis=-1, keepdims=True)
    inverse = lax.rsqrt(spread + epsilon)
    return centred * inverse, inverse


def norm_backward(xhat, inverse, gain, upstream):
    g = upstream * gain
    mean_g = jnp.mean(g, axis=-1, keepdims=True)
    dv = inverse * (g - mean_g - xhat * jnp.mean(g * xhat, axis=-1, keepdims=True))
    return dv, jnp.sum(upstream * xhat, axis=0), jnp.sum(upstream, axis=0)


def pad_heads(matrix, axis):
    sizes = list(matrix.shape)
    heads = sizes[axis] // HEAD_DIM
    split = sizes[:axis] + [heads, HEAD_DIM] + sizes[axis + 1 :]
    pads = [(0, 0)] * len(split)
    pads[axis + 1] = (0, WIDE - HEAD_DIM)
    joined = sizes[:axis] + [heads * WIDE] + sizes[axis + 1 :]
    return jnp.pad(matrix.reshape(split), pads).reshape(joined)


def shards(
    tokens,
    memory,
    lengths,
    self_qkv,
    self_out,
    cross_q,
    cross_kv,
    cross_out,
    ffn_in,
    ffn_in_bias,
    ffn_out,
    ffn_out_bias,
    slot_weight,
    slot_bias,
    norm_gain,
    norm_shift,
    cotangent,
):
    tokens, memory, cotangent, length = tokens[0], memory[0], cotangent[0], lengths[0]
    rows, d = tokens.shape
    ff = ffn_in.shape[1]
    me = lax.axis_index("head")
    table = axis_bits("head", 1) + axis_bits("dp", 1)
    bits = jnp.stack([(lax.axis_index(axis) // bit) % 2 for axis, bit in table]).astype(jnp.int32)

    near_tokens, far_tokens = gather_pairs(tokens)
    near_memory, far_memory = gather_pairs(memory)
    keys = 4 * rows
    sources = 4 * memory.shape[0]
    local = jnp.arange(rows, dtype=jnp.int32)
    positions = me * rows + local
    live_slots = (positions < length - 1)[:, None]
    extra_index = jnp.arange(HEAD_DIM)[:, None]
    ones_rows = ((extra_index >= 1) & (extra_index <= 3)).astype(f32)
    key_positions = jnp.concatenate([(me ^ n) * rows + local for n in (0, 2, 1, 3)])
    dead = (key_positions >= length)[None, :]
    self_extra = jnp.where((extra_index == 0) & dead, masked_score, ones_rows).astype(bf16)
    cross_extra = jnp.broadcast_to(ones_rows, (HEAD_DIM, sources)).astype(bf16)

    slot_grad = jnp.where(live_slots, cotangent, 0.0).astype(bf16)
    before = shifted(slot_grad[-1:], "head", 1)
    slot_grads = jnp.stack([slot_grad, jnp.concatenate([before, slot_grad[:-1]], axis=0)])
    third_grad = dot(slot_grads[0], slot_weight[:d], 1, 1) + dot(
        slot_grads[1], slot_weight[d:], 1, 1
    )
    grad_slot_bias = jnp.sum(slot_grad.astype(f32), axis=0)

    wq_pad = pad_heads(self_qkv[:, :d], 1)
    wout_pad = pad_heads(self_out, 0)
    cq_pad = pad_heads(cross_q, 1)
    cout_pad = pad_heads(cross_out, 0)

    queries = (dot(tokens, wq_pad) * scale).astype(bf16)
    keys_t, values_t = project_keys(self_qkv[:, d:], near_tokens, far_tokens)
    context, queries = attend_forward(queries, keys_t, values_t, self_extra)
    first_hat, first_inv = normed(tokens.astype(f32) + dot(context, wout_pad))
    first_norm = first_hat * norm_gain[0] + norm_shift[0]
    first_low = first_norm.astype(bf16)

    cross_queries = (dot(first_low, cq_pad) * scale).astype(bf16)
    mem_keys_t, mem_values_t = project_keys(cross_kv, near_memory, far_memory)
    cross_context, cross_queries = attend_forward(
        cross_queries, mem_keys_t, mem_values_t, cross_extra
    )
    second_hat, second_inv = normed(first_norm + dot(cross_context, cout_pad))
    second_norm = second_hat * norm_gain[1] + norm_shift[1]
    second_low = second_norm.astype(bf16)
    hidden_pre = dot(second_low, ffn_in) + ffn_in_bias.astype(f32)
    hidden, gelu_pull = jax.vjp(jax.nn.gelu, hidden_pre)
    hidden_low = hidden.astype(bf16)
    third_hat, third_inv = normed(
        second_norm + dot(hidden_low, ffn_out) + ffn_out_bias.astype(f32)
    )
    third_low = (third_hat * norm_gain[2] + norm_shift[2]).astype(bf16)
    arriving = shifted(third_low[:1], "head", -1)
    following = jnp.concatenate([third_low[1:], arriving], axis=0)
    slot_pre = (
        dot(third_low, slot_weight[:d])
        + dot(following, slot_weight[d:])
        + slot_bias.astype(f32)
    )
    slots = jnp.where(live_slots, slot_pre, 0.0).astype(bf16)

    third_in_grad, gain_late, shift_late = norm_backward(
        third_hat, third_inv, norm_gain[2], third_grad
    )
    ffn_grad = third_in_grad.astype(bf16)
    grad_out_bias = jnp.sum(ffn_grad.astype(f32), axis=0)
    hidden_grad = gelu_pull(dot(ffn_grad, ffn_out, 1, 1))[0].astype(bf16)
    grad_in_bias = jnp.sum(hidden_grad.astype(f32), axis=0)
    late = sum_rows(
        bits,
        table,
        *late_grads(bits, third_low, slot_grads, hidden_low, ffn_grad, hidden_grad, second_low),
        "late",
    )
    second_grad = third_in_grad + dot(hidden_grad, ffn_in, 1, 1)
    second_in_grad, gain_middle, shift_middle = norm_backward(
        second_hat, second_inv, norm_gain[1], second_grad
    )
    cross_branch = second_in_grad.astype(bf16)
    cross_dq_t, mem_dk_t, mem_dv_t = attend_backward(
        cross_queries,
        mem_keys_t,
        mem_values_t,
        cross_extra,
        cross_context,
        dot(cross_branch, cout_pad, 1, 1).astype(bf16),
    )
    middle = sum_rows(
        bits,
        table,
        *head_grads(
            bits,
            cross_context,
            cross_branch,
            cross_dq_t,
            first_low,
            mem_dk_t,
            mem_dv_t,
            near_memory,
            far_memory,
            False,
        ),
        "middle",
    )
    mem_partial = dot(mem_dk_t, cross_kv[:, :d], 0, 1) + dot(mem_dv_t, cross_kv[:, d:], 0, 1)
    memory_grad = scatter_pairs(mem_partial.astype(bf16))
    first_grad = second_in_grad + dot(cross_dq_t, cross_q, 0, 1)
    first_in_grad, gain_early, shift_early = norm_backward(
        first_hat, first_inv, norm_gain[0], first_grad
    )
    self_branch = first_in_grad.astype(bf16)
    small = sum_small(
        jnp.concatenate(
            [
                grad_in_bias,
                grad_out_bias,
                grad_slot_bias,
                gain_early,
                gain_middle,
                gain_late,
                shift_early,
                shift_middle,
                shift_late,
            ]
        )
    )
    dq_t, dk_t, dv_t = attend_backward(
        queries,
        keys_t,
        values_t,
        self_extra,
        context,
        dot(self_branch, wout_pad, 1, 1).astype(bf16),
    )
    early = sum_rows(
        bits,
        table,
        *head_grads(
            bits, context, self_branch, dq_t, tokens, dk_t, dv_t, near_tokens, far_tokens, True
        ),
        "early",
    )
    token_partial = dot(dk_t, self_qkv[:, d : 2 * d], 0, 1) + dot(dv_t, self_qkv[:, 2 * d :], 0, 1)
    token_grad = (
        first_in_grad
        + dot(dq_t, self_qkv[:, :d], 0, 1)
        + scatter_pairs(token_partial.astype(bf16))
    )
    grad_slot_weight, grad_ffn_out, grad_ffn_in = late_outputs(bits, *late, d, ff)
    grad_cross_out, grad_cross_q, grad_cross_kv = head_outputs(bits, *middle, d, True)
    grad_self_out, grad_self_qkv = head_outputs(bits, *early, d, False)
    return (
        slots[None],
        token_grad.astype(bf16)[None],
        memory_grad.astype(bf16)[None],
        grad_self_qkv,
        grad_self_out,
        grad_cross_q,
        grad_cross_kv,
        grad_cross_out,
        grad_ffn_in,
        small[:ff],
        grad_ffn_out,
        small[ff : ff + d],
        grad_slot_weight,
        small[ff + d : ff + 2 * d],
        small[ff + 2 * d : ff + 5 * d].reshape(3, d),
        small[ff + 5 * d :].reshape(3, d),
    )


def solution(mesh):
    split = P("dp", "head", None)
    return jax.shard_map(
        shards,
        mesh=mesh,
        in_specs=(split, split, P("dp")) + (P(),) * 13 + (split,),
        out_specs=(split,) * 3 + (P(),) * 13,
        check_vma=False,
    )
```

```python
import jax
import jax.numpy as jnp
from jax import lax
from jax.experimental import pallas as pl
from jax.experimental.pallas import tpu as pltpu
from jax.sharding import PartitionSpec as P

HEAD_DIM = 64
WIDE = 128
PAIR = 16
epsilon = 1e-05
masked_score = -1e30
log2_e = 1.4426950408889634
scale = HEAD_DIM**-0.5 * log2_e
largest_safe = 100.0
f32 = jnp.float32
bf16 = jnp.bfloat16
VMEM = pl.BlockSpec(memory_space=pltpu.VMEM)
ANY = pl.BlockSpec(memory_space=pl.ANY)


def dot(a, b, ca=1, cb=0):
    return lax.dot_general(a, b, (((ca,), (cb,)), ((), ())), preferred_element_type=f32)


def shape(rows, columns, dtype=bf16):
    return jax.ShapeDtypeStruct((rows, columns), dtype)


def kernel_call(body, name, outs, args, mib, specs=None, out_specs=None, scratch=()):
    return pl.pallas_call(
        body,
        out_shape=tuple(outs),
        in_specs=specs or [VMEM] * len(args),
        out_specs=tuple(out_specs or [VMEM] * len(outs)),
        scratch_shapes=list(scratch),
        compiler_params=pltpu.CompilerParams(vmem_limit_bytes=mib * 2**20),
        name=name,
    )(*args)


def span(start, size):
    return pl.ds(pl.multiple_of(start, size), size)


def in_parts(base, index, first, values):
    high = values.astype(bf16).astype(f32)
    rest = values - high
    middle = rest.astype(bf16).astype(f32)
    low = rest - middle
    base = jnp.where(index == first, high, base)
    base = jnp.where(index == first + 1, middle, base)
    return jnp.where(index == first + 2, low, base)


def feats(h):
    return span(h * HEAD_DIM, HEAD_DIM)


def with_one(q_t):
    sub = lax.broadcasted_iota(jnp.int32, q_t.shape, 0)
    return jnp.concatenate([q_t, jnp.where(sub == 0, 1.0, 0.0).astype(bf16)], axis=0)


def scores_of(q_more, k, e):
    return dot(jnp.concatenate([k, e], axis=0), q_more, 0, 0)


def weighted(p, v, e):
    return dot(jnp.concatenate([v, e[:PAIR]], axis=0), p.astype(bf16))


def plain_sums(q_more, keyed):
    totals = [None] * len(q_more)
    for k_ref, v_ref, e_ref in keyed:
        e = e_ref[...]
        for n, (h, q) in enumerate(q_more):
            p = jnp.exp2(scores_of(q, k_ref[feats(h)], e))
            part = weighted(p, v_ref[feats(h)], e)
            totals[n] = part if totals[n] is None else totals[n] + part
    return totals


def finish(h, pair, totals, tops, o_ref, qa_ref):
    outs = []
    for n, (total, top) in enumerate(zip(totals, tops)):
        weight = total[HEAD_DIM + 1 : HEAD_DIM + 2]
        outs.append(total[:HEAD_DIM] / weight)
        logs = jnp.log2(weight) if top is None else top + jnp.log2(weight)
        q = pair[n].astype(f32)
        sub = lax.broadcasted_iota(jnp.int32, q.shape, 0)
        more = in_parts(jnp.where(sub == 0, 1.0, 0.0), sub, 1, -logs)
        both = jnp.concatenate([more, q] if n else [q, more], axis=0)
        qa_ref[:, span((h + n) * WIDE, WIDE)] = both.astype(bf16).T
    o_ref[:, span(h * HEAD_DIM, WIDE)] = jnp.concatenate(outs, axis=0).astype(bf16).T


def attend_all(q_ref, keyed, first_sums, o_ref, qa_ref):
    heads = q_ref.shape[0] // HEAD_DIM
    group = 4

    def most(values):
        squares = jnp.sum(values * values, axis=0, keepdims=True)
        return jnp.max(squares, axis=1, keepdims=True)

    def step(i, carry):
        at = [i * group + n for n in range(group)]
        bound = jnp.zeros((1, 1), f32)
        for h in at:
            most_q = most(q_ref[feats(h)].astype(f32))
            for k_ref, _, _ in keyed:
                bound = jnp.maximum(bound, most_q * most(k_ref[feats(h)].astype(f32)))
        safe = bound[0, 0] < largest_safe**2

        @pl.when(safe)
        def _():
            held = [q_ref[feats(h)] for h in at]
            rest = keyed if first_sums is None else keyed[1:]
            totals = plain_sums([(h, with_one(q)) for h, q in zip(at, held)], rest)
            if first_sums is not None:
                totals = [total + first_sums[h] for total, h in zip(totals, at)]
            for n in range(0, group, 2):
                finish(at[n], held[n : n + 2], totals[n : n + 2], (None, None), o_ref, qa_ref)

        @pl.when(jnp.logical_not(safe))
        def _():
            def slow(n, c):
                held, totals, tops = [], [], []
                for m in range(2):
                    h = i * group + 2 * n + m
                    q_t = q_ref[feats(h)]
                    q = with_one(q_t)
                    top = jnp.full((1, q.shape[1]), -jnp.inf, f32)
                    for k_ref, _, e_ref in keyed:
                        s = scores_of(q, k_ref[feats(h)], e_ref[...])
                        top = jnp.maximum(top, jnp.max(s, axis=0, keepdims=True))
                    total = 0.0
                    for k_ref, v_ref, e_ref in keyed:
                        e = e_ref[...]
                        p = jnp.exp2(scores_of(q, k_ref[feats(h)], e) - top)
                        total = total + weighted(p, v_ref[feats(h)], e)
                    held.append(q_t)
                    totals.append(total)
                    tops.append(top)
                finish(i * group + 2 * n, held, totals, tops, o_ref, qa_ref)
                return c

            lax.fori_loop(0, group // 2, slow, 0)

        return carry

    lax.fori_loop(0, heads // group, step, 0)


def project_rows(weight, blocks, outs):
    w_t = weight.T
    features = w_t.shape[0] // len(outs)
    start = 0
    for block in blocks:
        size = block.shape[0]
        for n, out in enumerate(outs):
            w = w_t[n * features : (n + 1) * features]
            out[:, start : start + size] = dot(w, block[...], 1, 1).astype(bf16)
        start += size


def attend_near(tokens, other, self_qkv, extra):
    rows, d = tokens.shape
    heads = d // HEAD_DIM
    group = 4

    def body(a_ref, b_ref, w_ref, e_ref, q_ref, k_ref, v_ref, sums_ref):
        q_ref[...] = (dot(w_ref[:, :d].T, a_ref[...], 1, 1) * scale).astype(bf16)
        project_rows(w_ref[:, d:], (a_ref, b_ref), (k_ref, v_ref))

        def step(i, carry):
            at = [i * group + n for n in range(group)]
            q_more = [(h, with_one(q_ref[feats(h)])) for h in at]
            for h, total in zip(at, plain_sums(q_more, [(k_ref, v_ref, e_ref)])):
                sums_ref[h] = total
            return carry

        lax.fori_loop(0, heads // group, step, 0)

    outs = [shape(d, rows), shape(d, 2 * rows), shape(d, 2 * rows)]
    outs.append(jax.ShapeDtypeStruct((heads, HEAD_DIM + PAIR, rows), f32))
    return kernel_call(body, "attend_near", outs, (tokens, other, self_qkv, extra), 20)


def attend_far(facing, other, self_qkv, q_t, near, sums, near_extra, extra):
    rows, d = facing.shape
    heads = d // HEAD_DIM

    def body(a_ref, b_ref, w_ref, q_ref, nk, nv, s_ref, ne, e_ref, k_ref, v_ref, o_ref, qa_ref):
        project_rows(w_ref[:, d:], (a_ref, b_ref), (k_ref, v_ref))
        attend_all(q_ref, [(nk, nv, ne), (k_ref, v_ref, e_ref)], s_ref, o_ref, qa_ref)

    outs = [shape(d, 2 * rows), shape(d, 2 * rows), shape(rows, d), shape(rows, heads * WIDE)]
    args = (facing, other, self_qkv, q_t, *near, sums, near_extra, extra)
    return kernel_call(body, "attend_far", outs, args, 20)


def attend_memory(blocks, cross_kv, inputs, cross_q, extra):
    rows, d = inputs.shape
    heads = d // HEAD_DIM
    sources = sum(block.shape[0] for block in blocks)
    count = len(blocks)

    def body(*refs):
        w_ref, x_ref, wq_ref, e_ref, k_ref, v_ref, o_ref, qa_ref, q_ref = refs[count:]
        q_ref[...] = (dot(wq_ref[...].T, x_ref[...], 1, 1) * scale).astype(bf16)
        project_rows(w_ref[...], refs[:count], (k_ref, v_ref))
        attend_all(q_ref, [(k_ref, v_ref, e_ref)], None, o_ref, qa_ref)

    outs = [shape(d, sources), shape(d, sources), shape(rows, d), shape(rows, heads * WIDE)]
    args = (*blocks, cross_kv, inputs, cross_q, extra)
    scratch = [pltpu.VMEM((d, rows), bf16)]
    return kernel_call(body, "attend_memory", outs, args, 20, scratch=scratch)


def attend_backward(queries, keyed, outs, grads, first, heads, name):
    rows = queries.shape[0]
    sizes = [k.shape[1] for k, _, _ in keyed]
    group = 2
    features = heads * HEAD_DIM

    def body(q_ref, o_ref, g_ref, *refs):
        key_refs = [refs[3 * j : 3 * j + 3] for j in range(len(keyed))]
        dq_ref, dk_ref, dv_ref = refs[3 * len(keyed) :]
        lane = lax.broadcasted_iota(jnp.int32, (rows, WIDE), 1)
        low_half = lane < HEAD_DIM

        def step(i, carry):
            lanes = span((first + i * group) * HEAD_DIM, WIDE)
            g_low = g_ref[:, lanes]
            g = g_low.astype(f32)
            product = g * o_ref[:, lanes].astype(f32)
            g_t = g_low.T
            held = []
            for u in range(group):
                mine = low_half if u == 0 else jnp.logical_not(low_half)
                centre = jnp.sum(jnp.where(mine, product, 0.0), axis=1, keepdims=True)
                more = in_parts(jnp.zeros_like(g), lane, HEAD_DIM * (1 - u) + 1, -centre)
                q = q_ref[:, span((first + i * group + u) * WIDE, WIDE)]
                own = slice(u * HEAD_DIM, (u + 1) * HEAD_DIM)
                g_more = jnp.where(mine, g, more).astype(bf16)
                held.append((q, g_more, q.T[own], g_t[own]))
            totals = [None] * group
            start = 0
            for (k_ref, v_ref, e_ref), size in zip(key_refs, sizes):
                at = pl.ds(start, size)
                e = e_ref[...]
                for u, (q, g_more, q_t, g_own) in enumerate(held):
                    k = k_ref[feats(first + i * group + u)]
                    v = v_ref[feats(first + i * group + u)]
                    k_more = jnp.concatenate([e, k] if u else [k, e], axis=0)
                    v_more = jnp.concatenate([e, v] if u else [v, e], axis=0)
                    p = jnp.exp2(dot(q, k_more))
                    ds = (p * dot(g_more, v_more)).astype(bf16)
                    to = feats(i * group + u)
                    dv_ref[to, at] = dot(g_own, p.astype(bf16)).astype(bf16)
                    dk_ref[to, at] = (dot(q_t, ds) * (1.0 / log2_e)).astype(bf16)
                    part = dot(k, ds, 1, 1)
                    totals[u] = part if totals[u] is None else totals[u] + part
                start += size
            for u in range(group):
                dq_ref[feats(i * group + u)] = (totals[u] * HEAD_DIM**-0.5).astype(bf16)
            return carry

        lax.fori_loop(0, heads // group, step, 0)

    keys = sum(sizes)
    made = [shape(features, rows), shape(features, keys), shape(features, keys)]
    args = (queries, outs, grads, *[array for part in keyed for array in part])
    return kernel_call(body, name, made, args, 20)


def project_back(pairs, weights, name):
    sizes = [dks[0].shape[1] // 4 for dks, _ in pairs]
    d = weights[0].shape[0]
    rows = sum(sizes)
    args = list(weights) + [part for dks, dvs in pairs for part in (*dks, *dvs)]

    def body(*refs):
        ins = list(refs[len(weights) : len(args)])
        near, facing, other = refs[len(args) :]
        start = 0
        for (dks, dvs), size, w_ref in zip(pairs, sizes, refs):
            grads = [ins.pop(0) for _ in range(len(dks) + len(dvs))]
            for n, (out, at) in enumerate(((near, 0), (other, 0), (facing, 0), (other, rows))):
                total = None
                feature = w_ref.shape[1] - sum(ref.shape[0] for ref in grads)
                for ref in grads:
                    features = ref.shape[0]
                    w = w_ref[:, feature : feature + features]
                    part = dot(ref[:, n * size : (n + 1) * size], w, 0, 1)
                    total = part if total is None else total + part
                    feature += features
                out[pl.ds(at + start, size)] = total.astype(bf16)
            start += size

    outs = [shape(rows, d), shape(rows, d), shape(2 * rows, d)]
    return kernel_call(body, name, outs, args, 12)


def core_index():
    return lax.axis_index("head") % 2


def late_grads(third, slot_grads, hidden, ffn_grad, hidden_grad, second):
    rows, d = third.shape
    half = hidden.shape[1] // 2

    def body(t_ref, s_ref, h_ref, f_ref, g_ref, n_ref, send_ref, keep_ref):
        core = core_index()
        for side, out_ref in ((1 - core, send_ref), (core, keep_ref)):
            columns = span(side * half, half)
            out_ref[:d] = dot(t_ref[...], s_ref[side], 0, 0).astype(bf16)
            out_ref[d : d + half] = dot(h_ref[:, columns], f_ref[...], 0, 0).astype(bf16)
            out_ref[d + half :] = dot(g_ref[:, columns], n_ref[...], 0, 0).astype(bf16)

    out = shape(d + 2 * half, d)
    args = (third, slot_grads, hidden, ffn_grad, hidden_grad, second)
    return kernel_call(body, "late_grads", [out, out], args, 16)


def keyed_grad(ref, rows, blocks):
    total, start = None, 0
    for block in blocks:
        size = block.shape[0]
        part = dot(ref[rows, start : start + size], block)
        total = part if total is None else total + part
        start += size
    return total.astype(bf16)


def middle_grads(outs, out_grads, dq_t, inputs, dk_t, dv_t, blocks, context, branch, small):
    d = branch.shape[1]
    half = d // 2
    count = len(blocks)
    args = (*blocks, outs, out_grads, dq_t, inputs, dk_t, dv_t, context, branch, small)

    def body(*refs):
        o_ref, og_ref, q_ref, x_ref, k_ref, v_ref, c_ref, b_ref, s_ref, *to = refs[count:]
        core = core_index()
        for side, out_ref in ((1 - core, to[0]), (core, to[1])):
            at = span(side * half, half)
            out_ref[:half] = dot(o_ref[:, at], og_ref[...], 0, 0).astype(bf16)
            out_ref[half:d] = dot(q_ref[at], x_ref[...]).astype(bf16)
            for n, ref in enumerate((k_ref, v_ref)):

                @pl.when(side == n)
                def _():
                    memory = [block[...] for block in refs[:count]]
                    out_ref[d : 2 * d] = keyed_grad(ref, slice(None), memory)

            out_ref[2 * d : 2 * d + half] = dot(c_ref[:, at], b_ref[...], 0, 0).astype(bf16)
            rows = s_ref.shape[0]
            out_ref[2 * d + half + rows :] = jnp.zeros((half - rows, d), bf16)
            mine = jnp.where(side == 0, s_ref[...], 0.0)
            out_ref[2 * d + half : 2 * d + half + rows] = mine.astype(bf16)

    out = shape(3 * d, d)
    return kernel_call(body, "middle_grads", [out, out], args, 16)


def early_grads(dqs_t, dks_t, dvs_t, blocks):
    rows, d = blocks[0].shape
    half = d // 2
    calls = len(dqs_t)
    part_rows = d // calls
    count = len(blocks)

    def body(*refs):
        rest = refs[count:]
        core = core_index()
        for side, out_ref in ((1 - core, rest[-2]), (core, rest[-1])):
            at = span(side * half, half)
            cut = [block[:, at] for block in refs[:count]]
            for n in range(calls):
                to = pl.ds(n * part_rows, part_rows)
                out_ref[to] = dot(rest[n][...], cut[0]).astype(bf16)
                for m in (1, 2):
                    to = pl.ds(m * d + n * part_rows, part_rows)
                    out_ref[to] = keyed_grad(rest[m * calls + n], slice(None), cut)

    out = shape(3 * d, half)
    args = (*blocks, *dqs_t, *dks_t, *dvs_t)
    return kernel_call(body, "early_grads", [out, out], args, 16)


def place_in(group, head_bits):
    place = 0
    for n, bit in enumerate(group):
        if bit < head_bits:
            value = lax.axis_index("head") // (1 << bit) % 2
        else:
            value = lax.axis_index("dp") // (1 << (bit - head_bits)) % 2
        place = place + value * (1 << n)
    return place


def count_bits(axis):
    return (lax.axis_size(axis) - 1).bit_length()


def add_up(jobs, group_of, name, joint=False):
    outs, args = [], []
    head_bits = count_bits("head")
    count = len(group_of)
    for parts, group in zip(jobs, group_of):
        size = 1 << len(group)
        rows, d = parts[0].shape
        rows = rows // (size * count if joint else size)
        cut = (count, size, rows, d) if joint else (size, rows, d)
        args += [part.reshape(cut) for part in parts]
        outs += [shape(rows, d)] * size
    outs = outs * count if joint else outs

    def body(*refs):
        ins, results = list(refs[: len(args)]), list(refs[len(args) :])
        for m, group in enumerate(group_of):
            place = place_in(group, head_bits)
            if joint:
                first, *others = [ref.at[m] for ref in ins]
            else:
                first, *others = [ins.pop(0) for _ in jobs[m]]
            for n in range(1 << len(group)):
                total = first[place ^ n].astype(f32)
                for ref in others:
                    total += ref[place ^ n].astype(f32)
                results.pop(0)[...] = total.astype(bf16)

    blocks = list(kernel_call(body, name, outs, args, 8))
    return [[blocks.pop(0) for _ in range(1 << len(group))] for group in group_of]


def add_joint(jobs, group, name):
    head_bits = count_bits("head")
    size = 1 << len(group)
    rows, d = jobs[0][0].shape
    args = [part.reshape(size, rows // size, d) for parts in jobs for part in parts]

    def body(*refs):
        place = place_in(group, head_bits)
        ins, results = list(refs[: len(args)]), refs[len(args) :]
        for m, parts in enumerate(jobs):
            first, *others = [ins.pop(0) for _ in parts]
            for n in range(size):
                total = first[place ^ n].astype(f32)
                for ref in others:
                    total += ref[place ^ n].astype(f32)
                results[n][m] = total.astype(bf16)

    out = jax.ShapeDtypeStruct((len(jobs), rows // size, d), bf16)
    return list(kernel_call(body, name, [out] * size, args, 8))


def put_together(jobs, group_of, name):
    head_bits = count_bits("head")
    args = [part for parts in jobs for part in parts]
    outs = [
        jax.ShapeDtypeStruct((len(parts),) + parts[0].shape, parts[0].dtype) for parts in jobs
    ]

    def body(*refs):
        ins, results = list(refs[: len(args)]), refs[len(args) :]
        for parts, group, out in zip(jobs, group_of, results):
            place = place_in(group, head_bits)
            for n in range(len(parts)):
                out[place ^ n] = ins.pop(0)[...]

    joined = kernel_call(body, name, outs, args, 8)
    return [out.reshape(-1, out.shape[-1]) for out in joined]


def split_joint(parts, group, name):
    head_bits = count_bits("head")
    jobs, rows, d = parts[0].shape
    outs = [jax.ShapeDtypeStruct((len(parts), rows, d), bf16)] * jobs

    def body(*refs):
        place = place_in(group, head_bits)
        for m in range(jobs):
            for n in range(len(parts)):
                refs[len(parts) + m][place ^ n] = refs[n][m]

    joined = kernel_call(body, name, outs, parts, 8)
    return [out.reshape(-1, d) for out in joined]


def send_to(block, mask):
    devices = range(lax.axis_size("dp") * lax.axis_size("head"))
    return lax.ppermute(block, ("dp", "head"), [(i, i ^ mask) for i in devices])


def mask_of(group, n):
    return sum(1 << bit for m, bit in enumerate(group) if n >> m & 1)


def spread(blocks, group):
    return [blocks[0]] + [send_to(blocks[n], mask_of(group, n)) for n in range(1, len(blocks))]


def share(block, group):
    return [block] + [send_to(block, mask_of(group, n)) for n in range(1, 1 << len(group))]


def groups_of():
    bits = list(range(1, count_bits("dp") + count_bits("head")))
    plane = [1, count_bits("head")]
    rest = [bit for bit in bits if bit not in plane]
    return plane, [rest[n : n + 2] for n in range(0, len(rest), 2)]


class Sum:
    def __init__(self, send, keep, name, two):
        self.name, self.two = name, two
        self.plane, self.lines = groups_of()
        self.steps = 0
        self.jobs = [[keep, send_to(send, 1)]]

    def label(self):
        self.steps += 1
        return "%s_%d" % (self.name, self.steps)

    def tie(self, token):
        first = self.jobs[0][0]
        self.jobs[0][0] = lax.optimization_barrier((first, token))[0]

    def orders(self):
        a, b = self.plane
        return [[[a], [b]], [[b], [a]]] if self.two else [[self.plane]]

    def cut_plane(self, n):
        groups = [order[n] for order in self.orders()]
        blocks = add_up(self.jobs, groups, self.label(), self.two and n == 0)
        self.jobs = [spread(block, group) for block, group in zip(blocks, groups)]
        return blocks[0][0]

    def cut_line(self, n):
        jobs = self.jobs
        if n > 0:
            jobs = [[part.reshape(-1, part.shape[-1]) for part in jobs[0]]]
        blocks = add_joint(jobs, self.lines[n], self.label())
        self.jobs = [spread(blocks, self.lines[n])]
        return blocks[0]

    def sum_line(self):
        parts = self.jobs[0]
        whole = parts[0].shape
        flat = [part.reshape(-1, whole[-1]) for part in parts]
        total = add_up([flat], [[]], self.label())[0][0]
        self.jobs = [share(total.reshape(whole), self.lines[-1])]
        return total

    def join_line(self, n):
        if n == 0:
            self.jobs = [[part] for part in split_joint(self.jobs[0], self.lines[0], self.label())]
        else:
            self.jobs = [[put_together(self.jobs, [self.lines[n]], self.label())[0]]]
            whole = self.jobs[0][0]
            self.jobs = [share(whole.reshape(len(self.orders()), -1, whole.shape[-1]), self.lines[n - 1])]
            return whole
        groups = [order[-1] for order in self.orders()]
        token = self.jobs[0][0]
        self.jobs = [share(job[0], group) for job, group in zip(self.jobs, groups)]
        return token

    def join_plane(self, n):
        groups = [order[n] for order in self.orders()]
        wholes = put_together(self.jobs, groups, self.label())
        if n > 0:
            groups = [order[n - 1] for order in self.orders()]
            self.jobs = [share(whole, group) for whole, group in zip(wholes, groups)]
        else:
            self.own = wholes
            self.got = [send_to(whole, 1) for whole in wholes]
        return wholes[0]


def cast_outputs(total, shapes, pieces, name):
    count = len(total.own)
    part_rows = total.own[0].shape[0]

    def body(*refs):
        core = core_index()
        own, got, rest = refs[:count], refs[count : 2 * count], refs[2 * count :]
        outs, held, sems = rest[: len(shapes)], rest[len(shapes) : -1], rest[-1]
        copies = []
        for side, start, size, n, place, turned, at in pieces:
            part, row = divmod(start, part_rows)
            rows = pl.ds(row, size)
            block = jnp.where(core == side, own[part][rows], got[part][rows])
            to = pl.ds(place, size)
            if turned:
                index = (pl.ds(at, block.shape[1]), to)
                held[n][index] = block.T.astype(f32)
            else:
                index = (to, slice(None))
                held[n][index] = block.astype(f32)
            copies.append(
                pltpu.make_async_copy(
                    held[n].at[index], outs[n].at[index], sems.at[len(copies)]
                )
            )
            copies[-1].start()
        for copy in copies:
            copy.wait()

    scratch = [pltpu.VMEM(s.shape, f32) for s in shapes]
    scratch.append(pltpu.SemaphoreType.DMA((len(pieces),)))
    outs = [ANY] * len(shapes)
    args = (*total.own, *total.got)
    mib = 6 + sum(s.shape[0] * s.shape[1] * 4 for s in shapes) // 2**20
    return kernel_call(body, name, shapes, args, mib, None, outs, scratch)


def late_outputs(total, d, ff):
    half, size = ff // 2, d // 2
    pieces = []
    for side in range(2):
        for start in range(0, d, size):
            pieces.append((side, start, size, 0, side * d + start, False, 0))
        for start in range(0, half, size):
            pieces.append((side, d + start, size, 1, side * half + start, False, 0))
            pieces.append((side, d + half + start, size, 2, side * half + start, True, 0))
    shapes = [shape(2 * d, d, f32), shape(ff, d, f32), shape(d, ff, f32)]
    return cast_outputs(total, shapes, pieces, "late_outputs")


def middle_outputs(total, d, count):
    half = d // 2
    pieces = []
    for side in range(2):
        pieces.append((side, 0, half, 0, side * half, False, 0))
        pieces.append((side, half, half, 1, side * half, True, 0))
        pieces.append((side, d, half, 2, side * d, True, 0))
        pieces.append((side, d + half, half, 2, side * d + half, True, 0))
        pieces.append((side, 2 * d, half, 3, side * half, False, 0))
    pieces.append((0, 2 * d + half, count, 4, 0, False, 0))
    shapes = [shape(d, d, f32), shape(d, d, f32), shape(d, 2 * d, f32), shape(d, d, f32)]
    shapes.append(shape(count, d, f32))
    return cast_outputs(total, shapes, pieces, "middle_outputs")


def early_outputs(total, d):
    half = d // 2
    pieces = []
    for side in range(2):
        for start in range(0, 3 * d, half):
            pieces.append((side, start, half, 0, start, True, side * half))
    return cast_outputs(total, [shape(d, 3 * d, f32)], pieces, "early_outputs")[0]


def swap(block, axis, bit):
    devices = range(lax.axis_size(axis))
    return lax.ppermute(block, axis, [(i, i ^ bit) for i in devices])


def after(value, *tokens):
    return lax.optimization_barrier((value, *tokens))[0]


def shifted(block, axis, distance):
    devices = range(lax.axis_size(axis))
    route = [(i - distance, i) for i in devices if i - distance in devices]
    return lax.ppermute(block, axis, route)


def normed(values):
    centred = values - jnp.mean(values, axis=-1, keepdims=True)
    spread = jnp.mean(centred * centred, axis=-1, keepdims=True)
    inverse = lax.rsqrt(spread + epsilon)
    return centred * inverse, inverse


def norm_backward(xhat, inverse, gain, upstream):
    g = upstream * gain
    mean_g = jnp.mean(g, axis=-1, keepdims=True)
    dv = inverse * (g - mean_g - xhat * jnp.mean(g * xhat, axis=-1, keepdims=True))
    return dv, jnp.sum(upstream * xhat, axis=0), jnp.sum(upstream, axis=0)


def shards(
    tokens,
    memory,
    lengths,
    self_qkv,
    self_out,
    cross_q,
    cross_kv,
    cross_out,
    ffn_in,
    ffn_in_bias,
    ffn_out,
    ffn_out_bias,
    slot_weight,
    slot_bias,
    norm_gain,
    norm_shift,
    cotangent,
):
    tokens, memory, cotangent, length = tokens[0], memory[0], cotangent[0], lengths[0]
    rows, d = tokens.shape
    ff = ffn_in.shape[1]
    me = lax.axis_index("head")

    other_tokens, facing_tokens = swap(tokens, "head", 1), swap(tokens, "head", 2)
    local = jnp.arange(rows, dtype=jnp.int32)
    positions = me * rows + local
    live_slots = (positions < length - 1)[:, None]
    extra_index = jnp.arange(HEAD_DIM)[:, None]
    ones_rows = ((extra_index >= 1) & (extra_index <= 3)).astype(f32)

    def extra_of(members):
        key_positions = jnp.concatenate([(me ^ n) * rows + local for n in members])
        dead = (key_positions >= length)[None, :]
        return jnp.where((extra_index == 0) & dead, masked_score, ones_rows).astype(bf16)

    near_extra, far_extra = extra_of((0, 1)), extra_of((2, 3))
    cross_extra = jnp.broadcast_to(ones_rows, (HEAD_DIM, 4 * memory.shape[0])).astype(bf16)

    q_t, *near_keyed, near_sums = attend_near(tokens, other_tokens, self_qkv, near_extra)
    cotangent = after(cotangent, near_sums)
    slot_grad = jnp.where(live_slots, cotangent, 0.0).astype(bf16)
    before = shifted(slot_grad[-1:], "head", 1)
    slot_grads = jnp.stack([slot_grad, jnp.concatenate([before, slot_grad[:-1]], axis=0)])
    third_grad = dot(slot_grads[0], slot_weight[:d], 1, 1) + dot(
        slot_grads[1], slot_weight[d:], 1, 1
    )
    grad_slot_bias = jnp.sum(slot_grad.astype(f32), axis=0)

    facing_tokens = after(facing_tokens, third_grad)
    token_blocks = (tokens, other_tokens, facing_tokens, swap(facing_tokens, "head", 1))
    facing_memory = swap(after(memory, facing_tokens), "head", 2)
    *far_keyed, context, queries = attend_far(
        *token_blocks[2:], self_qkv, q_t, near_keyed, near_sums, near_extra, far_extra
    )
    facing_memory = after(facing_memory, queries)
    memory_blocks = (
        memory,
        swap(memory, "head", 1),
        facing_memory,
        swap(facing_memory, "head", 1),
    )
    first_hat, first_inv = normed(tokens.astype(f32) + dot(context, self_out))
    first_norm = first_hat * norm_gain[0] + norm_shift[0]
    first_low = first_norm.astype(bf16)

    mem_k, mem_v, cross_context, cross_queries = attend_memory(
        memory_blocks, cross_kv, first_low, cross_q, cross_extra
    )
    second_hat, second_inv = normed(first_norm + dot(cross_context, cross_out))
    second_norm = second_hat * norm_gain[1] + norm_shift[1]
    second_low = second_norm.astype(bf16)
    hidden_pre = dot(second_low, ffn_in) + ffn_in_bias.astype(f32)
    hidden, gelu_pull = jax.vjp(jax.nn.gelu, hidden_pre)
    hidden_low = hidden.astype(bf16)
    third_hat, third_inv = normed(
        second_norm + dot(hidden_low, ffn_out) + ffn_out_bias.astype(f32)
    )
    third_low = (third_hat * norm_gain[2] + norm_shift[2]).astype(bf16)
    arriving = shifted(third_low[:1], "head", -1)
    following = jnp.concatenate([third_low[1:], arriving], axis=0)
    slot_pre = (
        dot(third_low, slot_weight[:d])
        + dot(following, slot_weight[d:])
        + slot_bias.astype(f32)
    )
    slots = jnp.where(live_slots, slot_pre, 0.0).astype(bf16)

    third_in_grad, gain_late, shift_late = norm_backward(
        third_hat, third_inv, norm_gain[2], third_grad
    )
    ffn_grad = third_in_grad.astype(bf16)
    grad_out_bias = jnp.sum(ffn_grad.astype(f32), axis=0)
    hidden_grad = gelu_pull(dot(ffn_grad, ffn_out, 1, 1))[0].astype(bf16)
    grad_in_bias = jnp.sum(hidden_grad.astype(f32), axis=0)
    late_send, late_keep = late_grads(
        third_low, slot_grads, hidden_low, ffn_grad, hidden_grad, second_low
    )
    late = Sum(late_send, late_keep, "late", True)
    second_grad = third_in_grad + dot(hidden_grad, ffn_in, 1, 1)
    second_in_grad, gain_middle, shift_middle = norm_backward(
        second_hat, second_inv, norm_gain[1], second_grad
    )
    cross_branch = second_in_grad.astype(bf16)
    cross_grad = dot(cross_branch, cross_out, 1, 1).astype(bf16)
    heads = d // HEAD_DIM
    cross_dq, mem_dk, mem_dv = attend_backward(
        cross_queries,
        [(mem_k, mem_v, cross_extra)],
        cross_context,
        after(cross_grad, late_send),
        0,
        heads,
        "cross_backward",
    )
    late.tie(cross_dq)
    token = late.cut_plane(0)
    first_grad = second_in_grad + dot(cross_dq, cross_q, 0, 1)
    first_in_grad, gain_early, shift_early = norm_backward(
        first_hat, first_inv, norm_gain[0], first_grad
    )
    self_branch = first_in_grad.astype(bf16)
    self_grad = dot(self_branch, self_out, 1, 1).astype(bf16)
    small = [grad_in_bias, grad_out_bias, grad_slot_bias, gain_early, gain_middle, gain_late]
    small = jnp.concatenate(small + [shift_early, shift_middle, shift_late]).reshape(-1, d)
    count = small.shape[0]
    padded = -(-count // PAIR) * PAIR
    middle_send, middle_keep = middle_grads(
        cross_context,
        cross_branch,
        cross_dq,
        first_low,
        mem_dk,
        mem_dv,
        memory_blocks,
        context,
        self_branch,
        after(jnp.pad(small, ((0, padded - count), (0, 0))), token),
    )
    middle = Sum(middle_send, middle_keep, "middle", True)
    token = middle_send
    keyed = [(*near_keyed, near_extra), (*far_keyed, far_extra)]

    def self_backward(first, token):
        return attend_backward(
            queries, keyed, context, after(self_grad, token), first, heads // 2, "self_backward"
        )

    self_parts = [self_backward(0, token)]
    late.tie(self_parts[0][0])
    token = late.cut_plane(1)
    middle.tie(token)
    token = middle.cut_plane(0)
    self_parts.append(self_backward(heads // 2, token))
    dqs, dks, dvs = zip(*self_parts)
    late.tie(dqs[1])
    token = late.cut_line(0)
    early_send, early_keep = early_grads(
        dqs, dks, dvs, (after(tokens, token), *token_blocks[1:])
    )
    early = Sum(early_send, early_keep, "early", False)
    middle.tie(early_send)
    token = middle.cut_plane(1)
    early.tie(token)
    token = early.cut_plane(0)
    near, facing, other = project_back(
        [(dks, dvs), ((mem_dk,), (mem_dv,))],
        [after(self_qkv, token), cross_kv],
        "input_partial",
    )
    got = send_to(other, 1)
    near = near.astype(f32) + got[: near.shape[0]].astype(f32)
    lines = len(late.lines)
    late.tie(facing)
    for n in range(1, lines):
        token = late.cut_line(n)
        late.tie(token)
    token = late.sum_line()
    middle.tie(token)
    for n in range(lines):
        token = middle.cut_line(n)
        middle.tie(token)
    facing = add_up([[facing, after(got[near.shape[0] :], token)]], [[]], "facing")[0][0]
    got = send_to(facing, 2)
    early.tie(facing)
    for n in range(lines):
        token = early.cut_line(n)
        early.tie(token)
    late.tie(token)
    for n in reversed(range(lines)):
        token = late.join_line(n)
    near = near + after(got, token).astype(f32)
    size = dqs[0].shape[0]
    own_part = first_in_grad + near[:rows]
    for n, part in enumerate(dqs):
        own_part = own_part + dot(part, self_qkv[:, n * size : (n + 1) * size], 0, 1)
    token_grad = own_part
    memory_grad = near[rows:]
    order = [(middle, "sum_line", None), (late, "join_plane", 1), (early, "sum_line", None)]
    order += [(middle, "join_line", n) for n in reversed(range(lines))]
    order += [(early, "join_line", n) for n in reversed(range(lines))]
    order += [(late, "join_plane", 0), (middle, "join_plane", 1), (early, "join_plane", 0)]
    order += [(middle, "join_plane", 0)]
    for total, step, n in order:
        total.tie(token)
        token = getattr(total, step)(*([] if n is None else [n]))
    grad_self_qkv = early_outputs(early, d)
    grad_cross_out, grad_cross_q, grad_cross_kv, grad_self_out, sums = middle_outputs(
        middle, d, padded
    )
    grad_slot_weight, grad_ffn_out, grad_ffn_in = late_outputs(late, d, ff)
    small = sums.reshape(-1)
    return (
        slots[None],
        token_grad.astype(bf16)[None],
        memory_grad.astype(bf16)[None],
        grad_self_qkv,
        grad_self_out,
        grad_cross_q,
        grad_cross_kv,
        grad_cross_out,
        grad_ffn_in,
        small[:ff],
        grad_ffn_out,
        small[ff : ff + d],
        grad_slot_weight,
        small[ff + d : ff + 2 * d],
        small[ff + 2 * d : ff + 5 * d].reshape(3, d),
        small[ff + 5 * d : ff + 8 * d].reshape(3, d),
    )


def solution(mesh):
    split = P("dp", "head", None)
    return jax.shard_map(
        shards,
        mesh=mesh,
        in_specs=(split, split, P("dp")) + (P(),) * 13 + (split,),
        out_specs=(split,) * 3 + (P(),) * 13,
        check_vma=False,
    )
```

```python
import jax
import jax.numpy as jnp
from jax import lax
from jax.experimental import pallas as pl
from jax.experimental.pallas import tpu as pltpu
from jax.sharding import PartitionSpec as P

HEAD_DIM = 64
WIDE = 128
PAIR = 16
epsilon = 1e-05
masked_score = -1e30
log2_e = 1.4426950408889634
scale = HEAD_DIM**-0.5 * log2_e
largest_safe = 100.0
f32 = jnp.float32
bf16 = jnp.bfloat16
VMEM = pl.BlockSpec(memory_space=pltpu.VMEM)
ANY = pl.BlockSpec(memory_space=pl.ANY)


def dot(a, b, ca=1, cb=0):
    return lax.dot_general(a, b, (((ca,), (cb,)), ((), ())), preferred_element_type=f32)


def shape(rows, columns, dtype=bf16):
    return jax.ShapeDtypeStruct((rows, columns), dtype)


def kernel_call(body, name, outs, args, mib, specs=None, out_specs=None, scratch=()):
    return pl.pallas_call(
        body,
        out_shape=tuple(outs),
        in_specs=specs or [VMEM] * len(args),
        out_specs=tuple(out_specs or [VMEM] * len(outs)),
        scratch_shapes=list(scratch),
        compiler_params=pltpu.CompilerParams(vmem_limit_bytes=mib * 2**20),
        name=name,
    )(*args)


def span(start, size):
    return pl.ds(pl.multiple_of(start, size), size)


def in_parts(base, index, first, values):
    high = values.astype(bf16).astype(f32)
    rest = values - high
    middle = rest.astype(bf16).astype(f32)
    low = rest - middle
    base = jnp.where(index == first, high, base)
    base = jnp.where(index == first + 1, middle, base)
    return jnp.where(index == first + 2, low, base)


def feats(h):
    return span(h * HEAD_DIM, HEAD_DIM)


def with_one(q_t):
    sub = lax.broadcasted_iota(jnp.int32, q_t.shape, 0)
    return jnp.concatenate([q_t, jnp.where(sub == 0, 1.0, 0.0).astype(bf16)], axis=0)


def scores_of(q_more, k, e):
    return dot(jnp.concatenate([k, e], axis=0), q_more, 0, 0)


def weighted(p, v, e):
    return dot(jnp.concatenate([v, e[:PAIR]], axis=0), p.astype(bf16))


def plain_sums(q_more, keyed):
    totals = [None] * len(q_more)
    for k_ref, v_ref, e_ref in keyed:
        e = e_ref[...]
        for n, (h, q) in enumerate(q_more):
            p = jnp.exp2(scores_of(q, k_ref[feats(h)], e))
            part = weighted(p, v_ref[feats(h)], e)
            totals[n] = part if totals[n] is None else totals[n] + part
    return totals


def finish(h, pair, totals, tops, o_ref, qa_ref):
    outs = []
    for n, (total, top) in enumerate(zip(totals, tops)):
        weight = total[HEAD_DIM + 1 : HEAD_DIM + 2]
        outs.append(total[:HEAD_DIM] / weight)
        logs = jnp.log2(weight) if top is None else top + jnp.log2(weight)
        q = pair[n].astype(f32)
        sub = lax.broadcasted_iota(jnp.int32, q.shape, 0)
        more = in_parts(jnp.where(sub == 0, 1.0, 0.0), sub, 1, -logs)
        both = jnp.concatenate([more, q] if n else [q, more], axis=0)
        qa_ref[:, span((h + n) * WIDE, WIDE)] = both.astype(bf16).T
    o_ref[:, span(h * HEAD_DIM, WIDE)] = jnp.concatenate(outs, axis=0).astype(bf16).T


def attend_all(q_ref, keyed, first_sums, o_ref, qa_ref):
    heads = q_ref.shape[0] // HEAD_DIM
    group = 4

    def most(values):
        squares = jnp.sum(values * values, axis=0, keepdims=True)
        return jnp.max(squares, axis=1, keepdims=True)

    def step(i, carry):
        at = [i * group + n for n in range(group)]
        bound = jnp.zeros((1, 1), f32)
        for h in at:
            most_q = most(q_ref[feats(h)].astype(f32))
            for k_ref, _, _ in keyed:
                bound = jnp.maximum(bound, most_q * most(k_ref[feats(h)].astype(f32)))
        safe = bound[0, 0] < largest_safe**2

        @pl.when(safe)
        def _():
            held = [q_ref[feats(h)] for h in at]
            rest = keyed if first_sums is None else keyed[1:]
            totals = plain_sums([(h, with_one(q)) for h, q in zip(at, held)], rest)
            if first_sums is not None:
                totals = [total + first_sums[h] for total, h in zip(totals, at)]
            for n in range(0, group, 2):
                finish(at[n], held[n : n + 2], totals[n : n + 2], (None, None), o_ref, qa_ref)

        @pl.when(jnp.logical_not(safe))
        def _():
            def slow(n, c):
                held, totals, tops = [], [], []
                for m in range(2):
                    h = i * group + 2 * n + m
                    q_t = q_ref[feats(h)]
                    q = with_one(q_t)
                    top = jnp.full((1, q.shape[1]), -jnp.inf, f32)
                    for k_ref, _, e_ref in keyed:
                        s = scores_of(q, k_ref[feats(h)], e_ref[...])
                        top = jnp.maximum(top, jnp.max(s, axis=0, keepdims=True))
                    total = 0.0
                    for k_ref, v_ref, e_ref in keyed:
                        e = e_ref[...]
                        p = jnp.exp2(scores_of(q, k_ref[feats(h)], e) - top)
                        total = total + weighted(p, v_ref[feats(h)], e)
                    held.append(q_t)
                    totals.append(total)
                    tops.append(top)
                finish(i * group + 2 * n, held, totals, tops, o_ref, qa_ref)
                return c

            lax.fori_loop(0, group // 2, slow, 0)

        return carry

    lax.fori_loop(0, heads // group, step, 0)


def project_rows(weight, blocks, outs):
    w_t = weight.T
    features = w_t.shape[0] // len(outs)
    start = 0
    for block in blocks:
        size = block.shape[0]
        for n, out in enumerate(outs):
            w = w_t[n * features : (n + 1) * features]
            out[:, start : start + size] = dot(w, block[...], 1, 1).astype(bf16)
        start += size


def attend_near(tokens, other, self_qkv, extra):
    rows, d = tokens.shape
    heads = d // HEAD_DIM
    group = 4

    def body(a_ref, b_ref, w_ref, e_ref, q_ref, k_ref, v_ref, sums_ref):
        q_ref[...] = (dot(w_ref[:, :d].T, a_ref[...], 1, 1) * scale).astype(bf16)
        project_rows(w_ref[:, d:], (a_ref, b_ref), (k_ref, v_ref))

        def step(i, carry):
            at = [i * group + n for n in range(group)]
            q_more = [(h, with_one(q_ref[feats(h)])) for h in at]
            for h, total in zip(at, plain_sums(q_more, [(k_ref, v_ref, e_ref)])):
                sums_ref[h] = total
            return carry

        lax.fori_loop(0, heads // group, step, 0)

    outs = [shape(d, rows), shape(d, 2 * rows), shape(d, 2 * rows)]
    outs.append(jax.ShapeDtypeStruct((heads, HEAD_DIM + PAIR, rows), f32))
    return kernel_call(body, "attend_near", outs, (tokens, other, self_qkv, extra), 20)


def attend_far(facing, other, self_qkv, q_t, near, sums, near_extra, extra):
    rows, d = facing.shape
    heads = d // HEAD_DIM

    def body(a_ref, b_ref, w_ref, q_ref, nk, nv, s_ref, ne, e_ref, k_ref, v_ref, o_ref, qa_ref):
        project_rows(w_ref[:, d:], (a_ref, b_ref), (k_ref, v_ref))
        attend_all(q_ref, [(nk, nv, ne), (k_ref, v_ref, e_ref)], s_ref, o_ref, qa_ref)

    outs = [shape(d, 2 * rows), shape(d, 2 * rows), shape(rows, d), shape(rows, heads * WIDE)]
    args = (facing, other, self_qkv, q_t, *near, sums, near_extra, extra)
    return kernel_call(body, "attend_far", outs, args, 20)


def attend_memory(blocks, cross_kv, inputs, cross_q, extra):
    rows, d = inputs.shape
    heads = d // HEAD_DIM
    sources = sum(block.shape[0] for block in blocks)
    count = len(blocks)

    def body(*refs):
        w_ref, x_ref, wq_ref, e_ref, k_ref, v_ref, o_ref, qa_ref, q_ref = refs[count:]
        q_ref[...] = (dot(wq_ref[...].T, x_ref[...], 1, 1) * scale).astype(bf16)
        project_rows(w_ref[...], refs[:count], (k_ref, v_ref))
        attend_all(q_ref, [(k_ref, v_ref, e_ref)], None, o_ref, qa_ref)

    outs = [shape(d, sources), shape(d, sources), shape(rows, d), shape(rows, heads * WIDE)]
    args = (*blocks, cross_kv, inputs, cross_q, extra)
    scratch = [pltpu.VMEM((d, rows), bf16)]
    return kernel_call(body, "attend_memory", outs, args, 20, scratch=scratch)


def run(name, piece):
    body, outs, args, mib = piece
    return kernel_call(body, name, outs, args, mib)


def attend_backward(queries, keyed, outs, grads, first, heads):
    rows = queries.shape[0]
    sizes = [k.shape[1] for k, _, _ in keyed]
    group = 2
    features = heads * HEAD_DIM

    def body(q_ref, o_ref, g_ref, *refs):
        key_refs = [refs[3 * j : 3 * j + 3] for j in range(len(keyed))]
        dq_ref, dk_ref, dv_ref = refs[3 * len(keyed) :]
        lane = lax.broadcasted_iota(jnp.int32, (rows, WIDE), 1)
        low_half = lane < HEAD_DIM

        def step(i, carry):
            lanes = span((first + i * group) * HEAD_DIM, WIDE)
            g_low = g_ref[:, lanes]
            g = g_low.astype(f32)
            product = g * o_ref[:, lanes].astype(f32)
            g_t = g_low.T
            held = []
            for u in range(group):
                mine = low_half if u == 0 else jnp.logical_not(low_half)
                centre = jnp.sum(jnp.where(mine, product, 0.0), axis=1, keepdims=True)
                more = in_parts(jnp.zeros_like(g), lane, HEAD_DIM * (1 - u) + 1, -centre)
                q = q_ref[:, span((first + i * group + u) * WIDE, WIDE)]
                own = slice(u * HEAD_DIM, (u + 1) * HEAD_DIM)
                g_more = jnp.where(mine, g, more).astype(bf16)
                held.append((q, g_more, q.T[own], g_t[own]))
            totals = [None] * group
            start = 0
            for (k_ref, v_ref, e_ref), size in zip(key_refs, sizes):
                at = pl.ds(start, size)
                e = e_ref[...]
                for u, (q, g_more, q_t, g_own) in enumerate(held):
                    k = k_ref[feats(first + i * group + u)]
                    v = v_ref[feats(first + i * group + u)]
                    k_more = jnp.concatenate([e, k] if u else [k, e], axis=0)
                    v_more = jnp.concatenate([e, v] if u else [v, e], axis=0)
                    p = jnp.exp2(dot(q, k_more))
                    ds = (p * dot(g_more, v_more)).astype(bf16)
                    to = feats(i * group + u)
                    dv_ref[to, at] = dot(g_own, p.astype(bf16)).astype(bf16)
                    dk_ref[to, at] = (dot(q_t, ds) * (1.0 / log2_e)).astype(bf16)
                    part = dot(k, ds, 1, 1)
                    totals[u] = part if totals[u] is None else totals[u] + part
                start += size
            for u in range(group):
                dq_ref[feats(i * group + u)] = (totals[u] * HEAD_DIM**-0.5).astype(bf16)
            return carry

        lax.fori_loop(0, heads // group, step, 0)

    keys = sum(sizes)
    made = [shape(features, rows), shape(features, keys), shape(features, keys)]
    args = (queries, outs, grads, *[array for part in keyed for array in part])
    return body, made, args, 20


def back_through_norm(x, inverse, gain, upstream):
    g = upstream * gain
    mean_g = jnp.mean(g, axis=1, keepdims=True)
    mean_gx = jnp.mean(g * x, axis=1, keepdims=True)
    sums = [jnp.sum(part, axis=0, keepdims=True) for part in (upstream * x, upstream)]
    return inverse * (g - mean_g - x * mean_gx), *sums


def cross_and_first_backward(attention, upstream, first_in, gain, cross_q, self_out):
    inner, made, ins, mib = attention
    rows, d = first_in.shape
    args = (upstream, first_in, gain, cross_q, self_out, *ins)

    def body(u_ref, f_ref, g_ref, wq_ref, wo_ref, *refs):
        inner(*refs[: len(ins) + len(made)])
        dq_ref = refs[len(ins)]
        grad_ref, branch_ref, back_ref, sums_ref = refs[len(ins) + len(made) :]
        x, inverse = normed(f_ref[...])
        up = u_ref[...] + dot(dq_ref[...], wq_ref[...], 0, 1)
        grad, sums_ref[0:1], sums_ref[1:2] = back_through_norm(x, inverse, g_ref[...], up)
        grad_ref[...] = grad
        branch = grad.astype(bf16)
        branch_ref[...] = branch
        back_ref[...] = dot(branch, wo_ref[...], 1, 1).astype(bf16)

    outs = [*made, shape(rows, d, f32), shape(rows, d), shape(rows, d), shape(2, d, f32)]
    return body, outs, args, mib


def feed_forward(context, first_norm, third_grad, slot_grads, weights, biases, gains, shifts):
    rows, d = first_norm.shape
    cross_out, ffn_in, ffn_out = weights
    ff = ffn_in.shape[1]
    half = ff // 2
    block = rows // 2
    bend, slope = 0.044715, (2.0 / jnp.pi) ** 0.5
    slope = float(slope)

    def body(*refs):
        c_ref, f_ref, u_ref, s_ref, wc_ref, wi_ref, wo_ref, bi_ref, bo_ref, g_ref, t_ref = refs[:11]
        third_ref, grad_ref, branch_ref, back_ref, sums_ref, in_ref, send_ref, keep_ref = refs[11:19]
        second_ref, hidden_ref, slope_ref, fg_ref, hg_ref = refs[19:]
        sums_ref[...] = jnp.zeros_like(sums_ref)
        in_ref[...] = jnp.zeros_like(in_ref)
        def step(n, carry):
            to = span(n * block, block)
            x2, inverse2 = normed(f_ref[to] + dot(c_ref[to], wc_ref[...]))
            second = x2 * g_ref[1:2] + t_ref[1:2]
            low = second.astype(bf16)
            second_ref[to] = low
            total = second + bo_ref[...].astype(f32)
            for start in range(0, ff, d):
                part = pl.ds(start, d)
                pre = dot(low, wi_ref[:, part]) + bi_ref[:, part].astype(f32)
                square = pre * pre
                tanh = jnp.tanh(slope * pre * (1.0 + bend * square))
                hidden = (0.5 * pre * (1.0 + tanh)).astype(bf16)
                hidden_ref[to, part] = hidden
                steep = slope * (1.0 + 3.0 * bend * square)
                slope_ref[:, part] = 0.5 * (1.0 + tanh) + 0.5 * pre * (1.0 - tanh * tanh) * steep
                total = total + dot(hidden, wo_ref[part])
            x3, inverse3 = normed(total)
            third_ref[to] = (x3 * g_ref[2:3] + t_ref[2:3]).astype(bf16)
            grad3, gain3, shift3 = back_through_norm(x3, inverse3, g_ref[2:3], u_ref[to])
            ffn_grad = grad3.astype(bf16)
            fg_ref[to] = ffn_grad
            sums_ref[0:1] += gain3
            sums_ref[1:2] += shift3
            sums_ref[4:5] += jnp.sum(ffn_grad.astype(f32), axis=0, keepdims=True)
            total = grad3
            for start in range(0, ff, d):
                part = pl.ds(start, d)
                back = (dot(ffn_grad, wo_ref[part], 1, 1) * slope_ref[:, part]).astype(bf16)
                hg_ref[to, part] = back
                in_ref[:, part] += jnp.sum(back.astype(f32), axis=0, keepdims=True)
                total = total + dot(back, wi_ref[:, part], 1, 1)
            grad2, gain2, shift2 = back_through_norm(x2, inverse2, g_ref[1:2], total)
            sums_ref[2:3] += gain2
            sums_ref[3:4] += shift2
            grad_ref[to] = grad2
            branch = grad2.astype(bf16)
            branch_ref[to] = branch
            back_ref[to] = dot(branch, wc_ref[...], 1, 1).astype(bf16)
            return carry

        lax.fori_loop(0, rows // block, step, 0)
        core = core_index()
        for side, out_ref in ((1 - core, send_ref), (core, keep_ref)):
            columns = span(side * half, half)
            out_ref[:d] = dot(third_ref[...], s_ref[side], 0, 0).astype(bf16)
            out_ref[d : d + half] = dot(hidden_ref[:, columns], fg_ref[...], 0, 0).astype(bf16)
            out_ref[d + half :] = dot(hg_ref[:, columns], second_ref[...], 0, 0).astype(bf16)

    outs = [shape(rows, d), shape(rows, d, f32), shape(rows, d), shape(rows, d)]
    outs += [shape(8, d, f32), shape(1, ff, f32)] + [shape(d + 2 * half, d)] * 2
    args = (context, first_norm, third_grad, slot_grads, *weights, *biases, gains, shifts)
    scratch = [pltpu.VMEM((rows, d), bf16), pltpu.VMEM((rows, ff), bf16)]
    scratch += [pltpu.VMEM((block, ff), f32), pltpu.VMEM((rows, d), bf16)]
    scratch += [pltpu.VMEM((rows, ff), bf16)]
    return kernel_call(body, "feed_forward", outs, args, 30, scratch=scratch)


def project_back(pairs, weights, name):
    sizes = [dks[0].shape[1] // 4 for dks, _ in pairs]
    d = weights[0].shape[0]
    rows = sum(sizes)
    args = list(weights) + [part for dks, dvs in pairs for part in (*dks, *dvs)]

    def body(*refs):
        ins = list(refs[len(weights) : len(args)])
        near, facing, other = refs[len(args) :]
        start = 0
        for (dks, dvs), size, w_ref in zip(pairs, sizes, refs):
            grads = [ins.pop(0) for _ in range(len(dks) + len(dvs))]
            for n, (out, at) in enumerate(((near, 0), (other, 0), (facing, 0), (other, rows))):
                total = None
                feature = w_ref.shape[1] - sum(ref.shape[0] for ref in grads)
                for ref in grads:
                    features = ref.shape[0]
                    w = w_ref[:, feature : feature + features]
                    part = dot(ref[:, n * size : (n + 1) * size], w, 0, 1)
                    total = part if total is None else total + part
                    feature += features
                out[pl.ds(at + start, size)] = total.astype(bf16)
            start += size

    outs = [shape(rows, d), shape(rows, d), shape(2 * rows, d)]
    return kernel_call(body, name, outs, args, 12)


def core_index():
    return lax.axis_index("head") % 2


def keyed_grad(ref, rows, blocks):
    total, start = None, 0
    for block in blocks:
        size = block.shape[0]
        part = dot(ref[rows, start : start + size], block)
        total = part if total is None else total + part
        start += size
    return total.astype(bf16)


def middle_grads(outs, out_grads, dq_t, inputs, dk_t, dv_t, blocks, context, branch, sums):
    d = branch.shape[1]
    half = d // 2
    count = len(blocks)
    args = (*blocks, outs, out_grads, dq_t, inputs, dk_t, dv_t, context, branch, *sums)

    def body(*refs):
        o_ref, og_ref, q_ref, x_ref, k_ref, v_ref, c_ref, b_ref, *rest = refs[count:]
        in_bias, late, early, slot_bias, *to = rest
        core = core_index()
        small = [in_bias[:, n : n + d] for n in range(0, in_bias.shape[1], d)]
        small += [late[4:5], slot_bias[...], early[0:1], late[2:3], late[0:1]]
        small += [early[1:2], late[3:4], late[1:2]]
        rows = -(-len(small) // PAIR) * PAIR
        small.append(jnp.zeros((rows - len(small), d), f32))
        small = jnp.concatenate(small, axis=0)
        for side, out_ref in ((1 - core, to[0]), (core, to[1])):
            at = span(side * half, half)
            out_ref[:half] = dot(o_ref[:, at], og_ref[...], 0, 0).astype(bf16)
            out_ref[half:d] = dot(q_ref[at], x_ref[...]).astype(bf16)
            for n, ref in enumerate((k_ref, v_ref)):

                @pl.when(side == n)
                def _():
                    memory = [block[...] for block in refs[:count]]
                    out_ref[d : 2 * d] = keyed_grad(ref, slice(None), memory)

            out_ref[2 * d : 2 * d + half] = dot(c_ref[:, at], b_ref[...], 0, 0).astype(bf16)
            out_ref[2 * d + half + rows :] = jnp.zeros((half - rows, d), bf16)
            mine = jnp.where(side == 0, small, 0.0)
            out_ref[2 * d + half : 2 * d + half + rows] = mine.astype(bf16)

    out = shape(3 * d, d)
    return kernel_call(body, "middle_grads", [out, out], args, 16)


def early_grads(dqs_t, dks_t, dvs_t, blocks):
    rows, d = blocks[0].shape
    half = d // 2
    count = len(blocks)

    def body(*refs):
        calls = [refs[count + n : count + 6 : 2] for n in range(2)]
        core = core_index()
        for side, out_ref in ((1 - core, refs[-2]), (core, refs[-1])):
            for n, (q_ref, k_ref, v_ref) in enumerate(calls):

                @pl.when(side == n)
                def _():
                    inputs = [block[...] for block in refs[:count]]
                    out_ref[:half] = dot(q_ref[...], inputs[0]).astype(bf16)
                    out_ref[half:d] = keyed_grad(k_ref, slice(None), inputs)
                    out_ref[d:] = keyed_grad(v_ref, slice(None), inputs)

    out = shape(3 * half, d)
    args = (*blocks, *dqs_t, *dks_t, *dvs_t)
    return kernel_call(body, "early_grads", [out, out], args, 16)


def place_in(group, head_bits):
    place = 0
    for n, bit in enumerate(group):
        if bit < head_bits:
            value = lax.axis_index("head") // (1 << bit) % 2
        else:
            value = lax.axis_index("dp") // (1 << (bit - head_bits)) % 2
        place = place + value * (1 << n)
    return place


def count_bits(axis):
    return (lax.axis_size(axis) - 1).bit_length()


def add_up(jobs, group_of, name, joint=False):
    outs, args = [], []
    head_bits = count_bits("head")
    count = len(group_of)
    for parts, group in zip(jobs, group_of):
        size = 1 << len(group)
        rows, d = parts[0].shape
        rows = rows // (size * count if joint else size)
        cut = (count, size, rows, d) if joint else (size, rows, d)
        args += [part.reshape(cut) for part in parts]
        outs += [shape(rows, d)] * size
    outs = outs * count if joint else outs

    def body(*refs):
        ins, results = list(refs[: len(args)]), list(refs[len(args) :])
        for m, group in enumerate(group_of):
            place = place_in(group, head_bits)
            if joint:
                first, *others = [ref.at[m] for ref in ins]
            else:
                first, *others = [ins.pop(0) for _ in jobs[m]]
            for n in range(1 << len(group)):
                total = first[place ^ n].astype(f32)
                for ref in others:
                    total += ref[place ^ n].astype(f32)
                results.pop(0)[...] = total.astype(bf16)

    blocks = list(kernel_call(body, name, outs, args, 8))
    return [[blocks.pop(0) for _ in range(1 << len(group))] for group in group_of]


def add_joint(jobs, group, name):
    head_bits = count_bits("head")
    size = 1 << len(group)
    rows, d = jobs[0][0].shape
    args = [part.reshape(size, rows // size, d) for parts in jobs for part in parts]

    def body(*refs):
        place = place_in(group, head_bits)
        ins, results = list(refs[: len(args)]), refs[len(args) :]
        for m, parts in enumerate(jobs):
            first, *others = [ins.pop(0) for _ in parts]
            for n in range(size):
                total = first[place ^ n].astype(f32)
                for ref in others:
                    total += ref[place ^ n].astype(f32)
                results[n][m] = total.astype(bf16)

    out = jax.ShapeDtypeStruct((len(jobs), rows // size, d), bf16)
    return list(kernel_call(body, name, [out] * size, args, 8))


def put_together(jobs, group_of, name):
    head_bits = count_bits("head")
    args = [part for parts in jobs for part in parts]
    outs = [
        jax.ShapeDtypeStruct((len(parts),) + parts[0].shape, parts[0].dtype) for parts in jobs
    ]

    def body(*refs):
        ins, results = list(refs[: len(args)]), refs[len(args) :]
        for parts, group, out in zip(jobs, group_of, results):
            place = place_in(group, head_bits)
            for n in range(len(parts)):
                out[place ^ n] = ins.pop(0)[...]

    joined = kernel_call(body, name, outs, args, 8)
    return [out.reshape(-1, out.shape[-1]) for out in joined]


def split_joint(parts, group, name):
    head_bits = count_bits("head")
    jobs, rows, d = parts[0].shape
    outs = [jax.ShapeDtypeStruct((len(parts), rows, d), bf16)] * jobs

    def body(*refs):
        place = place_in(group, head_bits)
        for m in range(jobs):
            for n in range(len(parts)):
                refs[len(parts) + m][place ^ n] = refs[n][m]

    joined = kernel_call(body, name, outs, parts, 8)
    return [out.reshape(-1, d) for out in joined]


def send_to(block, mask):
    devices = range(lax.axis_size("dp") * lax.axis_size("head"))
    return lax.ppermute(block, ("dp", "head"), [(i, i ^ mask) for i in devices])


def mask_of(group, n):
    return sum(1 << bit for m, bit in enumerate(group) if n >> m & 1)


def spread(blocks, group):
    return [blocks[0]] + [send_to(blocks[n], mask_of(group, n)) for n in range(1, len(blocks))]


def share(block, group):
    return [block] + [send_to(block, mask_of(group, n)) for n in range(1, 1 << len(group))]


def groups_of(at_once):
    bits = list(range(1, count_bits("dp") + count_bits("head")))
    plane = [1, count_bits("head")]
    rest = [bit for bit in bits if bit not in plane]
    return plane, [rest[n : n + at_once] for n in range(0, len(rest), at_once)]


AT_ONCE = (2, 1)
ORDER = (
    "xb", "L1", "mg", "sa", "L2", "M1", "sb", "L3", "M2", "eg", "E1", "tp",
    "L4", "T1", "S1", "J1", "S2", "L5", "J2", "L6", "J3", "J4", "T2", "J5",
    "J6", "L7", "Lo", "J7", "Jo",
)


class Sum:
    def __init__(self, send, keep, name, two, at_once):
        self.name, self.two = name, two
        self.plane, self.lines = groups_of(at_once)
        self.steps = 0
        self.jobs = [[keep, send_to(send, 1)]]

    def label(self):
        self.steps += 1
        return "%s_%d" % (self.name, self.steps)

    def tie(self, token):
        first = self.jobs[0][0]
        self.jobs[0][0] = lax.optimization_barrier((first, token))[0]

    def orders(self):
        a, b = self.plane
        return [[[a], [b]], [[b], [a]]] if self.two else [[self.plane]]

    def cut_plane(self, n):
        groups = [order[n] for order in self.orders()]
        blocks = add_up(self.jobs, groups, self.label(), self.two and n == 0)
        self.jobs = [spread(block, group) for block, group in zip(blocks, groups)]
        return blocks[0][0]

    def cut_line(self, n):
        jobs = self.jobs
        if n > 0:
            jobs = [[part.reshape(-1, part.shape[-1]) for part in jobs[0]]]
        blocks = add_joint(jobs, self.lines[n], self.label())
        self.jobs = [spread(blocks, self.lines[n])]
        return blocks[0]

    def sum_line(self):
        parts = self.jobs[0]
        whole = parts[0].shape
        flat = [part.reshape(-1, whole[-1]) for part in parts]
        total = add_up([flat], [[]], self.label())[0][0]
        self.jobs = [share(total.reshape(whole), self.lines[-1])]
        return total

    def join_line(self, n):
        if n == 0:
            self.jobs = [[part] for part in split_joint(self.jobs[0], self.lines[0], self.label())]
        else:
            self.jobs = [[put_together(self.jobs, [self.lines[n]], self.label())[0]]]
            whole = self.jobs[0][0]
            self.jobs = [share(whole.reshape(len(self.orders()), -1, whole.shape[-1]), self.lines[n - 1])]
            return whole
        groups = [order[-1] for order in self.orders()]
        token = self.jobs[0][0]
        self.jobs = [share(job[0], group) for job, group in zip(self.jobs, groups)]
        return token

    def join_plane(self, n):
        groups = [order[n] for order in self.orders()]
        wholes = put_together(self.jobs, groups, self.label())
        if n > 0:
            groups = [order[n - 1] for order in self.orders()]
            self.jobs = [share(whole, group) for whole, group in zip(wholes, groups)]
        else:
            self.own = wholes
            self.got = [send_to(whole, 1) for whole in wholes]
        return wholes[0]


class Joint:
    def __init__(self, halves, whole):
        self.jobs = [*halves.jobs, whole.jobs[0]]
        self.plane, self.lines = halves.plane, halves.lines
        self.name, self.steps = "joint", 0
        self.rows = whole.jobs[0][0].shape[0]

    tie, label = Sum.tie, Sum.label
    cut_line, sum_line = Sum.cut_line, Sum.sum_line

    def join_line(self, n):
        if n > 0:
            whole = put_together(self.jobs, [self.lines[n]], self.label())[0]
            whole = whole.reshape(3, -1, whole.shape[-1])
            self.jobs = [share(whole, self.lines[n - 1])]
            return whole
        parts = self.jobs[0]
        head_bits = count_bits("head")
        members = len(parts)
        _, rows, d = parts[0].shape
        most = members * rows
        group = self.lines[0]

        def body(*refs):
            place = place_in(group, head_bits)
            sorted_ref = refs[-1]
            for m in range(3):
                for n in range(members):
                    at = pl.multiple_of((place ^ n) * rows, rows)
                    to = refs[members + m] if m < 2 else sorted_ref
                    to[pl.ds(at, rows)] = refs[n][m]
            for m in range(2):
                refs[members + m][most:] = sorted_ref[m * most // 2 : (m + 1) * most // 2]

        outs = [shape(most + most // 2, d)] * 2
        scratch = [pltpu.VMEM((most, d), bf16)]
        wholes = kernel_call(body, self.label(), outs, parts, 8, scratch=scratch)
        a, b = self.plane
        self.orders = [[[a], [b]], [[b], [a]]]
        self.jobs = [share(whole, order[1]) for whole, order in zip(wholes, self.orders)]
        return wholes[0]

    def join_plane(self, n):
        wholes = put_together(self.jobs, [order[n] for order in self.orders], self.label())
        if n > 0:
            self.jobs = [share(w, order[0]) for w, order in zip(wholes, self.orders)]
        else:
            self.own = wholes
            self.got = [send_to(whole, 1) for whole in wholes]
        return wholes[0]

    def homes(self):
        most = self.rows
        homes = []
        for part in range(2):
            for first in range(2):
                for second in range(2):
                    at = (2 * first + second) * (most + most // 2)
                    row = part * 4 * most + (2 * first + second) * most
                    homes.append((part, at, 0, row, most))
                    x, y = (first, second) if part == 0 else (second, first)
                    row = (x + 2 * y) * most + part * most // 2
                    homes.append((part, at + most, 1, row, most // 2))
        return homes


def cast_outputs(total, homes, lengths, shapes, pieces, name):
    args = [*total.own, *total.got]
    count = len(total.own)
    d = total.own[0].shape[1]

    def body(*refs):
        core = core_index()
        outs, rest = refs[len(args) : len(args) + len(shapes)], refs[len(args) + len(shapes) :]
        held, ready, sems = rest[: len(shapes)], rest[len(shapes) : -1], rest[-1]
        copies = []
        for part, at, which, row, size in homes:
            mine, other = refs[part][at : at + size], refs[count + part][at : at + size]
            to = slice(row, row + size)
            ready[which][0, to] = jnp.where(core == 0, mine, other)
            ready[which][1, to] = jnp.where(core == 0, other, mine)
        for which, side, start, size, n, place, turned in pieces:
            block = ready[which][side, start : start + size]
            to = pl.ds(place, size)
            if turned:
                index = (slice(None), to)
                held[n][index] = block.T.astype(f32)
            else:
                index = (to, slice(None))
                held[n][index] = block.astype(f32)
            copies.append(
                pltpu.make_async_copy(
                    held[n].at[index], outs[n].at[index], sems.at[len(copies)]
                )
            )
            copies[-1].start()
        for copy in copies:
            copy.wait()

    scratch = [pltpu.VMEM(s.shape, f32) for s in shapes]
    scratch += [pltpu.VMEM((2, rows, d), bf16) for rows in lengths]
    scratch.append(pltpu.SemaphoreType.DMA((len(pieces),)))
    outs = [ANY] * len(shapes)
    mib = 14 + sum(s.shape[0] * s.shape[1] * 4 for s in shapes) // 2**20
    return kernel_call(body, name, shapes, args, mib, None, outs, scratch)


def late_outputs(total, d, ff):
    half, size = ff // 2, d // 2
    rows = total.own[0].shape[0]
    pieces = []
    for side in range(2):
        for start in range(0, d, size):
            pieces.append((0, side, start, size, 0, side * d + start, False))
        for start in range(0, half, size):
            pieces.append((0, side, d + start, size, 1, side * half + start, False))
            pieces.append((0, side, d + half + start, size, 2, side * half + start, True))
    shapes = [shape(2 * d, d, f32), shape(ff, d, f32), shape(d, ff, f32)]
    homes = [(part, 0, 0, part * rows, rows) for part in range(2)]
    return cast_outputs(total, homes, [2 * rows], shapes, pieces, "late_outputs")


def joint_outputs(total, d, count):
    half = d // 2
    pieces = []
    for side in range(2):
        for n in range(3):
            pieces.append((1, side, n * half, half, 5, n * d + side * half, True))
        pieces.append((0, side, 0, half, 0, side * half, False))
        pieces.append((0, side, half, half, 1, side * half, True))
        pieces.append((0, side, d, half, 2, side * d, True))
        pieces.append((0, side, d + half, half, 2, side * d + half, True))
        pieces.append((0, side, 2 * d, half, 3, side * half, False))
    pieces.append((0, 0, 2 * d + half, count, 4, 0, False))
    shapes = [shape(d, d, f32), shape(d, d, f32), shape(d, 2 * d, f32), shape(d, d, f32)]
    shapes += [shape(count, d, f32), shape(d, 3 * d, f32)]
    lengths = [3 * d, 3 * half]
    return cast_outputs(total, total.homes(), lengths, shapes, pieces, "joint_outputs")


def swap(block, axis, bit):
    devices = range(lax.axis_size(axis))
    return lax.ppermute(block, axis, [(i, i ^ bit) for i in devices])


def after(value, *tokens):
    return lax.optimization_barrier((value, *tokens))[0]


def shifted(block, axis, distance):
    devices = range(lax.axis_size(axis))
    route = [(i - distance, i) for i in devices if i - distance in devices]
    return lax.ppermute(block, axis, route)


def normed(values):
    centred = values - jnp.mean(values, axis=-1, keepdims=True)
    spread = jnp.mean(centred * centred, axis=-1, keepdims=True)
    inverse = lax.rsqrt(spread + epsilon)
    return centred * inverse, inverse


def shards(
    tokens,
    memory,
    lengths,
    self_qkv,
    self_out,
    cross_q,
    cross_kv,
    cross_out,
    ffn_in,
    ffn_in_bias,
    ffn_out,
    ffn_out_bias,
    slot_weight,
    slot_bias,
    norm_gain,
    norm_shift,
    cotangent,
):
    tokens, memory, cotangent, length = tokens[0], memory[0], cotangent[0], lengths[0]
    rows, d = tokens.shape
    ff = ffn_in.shape[1]
    me = lax.axis_index("head")

    other_tokens, facing_tokens = swap(tokens, "head", 1), swap(tokens, "head", 2)
    local = jnp.arange(rows, dtype=jnp.int32)
    positions = me * rows + local
    live_slots = (positions < length - 1)[:, None]
    extra_index = jnp.arange(HEAD_DIM)[:, None]
    ones_rows = ((extra_index >= 1) & (extra_index <= 3)).astype(f32)

    def extra_of(members):
        key_positions = jnp.concatenate([(me ^ n) * rows + local for n in members])
        dead = (key_positions >= length)[None, :]
        return jnp.where((extra_index == 0) & dead, masked_score, ones_rows).astype(bf16)

    near_extra, far_extra = extra_of((0, 1)), extra_of((2, 3))
    cross_extra = jnp.broadcast_to(ones_rows, (HEAD_DIM, 4 * memory.shape[0])).astype(bf16)

    q_t, *near_keyed, near_sums = attend_near(tokens, other_tokens, self_qkv, near_extra)
    cotangent = after(cotangent, near_sums)
    slot_grad = jnp.where(live_slots, cotangent, 0.0).astype(bf16)
    before = shifted(slot_grad[-1:], "head", 1)
    slot_grads = jnp.stack([slot_grad, jnp.concatenate([before, slot_grad[:-1]], axis=0)])
    third_grad = dot(slot_grads[0], slot_weight[:d], 1, 1) + dot(
        slot_grads[1], slot_weight[d:], 1, 1
    )
    grad_slot_bias = jnp.sum(slot_grad.astype(f32), axis=0, keepdims=True)

    facing_tokens = after(facing_tokens, third_grad)
    token_blocks = (tokens, other_tokens, facing_tokens, swap(facing_tokens, "head", 1))
    facing_memory = swap(after(memory, facing_tokens), "head", 2)
    *far_keyed, context, queries = attend_far(
        *token_blocks[2:], self_qkv, q_t, near_keyed, near_sums, near_extra, far_extra
    )
    facing_memory = after(facing_memory, queries)
    memory_blocks = (
        memory,
        swap(memory, "head", 1),
        facing_memory,
        swap(facing_memory, "head", 1),
    )
    first_in = tokens.astype(f32) + dot(context, self_out)
    first_norm = normed(first_in)[0] * norm_gain[0] + norm_shift[0]
    first_low = first_norm.astype(bf16)

    mem_k, mem_v, cross_context, cross_queries = attend_memory(
        memory_blocks, cross_kv, first_low, cross_q, cross_extra
    )
    third_low, second_in_grad, cross_branch, cross_grad, late_sums, in_bias, *late_grads = (
        feed_forward(
            cross_context,
            first_norm,
            third_grad,
            slot_grads,
            (cross_out, ffn_in, ffn_out),
            (ffn_in_bias[None], ffn_out_bias[None]),
            norm_gain,
            norm_shift,
        )
    )
    late = Sum(*late_grads, "late", True, AT_ONCE[0])
    heads = d // HEAD_DIM
    keyed = [(*near_keyed, near_extra), (*far_keyed, far_extra)]
    made = {}
    state = {"token": late_grads[0]}

    def later(value):
        return after(value, state["token"])

    def cross_backward():
        attention = attend_backward(
            cross_queries,
            [(mem_k, mem_v, cross_extra)],
            cross_context,
            later(cross_grad),
            0,
            heads,
        )
        *made["cross"], grad, made["branch"], made["back"], made["early_sums"] = run(
            "cross_backward",
            cross_and_first_backward(
                attention, second_in_grad, first_in, norm_gain[:1], cross_q, self_out
            ),
        )
        made["first"] = grad
        return grad

    def middle_part():
        cross_dq, mem_dk, mem_dv = made["cross"]
        send, keep = middle_grads(
            cross_context,
            cross_branch,
            cross_dq,
            first_low,
            mem_dk,
            mem_dv,
            memory_blocks,
            context,
            made["branch"],
            (in_bias, later(late_sums), made["early_sums"], grad_slot_bias),
        )
        made["M"] = Sum(send, keep, "middle", True, AT_ONCE[1])
        return send

    def self_backward(n):
        half = heads // 2
        made["self", n] = run(
            "self_backward",
            attend_backward(queries, keyed, context, later(made["back"]), n * half, half),
        )
        return made["self", n][0]

    def early_part():
        dqs, dks, dvs = zip(made["self", 0], made["self", 1])
        send, keep = early_grads(dqs, dks, dvs, (later(tokens), *token_blocks[1:]))
        made["E"] = Sum(send, keep, "early", False, AT_ONCE[1])
        return send

    def partial_part():
        _, dks, dvs = zip(made["self", 0], made["self", 1])
        _, mem_dk, mem_dv = made["cross"]
        near, facing, other = project_back(
            [(dks, dvs), ((mem_dk,), (mem_dv,))], [later(self_qkv), cross_kv], "input_partial"
        )
        got = send_to(other, 1)
        made["near"] = near.astype(f32) + got[: near.shape[0]].astype(f32)
        made["facing"] = [facing, got[near.shape[0] :]]
        return near

    def send_facing():
        facing, got = made["facing"]
        facing = add_up([[facing, later(got)]], [[]], "facing")[0][0]
        made["got"] = send_to(facing, 2)
        return facing

    def send_first_row():
        first = later(third_low[:1])
        made["arriving"] = shifted(first, "head", -1)
        return first

    def slots_done():
        following = jnp.concatenate([third_low[1:], later(made["arriving"])], axis=0)
        slot_pre = (
            dot(third_low, slot_weight[:d])
            + dot(following, slot_weight[d:])
            + slot_bias.astype(f32)
        )
        made["slots"] = jnp.where(live_slots, slot_pre, 0.0).astype(bf16)
        return made["slots"]

    def inputs_done():
        near = made["near"] + later(made["got"]).astype(f32)
        total = made["first"] + near[:rows]
        for n in range(2):
            part = made["self", n][0]
            size = part.shape[0]
            total = total + dot(part, self_qkv[:, n * size : (n + 1) * size], 0, 1)
        made["token_grad"] = total.astype(bf16)
        made["memory_grad"] = near[rows:].astype(bf16)
        return made["token_grad"]

    made["L"] = late
    def along(count, usual):
        lines = list(range(count))
        cuts = [lines[n : n + 1] for n in range(usual - 1)] + [lines[usual - 1 :]]
        steps = [[("cut_line", n) for n in cut] for cut in cuts] + [[("sum_line", None)]]
        return steps + [[("join_line", n) for n in reversed(cut)] for cut in reversed(cuts)]

    across = [[("cut_plane", 0)], [("cut_plane", 1)]]
    back = [[("join_plane", 1)], [("join_plane", 0)]]
    late_along = along(len(late.lines), 2 // AT_ONCE[0])
    joint_along = along(len(groups_of(AT_ONCE[1])[1]), 2 // AT_ONCE[1])
    steps = {"L": across + late_along + back, "M": across, "E": across[:1]}
    steps["J"] = joint_along + back

    parts = {
        "xb": cross_backward,
        "mg": middle_part,
        "sa": lambda: self_backward(0),
        "sb": lambda: self_backward(1),
        "eg": early_part,
        "tp": partial_part,
        "T1": send_facing,
        "T2": inputs_done,
        "S1": send_first_row,
        "S2": slots_done,
    }

    def outputs(name):
        total = made[name]
        total.own[0] = later(total.own[0])
        if name == "L":
            made["late"] = late_outputs(total, d, ff)
            return made["late"][0]
        made["joint"] = joint_outputs(total, d, -(-(ff // d + 8) // PAIR) * PAIR)
        return made["joint"][0]

    for name in ORDER:
        if name in parts:
            state["token"] = parts[name]()
        elif name[1] == "o":
            state["token"] = outputs(name[0])
        else:
            if name == "J1":
                made["J"] = Joint(made["M"], made["E"])
            total = made[name[0]]
            for step, n in steps[name[0]][int(name[1]) - 1]:
                total.tie(state["token"])
                state["token"] = getattr(total, step)(*([] if n is None else [n]))
    grad_cross_out, grad_cross_q, grad_cross_kv, grad_self_out, sums, grad_self_qkv = made["joint"]
    grad_slot_weight, grad_ffn_out, grad_ffn_in = made["late"]
    token_grad, memory_grad = made["token_grad"], made["memory_grad"]
    small = sums.reshape(-1)
    return (
        made["slots"][None],
        token_grad[None],
        memory_grad[None],
        grad_self_qkv,
        grad_self_out,
        grad_cross_q,
        grad_cross_kv,
        grad_cross_out,
        grad_ffn_in,
        small[:ff],
        grad_ffn_out,
        small[ff : ff + d],
        grad_slot_weight,
        small[ff + d : ff + 2 * d],
        small[ff + 2 * d : ff + 5 * d].reshape(3, d),
        small[ff + 5 * d : ff + 8 * d].reshape(3, d),
    )


def solution(mesh):
    split = P("dp", "head", None)
    return jax.shard_map(
        shards,
        mesh=mesh,
        in_specs=(split, split, P("dp")) + (P(),) * 13 + (split,),
        out_specs=(split,) * 3 + (P(),) * 13,
        check_vma=False,
    )
```

```python
import jax
import jax.numpy as jnp
from jax import lax
from jax.experimental import pallas as pl
from jax.experimental.pallas import tpu as pltpu
from jax.sharding import PartitionSpec as P

HEAD_DIM = 64
WIDE = 128
PAIR = 16
epsilon = 1e-05
masked_score = -1e30
log2_e = 1.4426950408889634
scale = HEAD_DIM**-0.5 * log2_e
largest_safe = 100.0
f32 = jnp.float32
bf16 = jnp.bfloat16
VMEM = pl.BlockSpec(memory_space=pltpu.VMEM)
ANY = pl.BlockSpec(memory_space=pl.ANY)


def dot(a, b, ca=1, cb=0):
    return lax.dot_general(a, b, (((ca,), (cb,)), ((), ())), preferred_element_type=f32)


def shape(rows, columns, dtype=bf16):
    return jax.ShapeDtypeStruct((rows, columns), dtype)


def kernel_call(body, name, outs, args, mib, specs=None, out_specs=None, scratch=()):
    return pl.pallas_call(
        body,
        out_shape=tuple(outs),
        in_specs=specs or [VMEM] * len(args),
        out_specs=tuple(out_specs or [VMEM] * len(outs)),
        scratch_shapes=list(scratch),
        compiler_params=pltpu.CompilerParams(vmem_limit_bytes=mib * 2**20),
        name=name,
    )(*args)


def span(start, size):
    return pl.ds(pl.multiple_of(start, size), size)


def in_parts(base, index, first, values):
    high = values.astype(bf16).astype(f32)
    rest = values - high
    middle = rest.astype(bf16).astype(f32)
    low = rest - middle
    base = jnp.where(index == first, high, base)
    base = jnp.where(index == first + 1, middle, base)
    return jnp.where(index == first + 2, low, base)


def feats(h):
    return span(h * HEAD_DIM, HEAD_DIM)


def with_one(q_t):
    sub = lax.broadcasted_iota(jnp.int32, q_t.shape, 0)
    return jnp.concatenate([q_t, jnp.where(sub == 0, 1.0, 0.0).astype(bf16)], axis=0)


def scores_of(q_more, k, e):
    return dot(jnp.concatenate([k, e], axis=0), q_more, 0, 0)


def weighted(p, v, e):
    return dot(jnp.concatenate([v, e[:PAIR]], axis=0), p.astype(bf16))


def plain_sums(q_more, keyed):
    totals = [None] * len(q_more)
    for k_ref, v_ref, e_ref in keyed:
        e = e_ref[...]
        for n, (h, q) in enumerate(q_more):
            p = jnp.exp2(scores_of(q, k_ref[feats(h)], e))
            part = weighted(p, v_ref[feats(h)], e)
            totals[n] = part if totals[n] is None else totals[n] + part
    return totals


def finish(h, pair, totals, tops, o_ref, qa_ref):
    outs = []
    for n, (total, top) in enumerate(zip(totals, tops)):
        weight = total[HEAD_DIM + 1 : HEAD_DIM + 2]
        outs.append(total[:HEAD_DIM] / weight)
        logs = jnp.log2(weight) if top is None else top + jnp.log2(weight)
        q = pair[n].astype(f32)
        sub = lax.broadcasted_iota(jnp.int32, q.shape, 0)
        more = in_parts(jnp.where(sub == 0, 1.0, 0.0), sub, 1, -logs)
        both = jnp.concatenate([more, q] if n else [q, more], axis=0)
        qa_ref[:, span((h + n) * WIDE, WIDE)] = both.astype(bf16).T
    o_ref[:, span(h * HEAD_DIM, WIDE)] = jnp.concatenate(outs, axis=0).astype(bf16).T


def attend_all(q_ref, keyed, first_sums, o_ref, qa_ref):
    heads = q_ref.shape[0] // HEAD_DIM
    group = 4

    def most(values):
        squares = jnp.sum(values * values, axis=0, keepdims=True)
        return jnp.max(squares, axis=1, keepdims=True)

    def step(i, carry):
        at = [i * group + n for n in range(group)]
        bound = jnp.zeros((1, 1), f32)
        for h in at:
            most_q = most(q_ref[feats(h)].astype(f32))
            for k_ref, _, _ in keyed:
                bound = jnp.maximum(bound, most_q * most(k_ref[feats(h)].astype(f32)))
        safe = bound[0, 0] < largest_safe**2

        @pl.when(safe)
        def _():
            held = [q_ref[feats(h)] for h in at]
            rest = keyed if first_sums is None else keyed[1:]
            totals = plain_sums([(h, with_one(q)) for h, q in zip(at, held)], rest)
            if first_sums is not None:
                totals = [total + first_sums[h] for total, h in zip(totals, at)]
            for n in range(0, group, 2):
                finish(at[n], held[n : n + 2], totals[n : n + 2], (None, None), o_ref, qa_ref)

        @pl.when(jnp.logical_not(safe))
        def _():
            def slow(n, c):
                held, totals, tops = [], [], []
                for m in range(2):
                    h = i * group + 2 * n + m
                    q_t = q_ref[feats(h)]
                    q = with_one(q_t)
                    top = jnp.full((1, q.shape[1]), -jnp.inf, f32)
                    for k_ref, _, e_ref in keyed:
                        s = scores_of(q, k_ref[feats(h)], e_ref[...])
                        top = jnp.maximum(top, jnp.max(s, axis=0, keepdims=True))
                    total = 0.0
                    for k_ref, v_ref, e_ref in keyed:
                        e = e_ref[...]
                        p = jnp.exp2(scores_of(q, k_ref[feats(h)], e) - top)
                        total = total + weighted(p, v_ref[feats(h)], e)
                    held.append(q_t)
                    totals.append(total)
                    tops.append(top)
                finish(i * group + 2 * n, held, totals, tops, o_ref, qa_ref)
                return c

            lax.fori_loop(0, group // 2, slow, 0)

        return carry

    lax.fori_loop(0, heads // group, step, 0)


def project_rows(weight, blocks, outs):
    w_t = weight.T
    features = w_t.shape[0] // len(outs)
    start = 0
    for block in blocks:
        size = block.shape[0]
        for n, out in enumerate(outs):
            w = w_t[n * features : (n + 1) * features]
            out[:, start : start + size] = dot(w, block[...], 1, 1).astype(bf16)
        start += size


def attend_near(tokens, other, self_qkv, extra):
    rows, d = tokens.shape
    heads = d // HEAD_DIM
    group = 4

    def body(a_ref, b_ref, w_ref, e_ref, q_ref, k_ref, v_ref, sums_ref):
        q_ref[...] = (dot(w_ref[:, :d].T, a_ref[...], 1, 1) * scale).astype(bf16)
        project_rows(w_ref[:, d:], (a_ref, b_ref), (k_ref, v_ref))

        def step(i, carry):
            at = [i * group + n for n in range(group)]
            q_more = [(h, with_one(q_ref[feats(h)])) for h in at]
            for h, total in zip(at, plain_sums(q_more, [(k_ref, v_ref, e_ref)])):
                sums_ref[h] = total
            return carry

        lax.fori_loop(0, heads // group, step, 0)

    outs = [shape(d, rows), shape(d, 2 * rows), shape(d, 2 * rows)]
    outs.append(jax.ShapeDtypeStruct((heads, HEAD_DIM + PAIR, rows), f32))
    return kernel_call(body, "attend_near", outs, (tokens, other, self_qkv, extra), 20)


def attend_far(facing, other, self_qkv, q_t, near, sums, near_extra, extra):
    rows, d = facing.shape
    heads = d // HEAD_DIM

    def body(a_ref, b_ref, w_ref, q_ref, nk, nv, s_ref, ne, e_ref, k_ref, v_ref, o_ref, qa_ref):
        project_rows(w_ref[:, d:], (a_ref, b_ref), (k_ref, v_ref))
        attend_all(q_ref, [(nk, nv, ne), (k_ref, v_ref, e_ref)], s_ref, o_ref, qa_ref)

    outs = [shape(d, 2 * rows), shape(d, 2 * rows), shape(rows, d), shape(rows, heads * WIDE)]
    args = (facing, other, self_qkv, q_t, *near, sums, near_extra, extra)
    return kernel_call(body, "attend_far", outs, args, 20)


def attend_memory(blocks, cross_kv, inputs, cross_q, extra):
    rows, d = inputs.shape
    heads = d // HEAD_DIM
    sources = sum(block.shape[0] for block in blocks)
    count = len(blocks)

    def body(*refs):
        w_ref, x_ref, wq_ref, e_ref, k_ref, v_ref, o_ref, qa_ref, q_ref = refs[count:]
        q_ref[...] = (dot(wq_ref[...].T, x_ref[...], 1, 1) * scale).astype(bf16)
        project_rows(w_ref[...], refs[:count], (k_ref, v_ref))
        attend_all(q_ref, [(k_ref, v_ref, e_ref)], None, o_ref, qa_ref)

    outs = [shape(d, sources), shape(d, sources), shape(rows, d), shape(rows, heads * WIDE)]
    args = (*blocks, cross_kv, inputs, cross_q, extra)
    scratch = [pltpu.VMEM((d, rows), bf16)]
    return kernel_call(body, "attend_memory", outs, args, 20, scratch=scratch)


def run(name, *pieces):
    args = [arg for _, _, ins, _ in pieces for arg in ins]
    outs = [out for _, results, _, _ in pieces for out in results]

    def body(*refs):
        start, end = 0, len(args)
        for part, results, ins, _ in pieces:
            part(*refs[start : start + len(ins)], *refs[end : end + len(results)])
            start, end = start + len(ins), end + len(results)

    return kernel_call(body, name, outs, args, max(piece[3] for piece in pieces))


def attend_backward(queries, keyed, outs, grads, first, heads):
    rows = queries.shape[0]
    sizes = [k.shape[1] for k, _, _ in keyed]
    group = 2
    features = heads * HEAD_DIM

    def body(q_ref, o_ref, g_ref, *refs):
        key_refs = [refs[3 * j : 3 * j + 3] for j in range(len(keyed))]
        dq_ref, dk_ref, dv_ref = refs[3 * len(keyed) :]
        lane = lax.broadcasted_iota(jnp.int32, (rows, WIDE), 1)
        low_half = lane < HEAD_DIM

        def step(i, carry):
            lanes = span((first + i * group) * HEAD_DIM, WIDE)
            g_low = g_ref[:, lanes]
            g = g_low.astype(f32)
            product = g * o_ref[:, lanes].astype(f32)
            g_t = g_low.T
            held = []
            for u in range(group):
                mine = low_half if u == 0 else jnp.logical_not(low_half)
                centre = jnp.sum(jnp.where(mine, product, 0.0), axis=1, keepdims=True)
                more = in_parts(jnp.zeros_like(g), lane, HEAD_DIM * (1 - u) + 1, -centre)
                q = q_ref[:, span((first + i * group + u) * WIDE, WIDE)]
                own = slice(u * HEAD_DIM, (u + 1) * HEAD_DIM)
                g_more = jnp.where(mine, g, more).astype(bf16)
                held.append((q, g_more, q.T[own], g_t[own]))
            totals = [None] * group
            start = 0
            for (k_ref, v_ref, e_ref), size in zip(key_refs, sizes):
                at = pl.ds(start, size)
                e = e_ref[...]
                for u, (q, g_more, q_t, g_own) in enumerate(held):
                    k = k_ref[feats(first + i * group + u)]
                    v = v_ref[feats(first + i * group + u)]
                    k_more = jnp.concatenate([e, k] if u else [k, e], axis=0)
                    v_more = jnp.concatenate([e, v] if u else [v, e], axis=0)
                    p = jnp.exp2(dot(q, k_more))
                    ds = (p * dot(g_more, v_more)).astype(bf16)
                    to = feats(i * group + u)
                    dv_ref[to, at] = dot(g_own, p.astype(bf16)).astype(bf16)
                    dk_ref[to, at] = (dot(q_t, ds) * (1.0 / log2_e)).astype(bf16)
                    part = dot(k, ds, 1, 1)
                    totals[u] = part if totals[u] is None else totals[u] + part
                start += size
            for u in range(group):
                dq_ref[feats(i * group + u)] = (totals[u] * HEAD_DIM**-0.5).astype(bf16)
            return carry

        lax.fori_loop(0, heads // group, step, 0)

    keys = sum(sizes)
    made = [shape(features, rows), shape(features, keys), shape(features, keys)]
    args = (queries, outs, grads, *[array for part in keyed for array in part])
    return body, made, args, 20


def back_through_norm(x, inverse, gain, upstream):
    g = upstream * gain
    mean_g = jnp.mean(g, axis=1, keepdims=True)
    mean_gx = jnp.mean(g * x, axis=1, keepdims=True)
    sums = [jnp.sum(part, axis=0, keepdims=True) for part in (upstream * x, upstream)]
    return inverse * (g - mean_g - x * mean_gx), *sums


def cross_and_first_backward(attention, upstream, first_in, gain, cross_q, self_out):
    inner, made, ins, mib = attention
    rows, d = first_in.shape
    args = (upstream, first_in, gain, cross_q, self_out, *ins)

    def body(u_ref, f_ref, g_ref, wq_ref, wo_ref, *refs):
        inner(*refs[: len(ins) + len(made)])
        dq_ref = refs[len(ins)]
        grad_ref, branch_ref, back_ref, sums_ref = refs[len(ins) + len(made) :]
        x, inverse = normed(f_ref[...])
        up = u_ref[...] + dot(dq_ref[...], wq_ref[...], 0, 1)
        grad, sums_ref[0:1], sums_ref[1:2] = back_through_norm(x, inverse, g_ref[...], up)
        grad_ref[...] = grad
        branch = grad.astype(bf16)
        branch_ref[...] = branch
        back_ref[...] = dot(branch, wo_ref[...], 1, 1).astype(bf16)

    outs = [*made, shape(rows, d, f32), shape(rows, d), shape(rows, d), shape(2, d, f32)]
    return body, outs, args, mib


def feed_forward(context, first_norm, third_grad, slot_grads, weights, biases, gains, shifts):
    rows, d = first_norm.shape
    cross_out, ffn_in, ffn_out = weights
    ff = ffn_in.shape[1]
    half = ff // 2
    bend, slope = 0.044715, (2.0 / jnp.pi) ** 0.5
    slope = float(slope)

    def body(*refs):
        c_ref, f_ref, u_ref, s_ref, wc_ref, wi_ref, wo_ref, bi_ref, bo_ref, g_ref, t_ref = refs[:11]
        third_ref, grad_ref, branch_ref, back_ref, sums_ref, in_ref, send_ref, keep_ref = refs[11:19]
        second_ref, hidden_ref, slope_ref, fg_ref, hg_ref = refs[19:]
        sums_ref[...] = jnp.zeros_like(sums_ref)
        x2, inverse2 = normed(f_ref[...] + dot(c_ref[...], wc_ref[...]))
        second = x2 * g_ref[1:2] + t_ref[1:2]
        low = second.astype(bf16)
        second_ref[...] = low
        total = second + bo_ref[...].astype(f32)
        for start in range(0, ff, d):
            part = pl.ds(start, d)
            pre = dot(low, wi_ref[:, part]) + bi_ref[:, part].astype(f32)
            square = pre * pre
            tanh = jnp.tanh(slope * pre * (1.0 + bend * square))
            hidden = (0.5 * pre * (1.0 + tanh)).astype(bf16)
            hidden_ref[:, part] = hidden
            steep = slope * (1.0 + 3.0 * bend * square)
            slope_ref[:, part] = 0.5 * (1.0 + tanh) + 0.5 * pre * (1.0 - tanh * tanh) * steep
            total = total + dot(hidden, wo_ref[part])
        x3, inverse3 = normed(total)
        third_ref[...] = (x3 * g_ref[2:3] + t_ref[2:3]).astype(bf16)
        grad3, gain3, shift3 = back_through_norm(x3, inverse3, g_ref[2:3], u_ref[...])
        ffn_grad = grad3.astype(bf16)
        fg_ref[...] = ffn_grad
        sums_ref[0:1] = gain3
        sums_ref[1:2] = shift3
        sums_ref[4:5] = jnp.sum(ffn_grad.astype(f32), axis=0, keepdims=True)
        total = grad3
        for start in range(0, ff, d):
            part = pl.ds(start, d)
            back = (dot(ffn_grad, wo_ref[part], 1, 1) * slope_ref[:, part]).astype(bf16)
            hg_ref[:, part] = back
            in_ref[:, part] = jnp.sum(back.astype(f32), axis=0, keepdims=True)
            total = total + dot(back, wi_ref[:, part], 1, 1)
        grad2, gain2, shift2 = back_through_norm(x2, inverse2, g_ref[1:2], total)
        sums_ref[2:3] = gain2
        sums_ref[3:4] = shift2
        grad_ref[...] = grad2
        branch = grad2.astype(bf16)
        branch_ref[...] = branch
        back_ref[...] = dot(branch, wc_ref[...], 1, 1).astype(bf16)
        core = core_index()
        for side, out_ref in ((1 - core, send_ref), (core, keep_ref)):
            columns = span(side * half, half)
            out_ref[:d] = dot(third_ref[...], s_ref[side], 0, 0).astype(bf16)
            out_ref[d : d + half] = dot(hidden_ref[:, columns], fg_ref[...], 0, 0).astype(bf16)
            out_ref[d + half :] = dot(hg_ref[:, columns], second_ref[...], 0, 0).astype(bf16)

    outs = [shape(rows, d), shape(rows, d, f32), shape(rows, d), shape(rows, d)]
    outs += [shape(8, d, f32), shape(1, ff, f32)] + [shape(d + 2 * half, d)] * 2
    args = (context, first_norm, third_grad, slot_grads, *weights, *biases, gains, shifts)
    scratch = [pltpu.VMEM((rows, d), bf16), pltpu.VMEM((rows, ff), bf16)]
    scratch += [pltpu.VMEM((rows, ff), f32), pltpu.VMEM((rows, d), bf16)]
    scratch += [pltpu.VMEM((rows, ff), bf16)]
    return kernel_call(body, "feed_forward", outs, args, 30, scratch=scratch)


def project_back(pairs, weights):
    sizes = [dks[0].shape[1] // 4 for dks, _ in pairs]
    d = weights[0].shape[0]
    rows = sum(sizes)
    args = list(weights) + [part for dks, dvs in pairs for part in (*dks, *dvs)]

    def body(*refs):
        ins = list(refs[len(weights) : len(args)])
        near, facing, other = refs[len(args) :]
        start = 0
        for (dks, dvs), size, w_ref in zip(pairs, sizes, refs):
            grads = [ins.pop(0) for _ in range(len(dks) + len(dvs))]
            for n, (out, at) in enumerate(((near, 0), (other, 0), (facing, 0), (other, rows))):
                total = None
                feature = w_ref.shape[1] - sum(ref.shape[0] for ref in grads)
                for ref in grads:
                    features = ref.shape[0]
                    w = w_ref[:, feature : feature + features]
                    part = dot(ref[:, n * size : (n + 1) * size], w, 0, 1)
                    total = part if total is None else total + part
                    feature += features
                out[pl.ds(at + start, size)] = total.astype(bf16)
            start += size

    outs = [shape(rows, d), shape(rows, d), shape(2 * rows, d)]
    return body, outs, args, 12


def core_index():
    return lax.axis_index("head") % 2


def keyed_grad(ref, rows, blocks):
    total, start = None, 0
    for block in blocks:
        size = block.shape[0]
        part = dot(ref[rows, start : start + size], block)
        total = part if total is None else total + part
        start += size
    return total.astype(bf16)


def middle_grads(outs, out_grads, dq_t, inputs, dk_t, dv_t, blocks, context, branch, sums):
    d = branch.shape[1]
    half = d // 2
    count = len(blocks)
    args = (*blocks, outs, out_grads, dq_t, inputs, dk_t, dv_t, context, branch, *sums)

    def body(*refs):
        o_ref, og_ref, q_ref, x_ref, k_ref, v_ref, c_ref, b_ref, *rest = refs[count:]
        in_bias, late, early, slot_bias, *to = rest
        core = core_index()
        small = [in_bias[:, n : n + d] for n in range(0, in_bias.shape[1], d)]
        small += [late[4:5], slot_bias[...], early[0:1], late[2:3], late[0:1]]
        small += [early[1:2], late[3:4], late[1:2]]
        rows = -(-len(small) // PAIR) * PAIR
        small.append(jnp.zeros((rows - len(small), d), f32))
        small = jnp.concatenate(small, axis=0)
        for side, out_ref in ((1 - core, to[0]), (core, to[1])):
            at = span(side * half, half)
            out_ref[:half] = dot(o_ref[:, at], og_ref[...], 0, 0).astype(bf16)
            out_ref[half:d] = dot(q_ref[at], x_ref[...]).astype(bf16)
            for n, ref in enumerate((k_ref, v_ref)):

                @pl.when(side == n)
                def _():
                    memory = [block[...] for block in refs[:count]]
                    out_ref[d : 2 * d] = keyed_grad(ref, slice(None), memory)

            out_ref[2 * d : 2 * d + half] = dot(c_ref[:, at], b_ref[...], 0, 0).astype(bf16)
            out_ref[2 * d + half + rows :] = jnp.zeros((half - rows, d), bf16)
            mine = jnp.where(side == 0, small, 0.0)
            out_ref[2 * d + half : 2 * d + half + rows] = mine.astype(bf16)

    out = shape(3 * d, d)
    return kernel_call(body, "middle_grads", [out, out], args, 16)


def early_grads(dqs_t, dks_t, dvs_t, blocks):
    rows, d = blocks[0].shape
    half = d // 2
    count = len(blocks)

    def body(*refs):
        calls = [refs[count + n : count + 6 : 2] for n in range(2)]
        core = core_index()
        for side, out_ref in ((1 - core, refs[-2]), (core, refs[-1])):
            for n, (q_ref, k_ref, v_ref) in enumerate(calls):

                @pl.when(side == n)
                def _():
                    inputs = [block[...] for block in refs[:count]]
                    out_ref[:half] = dot(q_ref[...], inputs[0]).astype(bf16)
                    out_ref[half:d] = keyed_grad(k_ref, slice(None), inputs)
                    out_ref[d:] = keyed_grad(v_ref, slice(None), inputs)

    out = shape(3 * half, d)
    return body, [out, out], (*blocks, *dqs_t, *dks_t, *dvs_t), 16


def place_in(group, head_bits):
    place = 0
    for n, bit in enumerate(group):
        if bit < head_bits:
            value = lax.axis_index("head") // (1 << bit) % 2
        else:
            value = lax.axis_index("dp") // (1 << (bit - head_bits)) % 2
        place = place + value * (1 << n)
    return place


def count_bits(axis):
    return (lax.axis_size(axis) - 1).bit_length()


def add_up(jobs, group_of, name, joint=False):
    outs, args = [], []
    head_bits = count_bits("head")
    count = len(group_of)
    for parts, group in zip(jobs, group_of):
        size = 1 << len(group)
        rows, d = parts[0].shape
        rows = rows // (size * count if joint else size)
        cut = (count, size, rows, d) if joint else (size, rows, d)
        args += [part.reshape(cut) for part in parts]
        outs += [shape(rows, d)] * size
    outs = outs * count if joint else outs

    def body(*refs):
        ins, results = list(refs[: len(args)]), list(refs[len(args) :])
        for m, group in enumerate(group_of):
            place = place_in(group, head_bits)
            if joint:
                first, *others = [ref.at[m] for ref in ins]
            else:
                first, *others = [ins.pop(0) for _ in jobs[m]]
            for n in range(1 << len(group)):
                total = first[place ^ n].astype(f32)
                for ref in others:
                    total += ref[place ^ n].astype(f32)
                results.pop(0)[...] = total.astype(bf16)

    blocks = list(kernel_call(body, name, outs, args, 8))
    return [[blocks.pop(0) for _ in range(1 << len(group))] for group in group_of]


def add_joint(jobs, group, name):
    head_bits = count_bits("head")
    size = 1 << len(group)
    rows, d = jobs[0][0].shape
    args = [part.reshape(size, rows // size, d) for parts in jobs for part in parts]

    def body(*refs):
        place = place_in(group, head_bits)
        ins, results = list(refs[: len(args)]), refs[len(args) :]
        for m, parts in enumerate(jobs):
            first, *others = [ins.pop(0) for _ in parts]
            for n in range(size):
                total = first[place ^ n].astype(f32)
                for ref in others:
                    total += ref[place ^ n].astype(f32)
                results[n][m] = total.astype(bf16)

    out = jax.ShapeDtypeStruct((len(jobs), rows // size, d), bf16)
    return list(kernel_call(body, name, [out] * size, args, 8))


def put_together(jobs, group_of, name):
    head_bits = count_bits("head")
    args = [part for parts in jobs for part in parts]
    outs = [
        jax.ShapeDtypeStruct((len(parts),) + parts[0].shape, parts[0].dtype) for parts in jobs
    ]

    def body(*refs):
        ins, results = list(refs[: len(args)]), refs[len(args) :]
        for parts, group, out in zip(jobs, group_of, results):
            place = place_in(group, head_bits)
            for n in range(len(parts)):
                out[place ^ n] = ins.pop(0)[...]

    joined = kernel_call(body, name, outs, args, 8)
    return [out.reshape(-1, out.shape[-1]) for out in joined]


def split_joint(parts, group, name):
    head_bits = count_bits("head")
    jobs, rows, d = parts[0].shape
    outs = [jax.ShapeDtypeStruct((len(parts), rows, d), bf16)] * jobs

    def body(*refs):
        place = place_in(group, head_bits)
        for m in range(jobs):
            for n in range(len(parts)):
                refs[len(parts) + m][place ^ n] = refs[n][m]

    joined = kernel_call(body, name, outs, parts, 8)
    return [out.reshape(-1, d) for out in joined]


def send_to(block, mask):
    devices = range(lax.axis_size("dp") * lax.axis_size("head"))
    return lax.ppermute(block, ("dp", "head"), [(i, i ^ mask) for i in devices])


def mask_of(group, n):
    return sum(1 << bit for m, bit in enumerate(group) if n >> m & 1)


def spread(blocks, group):
    return [blocks[0]] + [send_to(blocks[n], mask_of(group, n)) for n in range(1, len(blocks))]


def share(block, group):
    return [block] + [send_to(block, mask_of(group, n)) for n in range(1, 1 << len(group))]


def groups_of(at_once):
    bits = list(range(1, count_bits("dp") + count_bits("head")))
    plane = [1, count_bits("head")]
    rest = [bit for bit in bits if bit not in plane]
    return plane, [rest[n : n + at_once] for n in range(0, len(rest), at_once)]


AT_ONCE = (2, 1)
ORDER = (
    "xb", "L1", "mg", "sa", "L2", "M1", "sb", "L3", "M2", "eg", "L4", "E0",
    "T0", "T1", "S1", "E1", "J1", "L5", "S2", "J2", "J3", "L6", "J4", "T2",
    "J5", "J6", "L7", "Lo", "J7", "Jo",
)


class Sum:
    def __init__(self, send, keep, name, two, at_once):
        self.name, self.two = name, two
        self.plane, self.lines = groups_of(at_once)
        self.steps = 0
        self.jobs = [[keep, send_to(send, 1)]]

    def label(self):
        self.steps += 1
        return "%s_%d" % (self.name, self.steps)

    def tie(self, token):
        first = self.jobs[0][0]
        self.jobs[0][0] = lax.optimization_barrier((first, token))[0]

    def orders(self):
        a, b = self.plane
        return [[[a], [b]], [[b], [a]]] if self.two else [[self.plane]]

    def cut_plane(self, n):
        groups = [order[n] for order in self.orders()]
        blocks = add_up(self.jobs, groups, self.label(), self.two and n == 0)
        self.jobs = [spread(block, group) for block, group in zip(blocks, groups)]
        return blocks[0][0]

    def cut_line(self, n):
        jobs = self.jobs
        if n > 0:
            jobs = [[part.reshape(-1, part.shape[-1]) for part in jobs[0]]]
        blocks = add_joint(jobs, self.lines[n], self.label())
        self.jobs = [spread(blocks, self.lines[n])]
        return blocks[0]

    def sum_line(self):
        parts = self.jobs[0]
        whole = parts[0].shape
        flat = [part.reshape(-1, whole[-1]) for part in parts]
        total = add_up([flat], [[]], self.label())[0][0]
        self.jobs = [share(total.reshape(whole), self.lines[-1])]
        return total

    def join_line(self, n):
        if n == 0:
            self.jobs = [[part] for part in split_joint(self.jobs[0], self.lines[0], self.label())]
        else:
            self.jobs = [[put_together(self.jobs, [self.lines[n]], self.label())[0]]]
            whole = self.jobs[0][0]
            self.jobs = [share(whole.reshape(len(self.orders()), -1, whole.shape[-1]), self.lines[n - 1])]
            return whole
        groups = [order[-1] for order in self.orders()]
        token = self.jobs[0][0]
        self.jobs = [share(job[0], group) for job, group in zip(self.jobs, groups)]
        return token

    def join_plane(self, n):
        groups = [order[n] for order in self.orders()]
        wholes = put_together(self.jobs, groups, self.label())
        if n > 0:
            groups = [order[n - 1] for order in self.orders()]
            self.jobs = [share(whole, group) for whole, group in zip(wholes, groups)]
        else:
            self.own = wholes
            self.got = [send_to(whole, 1) for whole in wholes]
        return wholes[0]


class Joint:
    def __init__(self, halves, whole):
        self.jobs = [*halves.jobs, whole.jobs[0]]
        self.plane, self.lines = halves.plane, halves.lines
        self.name, self.steps = "joint", 0
        self.rows = whole.jobs[0][0].shape[0]

    tie, label = Sum.tie, Sum.label
    cut_line, sum_line = Sum.cut_line, Sum.sum_line

    def join_line(self, n):
        if n > 0:
            whole = put_together(self.jobs, [self.lines[n]], self.label())[0]
            whole = whole.reshape(3, -1, whole.shape[-1])
            self.jobs = [share(whole, self.lines[n - 1])]
            return whole
        parts = self.jobs[0]
        head_bits = count_bits("head")
        members = len(parts)
        _, rows, d = parts[0].shape
        most = members * rows
        group = self.lines[0]

        def body(*refs):
            place = place_in(group, head_bits)
            sorted_ref = refs[-1]
            for m in range(3):
                for n in range(members):
                    at = pl.multiple_of((place ^ n) * rows, rows)
                    to = refs[members + m] if m < 2 else sorted_ref
                    to[pl.ds(at, rows)] = refs[n][m]
            for m in range(2):
                refs[members + m][most:] = sorted_ref[m * most // 2 : (m + 1) * most // 2]

        outs = [shape(most + most // 2, d)] * 2
        scratch = [pltpu.VMEM((most, d), bf16)]
        wholes = kernel_call(body, self.label(), outs, parts, 8, scratch=scratch)
        a, b = self.plane
        self.orders = [[[a], [b]], [[b], [a]]]
        self.jobs = [share(whole, order[1]) for whole, order in zip(wholes, self.orders)]
        return wholes[0]

    def join_plane(self, n):
        wholes = put_together(self.jobs, [order[n] for order in self.orders], self.label())
        if n > 0:
            self.jobs = [share(w, order[0]) for w, order in zip(wholes, self.orders)]
        else:
            self.own = wholes
            self.got = [send_to(whole, 1) for whole in wholes]
        return wholes[0]

    def homes(self):
        most = self.rows
        homes = []
        for part in range(2):
            for first in range(2):
                for second in range(2):
                    at = (2 * first + second) * (most + most // 2)
                    row = part * 4 * most + (2 * first + second) * most
                    homes.append((part, at, 0, row, most))
                    x, y = (first, second) if part == 0 else (second, first)
                    row = (x + 2 * y) * most + part * most // 2
                    homes.append((part, at + most, 1, row, most // 2))
        return homes


def cast_outputs(total, homes, lengths, shapes, pieces, name, small=(), sums=None):
    args = [*total.own, *total.got]
    count = len(total.own)
    d = total.own[0].shape[1]

    def body(*refs):
        core = core_index()
        outs, rest = refs[len(args) : len(args) + len(shapes)], refs[len(args) + len(shapes) :]
        small_refs, rest = rest[: len(small)], rest[len(small) :]
        held, ready, sems = rest[: len(shapes)], rest[len(shapes) : -1], rest[-1]
        copies = []
        for part, at, which, row, size in homes:
            mine, other = refs[part][at : at + size], refs[count + part][at : at + size]
            to = slice(row, row + size)
            ready[which][0, to] = jnp.where(core == 0, mine, other)
            ready[which][1, to] = jnp.where(core == 0, other, mine)
        for which, side, start, size, n, place, turned in pieces:
            block = ready[which][side, start : start + size]
            to = pl.ds(place, size)
            if turned:
                index = (slice(None), to)
                held[n][index] = block.T.astype(f32)
            else:
                index = (to, slice(None))
                held[n][index] = block.astype(f32)
            copies.append(
                pltpu.make_async_copy(
                    held[n].at[index], outs[n].at[index], sems.at[len(copies)]
                )
            )
            copies[-1].start()
        if sums is not None:
            sums(ready, small_refs)
        for copy in copies:
            copy.wait()

    scratch = [pltpu.VMEM(s.shape, f32) for s in shapes]
    scratch += [pltpu.VMEM((2, rows, d), bf16) for rows in lengths]
    scratch.append(pltpu.SemaphoreType.DMA((len(pieces),)))
    outs = [ANY] * len(shapes) + [VMEM] * len(small)
    mib = 14 + sum(s.shape[0] * s.shape[1] * 4 for s in shapes) // 2**20
    return kernel_call(body, name, [*shapes, *small], args, mib, None, outs, scratch)


def late_outputs(total, d, ff):
    half, size = ff // 2, d // 2
    rows = total.own[0].shape[0]
    pieces = []
    for side in range(2):
        for start in range(0, d, size):
            pieces.append((0, side, start, size, 0, side * d + start, False))
        for start in range(0, half, size):
            pieces.append((0, side, d + start, size, 1, side * half + start, False))
            pieces.append((0, side, d + half + start, size, 2, side * half + start, True))
    shapes = [shape(2 * d, d, f32), shape(ff, d, f32), shape(d, ff, f32)]
    homes = [(part, 0, 0, part * rows, rows) for part in range(2)]
    return cast_outputs(total, homes, [2 * rows], shapes, pieces, "late_outputs")


def joint_outputs(total, d, count):
    half = d // 2
    pieces = []
    for side in range(2):
        for n in range(3):
            pieces.append((1, side, n * half, half, 4, n * d + side * half, True))
        pieces.append((0, side, 0, half, 0, side * half, False))
        pieces.append((0, side, half, half, 1, side * half, True))
        pieces.append((0, side, d, half, 2, side * d, True))
        pieces.append((0, side, d + half, half, 2, side * d + half, True))
        pieces.append((0, side, 2 * d, half, 3, side * half, False))
    shapes = [shape(d, d, f32), shape(d, d, f32), shape(d, 2 * d, f32), shape(d, d, f32)]
    shapes.append(shape(d, 3 * d, f32))
    lengths = [3 * d, 3 * half]

    def sums(ready, outs):
        rows = ready[0][0, 2 * d + half : 2 * d + half + PAIR].astype(f32)
        outs[0][...] = jnp.concatenate([rows[n : n + 1] for n in range(count)], axis=1)
        for n in range(2):
            outs[1 + n][...] = rows[count + n : count + n + 1]
            outs[3 + n][...] = rows[count + 2 + 3 * n : count + 5 + 3 * n]

    small = [shape(1, count * d, f32), shape(1, d, f32), shape(1, d, f32)]
    small += [shape(3, d, f32), shape(3, d, f32)]
    homes = total.homes()
    return cast_outputs(total, homes, lengths, shapes, pieces, "joint_outputs", small, sums)


def swap(block, axis, bit):
    devices = range(lax.axis_size(axis))
    return lax.ppermute(block, axis, [(i, i ^ bit) for i in devices])


def after(value, *tokens):
    return lax.optimization_barrier((value, *tokens))[0]


def shifted(block, axis, distance):
    devices = range(lax.axis_size(axis))
    route = [(i - distance, i) for i in devices if i - distance in devices]
    return lax.ppermute(block, axis, route)


def normed(values):
    centred = values - jnp.mean(values, axis=-1, keepdims=True)
    spread = jnp.mean(centred * centred, axis=-1, keepdims=True)
    inverse = lax.rsqrt(spread + epsilon)
    return centred * inverse, inverse


def shards(
    tokens,
    memory,
    lengths,
    self_qkv,
    self_out,
    cross_q,
    cross_kv,
    cross_out,
    ffn_in,
    ffn_in_bias,
    ffn_out,
    ffn_out_bias,
    slot_weight,
    slot_bias,
    norm_gain,
    norm_shift,
    cotangent,
):
    tokens, memory, cotangent, length = tokens[0], memory[0], cotangent[0], lengths[0]
    rows, d = tokens.shape
    ff = ffn_in.shape[1]
    me = lax.axis_index("head")

    other_tokens, facing_tokens = swap(tokens, "head", 1), swap(tokens, "head", 2)
    local = jnp.arange(rows, dtype=jnp.int32)
    positions = me * rows + local
    live_slots = (positions < length - 1)[:, None]
    extra_index = jnp.arange(HEAD_DIM)[:, None]
    ones_rows = ((extra_index >= 1) & (extra_index <= 3)).astype(f32)

    def extra_of(members):
        key_positions = jnp.concatenate([(me ^ n) * rows + local for n in members])
        dead = (key_positions >= length)[None, :]
        return jnp.where((extra_index == 0) & dead, masked_score, ones_rows).astype(bf16)

    near_extra, far_extra = extra_of((0, 1)), extra_of((2, 3))
    cross_extra = jnp.broadcast_to(ones_rows, (HEAD_DIM, 4 * memory.shape[0])).astype(bf16)

    q_t, *near_keyed, near_sums = attend_near(tokens, other_tokens, self_qkv, near_extra)
    cotangent = after(cotangent, near_sums)
    slot_grad = jnp.where(live_slots, cotangent, 0.0).astype(bf16)
    before = shifted(slot_grad[-1:], "head", 1)
    slot_grads = jnp.stack([slot_grad, jnp.concatenate([before, slot_grad[:-1]], axis=0)])
    third_grad = dot(slot_grads[0], slot_weight[:d], 1, 1) + dot(
        slot_grads[1], slot_weight[d:], 1, 1
    )
    grad_slot_bias = jnp.sum(slot_grad.astype(f32), axis=0, keepdims=True)

    facing_tokens = after(facing_tokens, third_grad)
    token_blocks = (tokens, other_tokens, facing_tokens, swap(facing_tokens, "head", 1))
    facing_memory = swap(after(memory, facing_tokens), "head", 2)
    *far_keyed, context, queries = attend_far(
        *token_blocks[2:], self_qkv, q_t, near_keyed, near_sums, near_extra, far_extra
    )
    facing_memory = after(facing_memory, queries)
    memory_blocks = (
        memory,
        swap(memory, "head", 1),
        facing_memory,
        swap(facing_memory, "head", 1),
    )
    first_in = tokens.astype(f32) + dot(context, self_out)
    first_norm = normed(first_in)[0] * norm_gain[0] + norm_shift[0]
    first_low = first_norm.astype(bf16)

    mem_k, mem_v, cross_context, cross_queries = attend_memory(
        memory_blocks, cross_kv, first_low, cross_q, cross_extra
    )
    third_low, second_in_grad, cross_branch, cross_grad, late_sums, in_bias, *late_grads = (
        feed_forward(
            cross_context,
            first_norm,
            third_grad,
            slot_grads,
            (cross_out, ffn_in, ffn_out),
            (ffn_in_bias[None], ffn_out_bias[None]),
            norm_gain,
            norm_shift,
        )
    )
    late = Sum(*late_grads, "late", True, AT_ONCE[0])
    heads = d // HEAD_DIM
    keyed = [(*near_keyed, near_extra), (*far_keyed, far_extra)]
    made = {}
    state = {"token": late_grads[0]}

    def later(value):
        return after(value, state["token"])

    def cross_backward():
        attention = attend_backward(
            cross_queries,
            [(mem_k, mem_v, cross_extra)],
            cross_context,
            later(cross_grad),
            0,
            heads,
        )
        *made["cross"], grad, made["branch"], made["back"], made["early_sums"] = run(
            "cross_backward",
            cross_and_first_backward(
                attention, second_in_grad, first_in, norm_gain[:1], cross_q, self_out
            ),
        )
        made["first"] = grad
        return grad

    def middle_part():
        cross_dq, mem_dk, mem_dv = made["cross"]
        send, keep = middle_grads(
            cross_context,
            cross_branch,
            cross_dq,
            first_low,
            mem_dk,
            mem_dv,
            memory_blocks,
            context,
            made["branch"],
            (in_bias, later(late_sums), made["early_sums"], grad_slot_bias),
        )
        made["M"] = Sum(send, keep, "middle", True, AT_ONCE[1])
        return send

    def self_backward(n):
        half = heads // 2
        made["self", n] = run(
            "self_backward",
            attend_backward(queries, keyed, context, later(made["back"]), n * half, half),
        )
        return made["self", n][0]

    def early_part():
        dqs, dks, dvs = zip(made["self", 0], made["self", 1])
        _, mem_dk, mem_dv = made["cross"]
        send, keep, near, facing, other = run(
            "early_grads",
            early_grads(dqs, dks, dvs, (later(tokens), *token_blocks[1:])),
            project_back([(dks, dvs), ((mem_dk,), (mem_dv,))], [self_qkv, cross_kv]),
        )
        made["parts"] = send, keep, near, facing, other
        return send

    def send_early():
        send, keep, _, _, _ = made["parts"]
        send = later(send)
        made["E"] = Sum(send, keep, "early", False, AT_ONCE[1])
        return send

    def send_inputs():
        _, _, near, facing, other = made["parts"]
        other = later(other)
        got = send_to(other, 1)
        made["near"] = near.astype(f32) + got[: near.shape[0]].astype(f32)
        made["facing"] = [facing, got[near.shape[0] :]]
        return other

    def send_facing():
        facing, got = made["facing"]
        facing = add_up([[facing, later(got)]], [[]], "facing")[0][0]
        made["got"] = send_to(facing, 2)
        return facing

    def send_first_row():
        first = later(third_low[:1])
        made["arriving"] = shifted(first, "head", -1)
        return first

    def slots_done():
        following = jnp.concatenate([third_low[1:], later(made["arriving"])], axis=0)
        slot_pre = (
            dot(third_low, slot_weight[:d])
            + dot(following, slot_weight[d:])
            + slot_bias.astype(f32)
        )
        made["slots"] = jnp.where(live_slots, slot_pre, 0.0).astype(bf16)
        return made["slots"]

    def inputs_done():
        near = made["near"] + later(made["got"]).astype(f32)
        total = made["first"] + near[:rows]
        for n in range(2):
            part = made["self", n][0]
            size = part.shape[0]
            total = total + dot(part, self_qkv[:, n * size : (n + 1) * size], 0, 1)
        made["token_grad"] = total.astype(bf16)
        made["memory_grad"] = near[rows:].astype(bf16)
        return made["token_grad"]

    made["L"] = late
    def along(count, usual):
        lines = list(range(count))
        cuts = [lines[n : n + 1] for n in range(usual - 1)] + [lines[usual - 1 :]]
        steps = [[("cut_line", n) for n in cut] for cut in cuts] + [[("sum_line", None)]]
        return steps + [[("join_line", n) for n in reversed(cut)] for cut in reversed(cuts)]

    across = [[("cut_plane", 0)], [("cut_plane", 1)]]
    back = [[("join_plane", 1)], [("join_plane", 0)]]
    late_along = along(len(late.lines), 2 // AT_ONCE[0])
    joint_along = along(len(groups_of(AT_ONCE[1])[1]), 2 // AT_ONCE[1])
    steps = {"L": across + late_along + back, "M": across, "E": across[:1]}
    steps["J"] = joint_along + back

    parts = {
        "xb": cross_backward,
        "mg": middle_part,
        "sa": lambda: self_backward(0),
        "sb": lambda: self_backward(1),
        "eg": early_part,
        "E0": send_early,
        "T0": send_inputs,
        "T1": send_facing,
        "T2": inputs_done,
        "S1": send_first_row,
        "S2": slots_done,
    }

    def outputs(name):
        total = made[name]
        total.own[0] = later(total.own[0])
        if name == "L":
            made["late"] = late_outputs(total, d, ff)
            return made["late"][0]
        made["joint"] = joint_outputs(total, d, ff // d)
        return made["joint"][0]

    for name in ORDER:
        if name in parts:
            state["token"] = parts[name]()
        elif name[1] == "o":
            state["token"] = outputs(name[0])
        else:
            if name == "J1":
                made["J"] = Joint(made["M"], made["E"])
            total = made[name[0]]
            for step, n in steps[name[0]][int(name[1]) - 1]:
                total.tie(state["token"])
                state["token"] = getattr(total, step)(*([] if n is None else [n]))
    grad_cross_out, grad_cross_q, grad_cross_kv, grad_self_out, grad_self_qkv, *sums = made["joint"]
    grad_in_bias, grad_out_bias, grad_slot_bias, norm_gain_grad, norm_shift_grad = sums
    grad_slot_weight, grad_ffn_out, grad_ffn_in = made["late"]
    token_grad, memory_grad = made["token_grad"], made["memory_grad"]
    return (
        made["slots"][None],
        token_grad[None],
        memory_grad[None],
        grad_self_qkv,
        grad_self_out,
        grad_cross_q,
        grad_cross_kv,
        grad_cross_out,
        grad_ffn_in,
        grad_in_bias[0],
        grad_ffn_out,
        grad_out_bias[0],
        grad_slot_weight,
        grad_slot_bias[0],
        norm_gain_grad,
        norm_shift_grad,
    )


def solution(mesh):
    split = P("dp", "head", None)
    return jax.shard_map(
        shards,
        mesh=mesh,
        in_specs=(split, split, P("dp")) + (P(),) * 13 + (split,),
        out_specs=(split,) * 3 + (P(),) * 13,
        check_vma=False,
    )
```

```python
import jax
import jax.numpy as jnp
from jax import lax
from jax.experimental import pallas as pl
from jax.experimental.pallas import tpu as pltpu
from jax.sharding import PartitionSpec as P

HEAD_DIM = 64
WIDE = 128
PAIR = 16
epsilon = 1e-05
masked_score = -1e30
log2_e = 1.4426950408889634
scale = HEAD_DIM**-0.5 * log2_e
largest_safe = 100.0
f32 = jnp.float32
bf16 = jnp.bfloat16
VMEM = pl.BlockSpec(memory_space=pltpu.VMEM)
ANY = pl.BlockSpec(memory_space=pl.ANY)


def dot(a, b, ca=1, cb=0):
    return lax.dot_general(a, b, (((ca,), (cb,)), ((), ())), preferred_element_type=f32)


def shape(rows, columns, dtype=bf16):
    return jax.ShapeDtypeStruct((rows, columns), dtype)


def kernel_call(body, name, outs, args, mib, specs=None, out_specs=None, scratch=()):
    return pl.pallas_call(
        body,
        out_shape=tuple(outs),
        in_specs=specs or [VMEM] * len(args),
        out_specs=tuple(out_specs or [VMEM] * len(outs)),
        scratch_shapes=list(scratch),
        compiler_params=pltpu.CompilerParams(vmem_limit_bytes=mib * 2**20),
        name=name,
    )(*args)


def span(start, size):
    return pl.ds(pl.multiple_of(start, size), size)


def in_parts(base, index, first, values):
    high = values.astype(bf16).astype(f32)
    rest = values - high
    middle = rest.astype(bf16).astype(f32)
    low = rest - middle
    base = jnp.where(index == first, high, base)
    base = jnp.where(index == first + 1, middle, base)
    return jnp.where(index == first + 2, low, base)


def feats(h):
    return span(h * HEAD_DIM, HEAD_DIM)


def with_one(q_t):
    sub = lax.broadcasted_iota(jnp.int32, q_t.shape, 0)
    return jnp.concatenate([q_t, jnp.where(sub == 0, 1.0, 0.0).astype(bf16)], axis=0)


def scores_of(q_more, k, e):
    return dot(jnp.concatenate([k, e], axis=0), q_more, 0, 0)


def weighted(p, v, e):
    return dot(jnp.concatenate([v, e[:PAIR]], axis=0), p.astype(bf16))


def plain_sums(q_more, keyed):
    totals = [None] * len(q_more)
    for k_ref, v_ref, e_ref in keyed:
        e = e_ref[...]
        for n, (h, q) in enumerate(q_more):
            p = jnp.exp2(scores_of(q, k_ref[feats(h)], e))
            part = weighted(p, v_ref[feats(h)], e)
            totals[n] = part if totals[n] is None else totals[n] + part
    return totals


def finish(h, pair, totals, tops, o_ref, qa_ref):
    outs = []
    for n, (total, top) in enumerate(zip(totals, tops)):
        weight = total[HEAD_DIM + 1 : HEAD_DIM + 2]
        outs.append(total[:HEAD_DIM] / weight)
        logs = jnp.log2(weight) if top is None else top + jnp.log2(weight)
        q = pair[n].astype(f32)
        sub = lax.broadcasted_iota(jnp.int32, q.shape, 0)
        more = in_parts(jnp.where(sub == 0, 1.0, 0.0), sub, 1, -logs)
        both = jnp.concatenate([more, q] if n else [q, more], axis=0)
        qa_ref[:, span((h + n) * WIDE, WIDE)] = both.astype(bf16).T
    o_ref[:, span(h * HEAD_DIM, WIDE)] = jnp.concatenate(outs, axis=0).astype(bf16).T


def attend_all(q_ref, keyed, first_sums, o_ref, qa_ref):
    heads = q_ref.shape[0] // HEAD_DIM
    group = 4

    def most(values):
        squares = jnp.sum(values * values, axis=0, keepdims=True)
        return jnp.max(squares, axis=1, keepdims=True)

    def step(i, carry):
        at = [i * group + n for n in range(group)]
        bound = jnp.zeros((1, 1), f32)
        for h in at:
            most_q = most(q_ref[feats(h)].astype(f32))
            for k_ref, _, _ in keyed:
                bound = jnp.maximum(bound, most_q * most(k_ref[feats(h)].astype(f32)))
        safe = bound[0, 0] < largest_safe**2

        @pl.when(safe)
        def _():
            held = [q_ref[feats(h)] for h in at]
            rest = keyed if first_sums is None else keyed[1:]
            totals = plain_sums([(h, with_one(q)) for h, q in zip(at, held)], rest)
            if first_sums is not None:
                totals = [total + first_sums[h] for total, h in zip(totals, at)]
            for n in range(0, group, 2):
                finish(at[n], held[n : n + 2], totals[n : n + 2], (None, None), o_ref, qa_ref)

        @pl.when(jnp.logical_not(safe))
        def _():
            def slow(n, c):
                held, totals, tops = [], [], []
                for m in range(2):
                    h = i * group + 2 * n + m
                    q_t = q_ref[feats(h)]
                    q = with_one(q_t)
                    top = jnp.full((1, q.shape[1]), -jnp.inf, f32)
                    for k_ref, _, e_ref in keyed:
                        s = scores_of(q, k_ref[feats(h)], e_ref[...])
                        top = jnp.maximum(top, jnp.max(s, axis=0, keepdims=True))
                    total = 0.0
                    for k_ref, v_ref, e_ref in keyed:
                        e = e_ref[...]
                        p = jnp.exp2(scores_of(q, k_ref[feats(h)], e) - top)
                        total = total + weighted(p, v_ref[feats(h)], e)
                    held.append(q_t)
                    totals.append(total)
                    tops.append(top)
                finish(i * group + 2 * n, held, totals, tops, o_ref, qa_ref)
                return c

            lax.fori_loop(0, group // 2, slow, 0)

        return carry

    lax.fori_loop(0, heads // group, step, 0)


def project_rows(weight, blocks, outs):
    w_t = weight.T
    features = w_t.shape[0] // len(outs)
    start = 0
    for block in blocks:
        size = block.shape[0]
        for n, out in enumerate(outs):
            w = w_t[n * features : (n + 1) * features]
            out[:, start : start + size] = dot(w, block[...], 1, 1).astype(bf16)
        start += size


def attend_near(tokens, other, self_qkv, extra):
    rows, d = tokens.shape
    heads = d // HEAD_DIM
    group = 4

    def body(a_ref, b_ref, w_ref, e_ref, q_ref, k_ref, v_ref, sums_ref):
        q_ref[...] = (dot(w_ref[:, :d].T, a_ref[...], 1, 1) * scale).astype(bf16)
        project_rows(w_ref[:, d:], (a_ref, b_ref), (k_ref, v_ref))

        def step(i, carry):
            at = [i * group + n for n in range(group)]
            q_more = [(h, with_one(q_ref[feats(h)])) for h in at]
            for h, total in zip(at, plain_sums(q_more, [(k_ref, v_ref, e_ref)])):
                sums_ref[h] = total
            return carry

        lax.fori_loop(0, heads // group, step, 0)

    outs = [shape(d, rows), shape(d, 2 * rows), shape(d, 2 * rows)]
    outs.append(jax.ShapeDtypeStruct((heads, HEAD_DIM + PAIR, rows), f32))
    return kernel_call(body, "attend_near", outs, (tokens, other, self_qkv, extra), 14)


def attend_far(facing, other, self_qkv, q_t, near, sums, near_extra, extra):
    rows, d = facing.shape
    heads = d // HEAD_DIM

    def body(a_ref, b_ref, w_ref, q_ref, nk, nv, s_ref, ne, e_ref, k_ref, v_ref, o_ref, qa_ref):
        project_rows(w_ref[:, d:], (a_ref, b_ref), (k_ref, v_ref))
        attend_all(q_ref, [(nk, nv, ne), (k_ref, v_ref, e_ref)], s_ref, o_ref, qa_ref)

    outs = [shape(d, 2 * rows), shape(d, 2 * rows), shape(rows, d), shape(rows, heads * WIDE)]
    args = (facing, other, self_qkv, q_t, *near, sums, near_extra, extra)
    return kernel_call(body, "attend_far", outs, args, 14)


def attend_memory(blocks, cross_kv, inputs, cross_q, extra):
    rows, d = inputs.shape
    heads = d // HEAD_DIM
    sources = sum(block.shape[0] for block in blocks)
    count = len(blocks)

    def body(*refs):
        w_ref, x_ref, wq_ref, e_ref, k_ref, v_ref, o_ref, qa_ref, q_ref = refs[count:]
        q_ref[...] = (dot(wq_ref[...].T, x_ref[...], 1, 1) * scale).astype(bf16)
        project_rows(w_ref[...], refs[:count], (k_ref, v_ref))
        attend_all(q_ref, [(k_ref, v_ref, e_ref)], None, o_ref, qa_ref)

    outs = [shape(d, sources), shape(d, sources), shape(rows, d), shape(rows, heads * WIDE)]
    args = (*blocks, cross_kv, inputs, cross_q, extra)
    scratch = [pltpu.VMEM((d, rows), bf16)]
    return kernel_call(body, "attend_memory", outs, args, 14, scratch=scratch)


def run(name, *pieces):
    args = [arg for _, _, ins, _ in pieces for arg in ins]
    outs = [out for _, results, _, _ in pieces for out in results]

    def body(*refs):
        start, end = 0, len(args)
        for part, results, ins, _ in pieces:
            part(*refs[start : start + len(ins)], *refs[end : end + len(results)])
            start, end = start + len(ins), end + len(results)

    return kernel_call(body, name, outs, args, max(piece[3] for piece in pieces))


def attend_backward(queries, keyed, outs, grads, first, heads):
    rows = queries.shape[0]
    sizes = [k.shape[1] for k, _, _ in keyed]
    group = 2
    features = heads * HEAD_DIM

    def body(q_ref, o_ref, g_ref, *refs):
        key_refs = [refs[3 * j : 3 * j + 3] for j in range(len(keyed))]
        dq_ref, dk_ref, dv_ref = refs[3 * len(keyed) :]
        lane = lax.broadcasted_iota(jnp.int32, (rows, WIDE), 1)
        low_half = lane < HEAD_DIM

        def step(i, carry):
            lanes = span((first + i * group) * HEAD_DIM, WIDE)
            g_low = g_ref[:, lanes]
            g = g_low.astype(f32)
            product = g * o_ref[:, lanes].astype(f32)
            g_t = g_low.T
            held = []
            for u in range(group):
                mine = low_half if u == 0 else jnp.logical_not(low_half)
                centre = jnp.sum(jnp.where(mine, product, 0.0), axis=1, keepdims=True)
                more = in_parts(jnp.zeros_like(g), lane, HEAD_DIM * (1 - u) + 1, -centre)
                q = q_ref[:, span((first + i * group + u) * WIDE, WIDE)]
                own = slice(u * HEAD_DIM, (u + 1) * HEAD_DIM)
                g_more = jnp.where(mine, g, more).astype(bf16)
                held.append((q, g_more, q.T[own], g_t[own]))
            totals = [None] * group
            start = 0
            for (k_ref, v_ref, e_ref), size in zip(key_refs, sizes):
                at = pl.ds(start, size)
                e = e_ref[...]
                for u, (q, g_more, q_t, g_own) in enumerate(held):
                    k = k_ref[feats(first + i * group + u)]
                    v = v_ref[feats(first + i * group + u)]
                    k_more = jnp.concatenate([e, k] if u else [k, e], axis=0)
                    v_more = jnp.concatenate([e, v] if u else [v, e], axis=0)
                    p = jnp.exp2(dot(q, k_more))
                    ds = (p * dot(g_more, v_more)).astype(bf16)
                    to = feats(i * group + u)
                    dv_ref[to, at] = dot(g_own, p.astype(bf16)).astype(bf16)
                    dk_ref[to, at] = (dot(q_t, ds) * (1.0 / log2_e)).astype(bf16)
                    part = dot(k, ds, 1, 1)
                    totals[u] = part if totals[u] is None else totals[u] + part
                start += size
            for u in range(group):
                dq_ref[feats(i * group + u)] = (totals[u] * HEAD_DIM**-0.5).astype(bf16)
            return carry

        lax.fori_loop(0, heads // group, step, 0)

    keys = sum(sizes)
    made = [shape(features, rows), shape(features, keys), shape(features, keys)]
    args = (queries, outs, grads, *[array for part in keyed for array in part])
    return body, made, args, 14


def back_through_norm(x, inverse, gain, upstream):
    g = upstream * gain
    mean_g = jnp.mean(g, axis=1, keepdims=True)
    mean_gx = jnp.mean(g * x, axis=1, keepdims=True)
    sums = [jnp.sum(part, axis=0, keepdims=True) for part in (upstream * x, upstream)]
    return inverse * (g - mean_g - x * mean_gx), *sums


def cross_and_first_backward(attention, upstream, first_in, gain, cross_q, self_out):
    inner, made, ins, mib = attention
    rows, d = first_in.shape
    args = (upstream, first_in, gain, cross_q, self_out, *ins)

    def body(u_ref, f_ref, g_ref, wq_ref, wo_ref, *refs):
        inner(*refs[: len(ins) + len(made)])
        dq_ref = refs[len(ins)]
        grad_ref, branch_ref, back_ref, sums_ref = refs[len(ins) + len(made) :]
        x, inverse = normed(f_ref[...])
        up = u_ref[...] + dot(dq_ref[...], wq_ref[...], 0, 1)
        grad, sums_ref[0:1], sums_ref[1:2] = back_through_norm(x, inverse, g_ref[...], up)
        grad_ref[...] = grad
        branch = grad.astype(bf16)
        branch_ref[...] = branch
        back_ref[...] = dot(branch, wo_ref[...], 1, 1).astype(bf16)

    outs = [*made, shape(rows, d, f32), shape(rows, d), shape(rows, d), shape(2, d, f32)]
    return body, outs, args, mib


def feed_forward(context, first_norm, third_grad, slot_grads, weights, biases, gains, shifts):
    rows, d = first_norm.shape
    cross_out, ffn_in, ffn_out = weights
    ff = ffn_in.shape[1]
    half = ff // 2
    bend, slope = 0.044715, (2.0 / jnp.pi) ** 0.5
    slope = float(slope)

    def body(*refs):
        c_ref, f_ref, u_ref, s_ref, wc_ref, wi_ref, wo_ref, bi_ref, bo_ref, g_ref, t_ref = refs[:11]
        third_ref, grad_ref, branch_ref, back_ref, sums_ref, in_ref, send_ref, keep_ref = refs[11:19]
        second_ref, hidden_ref, slope_ref, fg_ref, hg_ref = refs[19:]
        sums_ref[...] = jnp.zeros_like(sums_ref)
        x2, inverse2 = normed(f_ref[...] + dot(c_ref[...], wc_ref[...]))
        second = x2 * g_ref[1:2] + t_ref[1:2]
        low = second.astype(bf16)
        second_ref[...] = low
        total = second + bo_ref[...].astype(f32)
        for start in range(0, ff, d):
            part = pl.ds(start, d)
            pre = dot(low, wi_ref[:, part]) + bi_ref[:, part].astype(f32)
            square = pre * pre
            tanh = jnp.tanh(slope * pre * (1.0 + bend * square))
            hidden = (0.5 * pre * (1.0 + tanh)).astype(bf16)
            hidden_ref[:, part] = hidden
            steep = slope * (1.0 + 3.0 * bend * square)
            slope_ref[:, part] = 0.5 * (1.0 + tanh) + 0.5 * pre * (1.0 - tanh * tanh) * steep
            total = total + dot(hidden, wo_ref[part])
        x3, inverse3 = normed(total)
        third_ref[...] = (x3 * g_ref[2:3] + t_ref[2:3]).astype(bf16)
        grad3, gain3, shift3 = back_through_norm(x3, inverse3, g_ref[2:3], u_ref[...])
        ffn_grad = grad3.astype(bf16)
        fg_ref[...] = ffn_grad
        sums_ref[0:1] = gain3
        sums_ref[1:2] = shift3
        sums_ref[4:5] = jnp.sum(ffn_grad.astype(f32), axis=0, keepdims=True)
        total = grad3
        for start in range(0, ff, d):
            part = pl.ds(start, d)
            back = (dot(ffn_grad, wo_ref[part], 1, 1) * slope_ref[:, part]).astype(bf16)
            hg_ref[:, part] = back
            in_ref[:, part] = jnp.sum(back.astype(f32), axis=0, keepdims=True)
            total = total + dot(back, wi_ref[:, part], 1, 1)
        grad2, gain2, shift2 = back_through_norm(x2, inverse2, g_ref[1:2], total)
        sums_ref[2:3] = gain2
        sums_ref[3:4] = shift2
        grad_ref[...] = grad2
        branch = grad2.astype(bf16)
        branch_ref[...] = branch
        back_ref[...] = dot(branch, wc_ref[...], 1, 1).astype(bf16)
        core = core_index()
        for side, out_ref in ((1 - core, send_ref), (core, keep_ref)):
            columns = span(side * half, half)
            out_ref[:d] = dot(third_ref[...], s_ref[side], 0, 0).astype(bf16)
            out_ref[d : d + half] = dot(hidden_ref[:, columns], fg_ref[...], 0, 0).astype(bf16)
            out_ref[d + half :] = dot(hg_ref[:, columns], second_ref[...], 0, 0).astype(bf16)

    outs = [shape(rows, d), shape(rows, d, f32), shape(rows, d), shape(rows, d)]
    outs += [shape(8, d, f32), shape(1, ff, f32)] + [shape(d + 2 * half, d)] * 2
    args = (context, first_norm, third_grad, slot_grads, *weights, *biases, gains, shifts)
    scratch = [pltpu.VMEM((rows, d), bf16), pltpu.VMEM((rows, ff), bf16)]
    scratch += [pltpu.VMEM((rows, ff), f32), pltpu.VMEM((rows, d), bf16)]
    scratch += [pltpu.VMEM((rows, ff), bf16)]
    return kernel_call(body, "feed_forward", outs, args, 22, scratch=scratch)


def project_back(pairs, weights):
    sizes = [dks[0].shape[1] // 4 for dks, _ in pairs]
    d = weights[0].shape[0]
    rows = sum(sizes)
    args = list(weights) + [part for dks, dvs in pairs for part in (*dks, *dvs)]

    def body(*refs):
        ins = list(refs[len(weights) : len(args)])
        near, facing, other = refs[len(args) :]
        start = 0
        for (dks, dvs), size, w_ref in zip(pairs, sizes, refs):
            grads = [ins.pop(0) for _ in range(len(dks) + len(dvs))]
            for n, (out, at) in enumerate(((near, 0), (other, 0), (facing, 0), (other, rows))):
                total = None
                feature = w_ref.shape[1] - sum(ref.shape[0] for ref in grads)
                for ref in grads:
                    features = ref.shape[0]
                    w = w_ref[:, feature : feature + features]
                    part = dot(ref[:, n * size : (n + 1) * size], w, 0, 1)
                    total = part if total is None else total + part
                    feature += features
                out[pl.ds(at + start, size)] = total.astype(bf16)
            start += size

    outs = [shape(rows, d), shape(rows, d), shape(2 * rows, d)]
    return body, outs, args, 12


def core_index():
    return lax.axis_index("head") % 2


def keyed_grad(ref, rows, blocks):
    total, start = None, 0
    for block in blocks:
        size = block.shape[0]
        part = dot(ref[rows, start : start + size], block)
        total = part if total is None else total + part
        start += size
    return total.astype(bf16)


def middle_grads(outs, out_grads, dq_t, inputs, dk_t, dv_t, blocks, context, branch, sums):
    d = branch.shape[1]
    half = d // 2
    count = len(blocks)
    args = (*blocks, outs, out_grads, dq_t, inputs, dk_t, dv_t, context, branch, *sums)

    def body(*refs):
        o_ref, og_ref, q_ref, x_ref, k_ref, v_ref, c_ref, b_ref, *rest = refs[count:]
        in_bias, late, early, slot_bias, *to = rest
        core = core_index()
        small = [in_bias[:, n : n + d] for n in range(0, in_bias.shape[1], d)]
        small += [late[4:5], slot_bias[...], early[0:1], late[2:3], late[0:1]]
        small += [early[1:2], late[3:4], late[1:2]]
        rows = -(-len(small) // PAIR) * PAIR
        small.append(jnp.zeros((rows - len(small), d), f32))
        small = jnp.concatenate(small, axis=0)
        for side, out_ref in ((1 - core, to[0]), (core, to[1])):
            at = span(side * half, half)
            out_ref[:half] = dot(o_ref[:, at], og_ref[...], 0, 0).astype(bf16)
            out_ref[half:d] = dot(q_ref[at], x_ref[...]).astype(bf16)
            for n, ref in enumerate((k_ref, v_ref)):

                @pl.when(side == n)
                def _():
                    memory = [block[...] for block in refs[:count]]
                    out_ref[d : 2 * d] = keyed_grad(ref, slice(None), memory)

            out_ref[2 * d : 2 * d + half] = dot(c_ref[:, at], b_ref[...], 0, 0).astype(bf16)
            out_ref[2 * d + half + rows :] = jnp.zeros((half - rows, d), bf16)
            mine = jnp.where(side == 0, small, 0.0)
            out_ref[2 * d + half : 2 * d + half + rows] = mine.astype(bf16)

    out = shape(3 * d, d)
    return kernel_call(body, "middle_grads", [out, out], args, 16)


def early_grads(dqs_t, dks_t, dvs_t, blocks):
    rows, d = blocks[0].shape
    half = d // 2
    count = len(blocks)

    def body(*refs):
        calls = [refs[count + n : count + 6 : 2] for n in range(2)]
        core = core_index()
        for side, out_ref in ((1 - core, refs[-2]), (core, refs[-1])):
            for n, (q_ref, k_ref, v_ref) in enumerate(calls):

                @pl.when(side == n)
                def _():
                    inputs = [block[...] for block in refs[:count]]
                    out_ref[:half] = dot(q_ref[...], inputs[0]).astype(bf16)
                    out_ref[half:d] = keyed_grad(k_ref, slice(None), inputs)
                    out_ref[d:] = keyed_grad(v_ref, slice(None), inputs)

    out = shape(3 * half, d)
    return body, [out, out], (*blocks, *dqs_t, *dks_t, *dvs_t), 12


def place_in(group, head_bits):
    place = 0
    for n, bit in enumerate(group):
        if bit < head_bits:
            value = lax.axis_index("head") // (1 << bit) % 2
        else:
            value = lax.axis_index("dp") // (1 << (bit - head_bits)) % 2
        place = place + value * (1 << n)
    return place


def count_bits(axis):
    return (lax.axis_size(axis) - 1).bit_length()


def add_up(jobs, group_of, name, joint=False):
    outs, args = [], []
    head_bits = count_bits("head")
    count = len(group_of)
    for parts, group in zip(jobs, group_of):
        size = 1 << len(group)
        rows, d = parts[0].shape
        rows = rows // (size * count if joint else size)
        cut = (count, size, rows, d) if joint else (size, rows, d)
        args += [part.reshape(cut) for part in parts]
        outs += [shape(rows, d)] * size
    outs = outs * count if joint else outs

    def body(*refs):
        ins, results = list(refs[: len(args)]), list(refs[len(args) :])
        for m, group in enumerate(group_of):
            place = place_in(group, head_bits)
            if joint:
                first, *others = [ref.at[m] for ref in ins]
            else:
                first, *others = [ins.pop(0) for _ in jobs[m]]
            for n in range(1 << len(group)):
                total = first[place ^ n].astype(f32)
                for ref in others:
                    total += ref[place ^ n].astype(f32)
                results.pop(0)[...] = total.astype(bf16)

    blocks = list(kernel_call(body, name, outs, args, 8))
    return [[blocks.pop(0) for _ in range(1 << len(group))] for group in group_of]


def add_joint(jobs, group, name):
    head_bits = count_bits("head")
    size = 1 << len(group)
    rows, d = jobs[0][0].shape
    args = [part.reshape(size, rows // size, d) for parts in jobs for part in parts]

    def body(*refs):
        place = place_in(group, head_bits)
        ins, results = list(refs[: len(args)]), refs[len(args) :]
        for m, parts in enumerate(jobs):
            first, *others = [ins.pop(0) for _ in parts]
            for n in range(size):
                total = first[place ^ n].astype(f32)
                for ref in others:
                    total += ref[place ^ n].astype(f32)
                results[n][m] = total.astype(bf16)

    out = jax.ShapeDtypeStruct((len(jobs), rows // size, d), bf16)
    return list(kernel_call(body, name, [out] * size, args, 8))


def put_together(jobs, group_of, name):
    head_bits = count_bits("head")
    args = [part for parts in jobs for part in parts]
    outs = [
        jax.ShapeDtypeStruct((len(parts),) + parts[0].shape, parts[0].dtype) for parts in jobs
    ]

    def body(*refs):
        ins, results = list(refs[: len(args)]), refs[len(args) :]
        for parts, group, out in zip(jobs, group_of, results):
            place = place_in(group, head_bits)
            for n in range(len(parts)):
                out[place ^ n] = ins.pop(0)[...]

    joined = kernel_call(body, name, outs, args, 8)
    return [out.reshape(-1, out.shape[-1]) for out in joined]


def split_joint(parts, group, name):
    head_bits = count_bits("head")
    jobs, rows, d = parts[0].shape
    outs = [jax.ShapeDtypeStruct((len(parts), rows, d), bf16)] * jobs

    def body(*refs):
        place = place_in(group, head_bits)
        for m in range(jobs):
            for n in range(len(parts)):
                refs[len(parts) + m][place ^ n] = refs[n][m]

    joined = kernel_call(body, name, outs, parts, 8)
    return [out.reshape(-1, d) for out in joined]


def send_to(block, mask):
    devices = range(lax.axis_size("dp") * lax.axis_size("head"))
    return lax.ppermute(block, ("dp", "head"), [(i, i ^ mask) for i in devices])


def mask_of(group, n):
    return sum(1 << bit for m, bit in enumerate(group) if n >> m & 1)


def spread(blocks, group):
    return [blocks[0]] + [send_to(blocks[n], mask_of(group, n)) for n in range(1, len(blocks))]


def share(block, group):
    return [block] + [send_to(block, mask_of(group, n)) for n in range(1, 1 << len(group))]


def groups_of(at_once):
    bits = list(range(1, count_bits("dp") + count_bits("head")))
    plane = [1, count_bits("head")]
    rest = [bit for bit in bits if bit not in plane]
    return plane, [rest[n : n + at_once] for n in range(0, len(rest), at_once)]


AT_ONCE = (2, 1)
ORDER = (
    "xb", "L1", "mg", "sa", "L2", "M1", "sb", "L3", "M2", "eg", "L4", "E0",
    "T0", "T1", "S1", "E1", "J1", "L5", "S2", "J2", "J3", "L6", "J4", "T2",
    "J5", "J6", "L7", "Lo", "J7", "Jo",
)


class Sum:
    def __init__(self, send, keep, name, two, at_once):
        self.name, self.two = name, two
        self.plane, self.lines = groups_of(at_once)
        self.steps = 0
        self.jobs = [[keep, send_to(send, 1)]]

    def label(self):
        self.steps += 1
        return "%s_%d" % (self.name, self.steps)

    def tie(self, token):
        first = self.jobs[0][0]
        self.jobs[0][0] = lax.optimization_barrier((first, token))[0]

    def orders(self):
        a, b = self.plane
        return [[[a], [b]], [[b], [a]]] if self.two else [[self.plane]]

    def cut_plane(self, n):
        groups = [order[n] for order in self.orders()]
        blocks = add_up(self.jobs, groups, self.label(), self.two and n == 0)
        self.jobs = [spread(block, group) for block, group in zip(blocks, groups)]
        return blocks[0][0]

    def cut_line(self, n):
        jobs = self.jobs
        if n > 0:
            jobs = [[part.reshape(-1, part.shape[-1]) for part in jobs[0]]]
        blocks = add_joint(jobs, self.lines[n], self.label())
        self.jobs = [spread(blocks, self.lines[n])]
        return blocks[0]

    def sum_line(self):
        parts = self.jobs[0]
        whole = parts[0].shape
        flat = [part.reshape(-1, whole[-1]) for part in parts]
        total = add_up([flat], [[]], self.label())[0][0]
        self.jobs = [share(total.reshape(whole), self.lines[-1])]
        return total

    def join_line(self, n):
        if n == 0:
            self.jobs = [[part] for part in split_joint(self.jobs[0], self.lines[0], self.label())]
        else:
            self.jobs = [[put_together(self.jobs, [self.lines[n]], self.label())[0]]]
            whole = self.jobs[0][0]
            self.jobs = [share(whole.reshape(len(self.orders()), -1, whole.shape[-1]), self.lines[n - 1])]
            return whole
        groups = [order[-1] for order in self.orders()]
        token = self.jobs[0][0]
        self.jobs = [share(job[0], group) for job, group in zip(self.jobs, groups)]
        return token

    def join_plane(self, n):
        groups = [order[n] for order in self.orders()]
        wholes = put_together(self.jobs, groups, self.label())
        if n > 0:
            groups = [order[n - 1] for order in self.orders()]
            self.jobs = [share(whole, group) for whole, group in zip(wholes, groups)]
        else:
            self.own = wholes
            self.got = [send_to(whole, 1) for whole in wholes]
        return wholes[0]


class Joint:
    def __init__(self, halves, whole):
        self.jobs = [*halves.jobs, whole.jobs[0]]
        self.plane, self.lines = halves.plane, halves.lines
        self.name, self.steps = "joint", 0
        self.rows = whole.jobs[0][0].shape[0]

    tie, label = Sum.tie, Sum.label
    cut_line, sum_line = Sum.cut_line, Sum.sum_line

    def join_line(self, n):
        if n > 0:
            whole = put_together(self.jobs, [self.lines[n]], self.label())[0]
            whole = whole.reshape(3, -1, whole.shape[-1])
            self.jobs = [share(whole, self.lines[n - 1])]
            return whole
        parts = self.jobs[0]
        head_bits = count_bits("head")
        members = len(parts)
        _, rows, d = parts[0].shape
        most = members * rows
        group = self.lines[0]

        def body(*refs):
            place = place_in(group, head_bits)
            sorted_ref = refs[-1]
            for m in range(3):
                for n in range(members):
                    at = pl.multiple_of((place ^ n) * rows, rows)
                    to = refs[members + m] if m < 2 else sorted_ref
                    to[pl.ds(at, rows)] = refs[n][m]
            for m in range(2):
                refs[members + m][most:] = sorted_ref[m * most // 2 : (m + 1) * most // 2]

        outs = [shape(most + most // 2, d)] * 2
        scratch = [pltpu.VMEM((most, d), bf16)]
        wholes = kernel_call(body, self.label(), outs, parts, 8, scratch=scratch)
        a, b = self.plane
        self.orders = [[[a], [b]], [[b], [a]]]
        self.jobs = [share(whole, order[1]) for whole, order in zip(wholes, self.orders)]
        return wholes[0]

    def join_plane(self, n):
        wholes = put_together(self.jobs, [order[n] for order in self.orders], self.label())
        if n > 0:
            self.jobs = [share(w, order[0]) for w, order in zip(wholes, self.orders)]
        else:
            self.own = wholes
            self.got = [send_to(whole, 1) for whole in wholes]
        return wholes[0]

    def homes(self):
        most = self.rows
        homes = []
        for part in range(2):
            for first in range(2):
                for second in range(2):
                    at = (2 * first + second) * (most + most // 2)
                    row = part * 4 * most + (2 * first + second) * most
                    homes.append((part, at, 0, row, most))
                    x, y = (first, second) if part == 0 else (second, first)
                    row = (x + 2 * y) * most + part * most // 2
                    homes.append((part, at + most, 1, row, most // 2))
        return homes


def cast_outputs(total, homes, lengths, shapes, pieces, name, small=(), sums=None):
    args = [*total.own, *total.got]
    count = len(total.own)
    d = total.own[0].shape[1]

    def body(*refs):
        core = core_index()
        outs, rest = refs[len(args) : len(args) + len(shapes)], refs[len(args) + len(shapes) :]
        small_refs, rest = rest[: len(small)], rest[len(small) :]
        held, ready, sems = rest[: len(shapes)], rest[len(shapes) : -1], rest[-1]
        copies = []
        for part, at, which, row, size in homes:
            mine, other = refs[part][at : at + size], refs[count + part][at : at + size]
            to = slice(row, row + size)
            ready[which][0, to] = jnp.where(core == 0, mine, other)
            ready[which][1, to] = jnp.where(core == 0, other, mine)
        for which, side, start, size, n, place, turned in pieces:
            block = ready[which][side, start : start + size]
            to = pl.ds(place, size)
            if turned:
                index = (slice(None), to)
                held[n][index] = block.T.astype(f32)
            else:
                index = (to, slice(None))
                held[n][index] = block.astype(f32)
            copies.append(
                pltpu.make_async_copy(
                    held[n].at[index], outs[n].at[index], sems.at[len(copies)]
                )
            )
            copies[-1].start()
        if sums is not None:
            sums(ready, small_refs)
        for copy in copies:
            copy.wait()

    scratch = [pltpu.VMEM(s.shape, f32) for s in shapes]
    scratch += [pltpu.VMEM((2, rows, d), bf16) for rows in lengths]
    scratch.append(pltpu.SemaphoreType.DMA((len(pieces),)))
    outs = [ANY] * len(shapes) + [VMEM] * len(small)
    mib = 14 + sum(s.shape[0] * s.shape[1] * 4 for s in shapes) // 2**20
    return kernel_call(body, name, [*shapes, *small], args, mib, None, outs, scratch)


def late_outputs(total, d, ff):
    half, size = ff // 2, d // 2
    rows = total.own[0].shape[0]
    pieces = []
    for side in range(2):
        for start in range(0, d, size):
            pieces.append((0, side, start, size, 0, side * d + start, False))
        for start in range(0, half, size):
            pieces.append((0, side, d + start, size, 1, side * half + start, False))
            pieces.append((0, side, d + half + start, size, 2, side * half + start, True))
    shapes = [shape(2 * d, d, f32), shape(ff, d, f32), shape(d, ff, f32)]
    homes = [(part, 0, 0, part * rows, rows) for part in range(2)]
    return cast_outputs(total, homes, [2 * rows], shapes, pieces, "late_outputs")


def joint_outputs(total, d, count):
    half = d // 2
    pieces = []
    for side in range(2):
        for n in range(3):
            pieces.append((1, side, n * half, half, 4, n * d + side * half, True))
        pieces.append((0, side, 0, half, 0, side * half, False))
        pieces.append((0, side, half, half, 1, side * half, True))
        pieces.append((0, side, d, half, 2, side * d, True))
        pieces.append((0, side, d + half, half, 2, side * d + half, True))
        pieces.append((0, side, 2 * d, half, 3, side * half, False))
    shapes = [shape(d, d, f32), shape(d, d, f32), shape(d, 2 * d, f32), shape(d, d, f32)]
    shapes.append(shape(d, 3 * d, f32))
    lengths = [3 * d, 3 * half]

    def sums(ready, outs):
        rows = ready[0][0, 2 * d + half : 2 * d + half + PAIR].astype(f32)
        outs[0][...] = jnp.concatenate([rows[n : n + 1] for n in range(count)], axis=1)
        for n in range(2):
            outs[1 + n][...] = rows[count + n : count + n + 1]
            outs[3 + n][...] = rows[count + 2 + 3 * n : count + 5 + 3 * n]

    small = [shape(1, count * d, f32), shape(1, d, f32), shape(1, d, f32)]
    small += [shape(3, d, f32), shape(3, d, f32)]
    homes = total.homes()
    return cast_outputs(total, homes, lengths, shapes, pieces, "joint_outputs", small, sums)


def swap(block, axis, bit):
    devices = range(lax.axis_size(axis))
    return lax.ppermute(block, axis, [(i, i ^ bit) for i in devices])


def after(value, *tokens):
    return lax.optimization_barrier((value, *tokens))[0]


def shifted(block, axis, distance):
    devices = range(lax.axis_size(axis))
    route = [(i - distance, i) for i in devices if i - distance in devices]
    return lax.ppermute(block, axis, route)


def normed(values):
    centred = values - jnp.mean(values, axis=-1, keepdims=True)
    spread = jnp.mean(centred * centred, axis=-1, keepdims=True)
    inverse = lax.rsqrt(spread + epsilon)
    return centred * inverse, inverse


def shards(
    tokens,
    memory,
    lengths,
    self_qkv,
    self_out,
    cross_q,
    cross_kv,
    cross_out,
    ffn_in,
    ffn_in_bias,
    ffn_out,
    ffn_out_bias,
    slot_weight,
    slot_bias,
    norm_gain,
    norm_shift,
    cotangent,
):
    tokens, memory, cotangent, length = tokens[0], memory[0], cotangent[0], lengths[0]
    rows, d = tokens.shape
    ff = ffn_in.shape[1]
    me = lax.axis_index("head")

    other_tokens, facing_tokens = swap(tokens, "head", 1), swap(tokens, "head", 2)
    local = jnp.arange(rows, dtype=jnp.int32)
    positions = me * rows + local
    live_slots = (positions < length - 1)[:, None]
    extra_index = jnp.arange(HEAD_DIM)[:, None]
    ones_rows = ((extra_index >= 1) & (extra_index <= 3)).astype(f32)

    def extra_of(members):
        key_positions = jnp.concatenate([(me ^ n) * rows + local for n in members])
        dead = (key_positions >= length)[None, :]
        return jnp.where((extra_index == 0) & dead, masked_score, ones_rows).astype(bf16)

    near_extra, far_extra = extra_of((0, 1)), extra_of((2, 3))
    cross_extra = jnp.broadcast_to(ones_rows, (HEAD_DIM, 4 * memory.shape[0])).astype(bf16)

    q_t, *near_keyed, near_sums = attend_near(tokens, other_tokens, self_qkv, near_extra)
    cotangent = after(cotangent, near_sums)
    slot_grad = jnp.where(live_slots, cotangent, 0.0).astype(bf16)
    before = shifted(slot_grad[-1:], "head", 1)
    slot_grads = jnp.stack([slot_grad, jnp.concatenate([before, slot_grad[:-1]], axis=0)])
    third_grad = dot(slot_grads[0], slot_weight[:d], 1, 1) + dot(
        slot_grads[1], slot_weight[d:], 1, 1
    )
    grad_slot_bias = jnp.sum(slot_grad.astype(f32), axis=0, keepdims=True)

    facing_tokens = after(facing_tokens, third_grad)
    token_blocks = (tokens, other_tokens, facing_tokens, swap(facing_tokens, "head", 1))
    facing_memory = swap(after(memory, facing_tokens), "head", 2)
    *far_keyed, context, queries = attend_far(
        *token_blocks[2:], self_qkv, q_t, near_keyed, near_sums, near_extra, far_extra
    )
    facing_memory = after(facing_memory, queries)
    memory_blocks = (
        memory,
        swap(memory, "head", 1),
        facing_memory,
        swap(facing_memory, "head", 1),
    )
    first_in = tokens.astype(f32) + dot(context, self_out)
    first_norm = normed(first_in)[0] * norm_gain[0] + norm_shift[0]
    first_low = first_norm.astype(bf16)

    mem_k, mem_v, cross_context, cross_queries = attend_memory(
        memory_blocks, cross_kv, first_low, cross_q, cross_extra
    )
    third_low, second_in_grad, cross_branch, cross_grad, late_sums, in_bias, *late_grads = (
        feed_forward(
            cross_context,
            first_norm,
            third_grad,
            slot_grads,
            (cross_out, ffn_in, ffn_out),
            (ffn_in_bias[None], ffn_out_bias[None]),
            norm_gain,
            norm_shift,
        )
    )
    late = Sum(*late_grads, "late", True, AT_ONCE[0])
    heads = d // HEAD_DIM
    keyed = [(*near_keyed, near_extra), (*far_keyed, far_extra)]
    made = {}
    state = {"token": late_grads[0]}

    def later(value):
        return after(value, state["token"])

    def cross_backward():
        attention = attend_backward(
            cross_queries,
            [(mem_k, mem_v, cross_extra)],
            cross_context,
            later(cross_grad),
            0,
            heads,
        )
        *made["cross"], grad, made["branch"], made["back"], made["early_sums"] = run(
            "cross_backward",
            cross_and_first_backward(
                attention, second_in_grad, first_in, norm_gain[:1], cross_q, self_out
            ),
        )
        made["first"] = grad
        return grad

    def middle_part():
        cross_dq, mem_dk, mem_dv = made["cross"]
        send, keep = middle_grads(
            cross_context,
            cross_branch,
            cross_dq,
            first_low,
            mem_dk,
            mem_dv,
            memory_blocks,
            context,
            made["branch"],
            (in_bias, later(late_sums), made["early_sums"], grad_slot_bias),
        )
        made["M"] = Sum(send, keep, "middle", True, AT_ONCE[1])
        return send

    def self_backward(n):
        half = heads // 2
        made["self", n] = run(
            "self_backward",
            attend_backward(queries, keyed, context, later(made["back"]), n * half, half),
        )
        return made["self", n][0]

    def early_part():
        dqs, dks, dvs = zip(made["self", 0], made["self", 1])
        _, mem_dk, mem_dv = made["cross"]
        send, keep, near, facing, other = run(
            "early_grads",
            early_grads(dqs, dks, dvs, (later(tokens), *token_blocks[1:])),
            project_back([(dks, dvs), ((mem_dk,), (mem_dv,))], [self_qkv, cross_kv]),
        )
        made["parts"] = send, keep, near, facing, other
        return send

    def send_early():
        send, keep, _, _, _ = made["parts"]
        send = later(send)
        made["E"] = Sum(send, keep, "early", False, AT_ONCE[1])
        return send

    def send_inputs():
        _, _, near, facing, other = made["parts"]
        other = later(other)
        got = send_to(other, 1)
        made["near"] = near.astype(f32) + got[: near.shape[0]].astype(f32)
        made["facing"] = [facing, got[near.shape[0] :]]
        return other

    def send_facing():
        facing, got = made["facing"]
        facing = add_up([[facing, later(got)]], [[]], "facing")[0][0]
        made["got"] = send_to(facing, 2)
        return facing

    def send_first_row():
        first = later(third_low[:1])
        made["arriving"] = shifted(first, "head", -1)
        return first

    def slots_done():
        following = jnp.concatenate([third_low[1:], later(made["arriving"])], axis=0)
        slot_pre = (
            dot(third_low, slot_weight[:d])
            + dot(following, slot_weight[d:])
            + slot_bias.astype(f32)
        )
        made["slots"] = jnp.where(live_slots, slot_pre, 0.0).astype(bf16)
        return made["slots"]

    def inputs_done():
        near = made["near"] + later(made["got"]).astype(f32)
        total = made["first"] + near[:rows]
        for n in range(2):
            part = made["self", n][0]
            size = part.shape[0]
            total = total + dot(part, self_qkv[:, n * size : (n + 1) * size], 0, 1)
        made["token_grad"] = total.astype(bf16)
        made["memory_grad"] = near[rows:].astype(bf16)
        return made["token_grad"]

    made["L"] = late
    def along(count, usual):
        lines = list(range(count))
        cuts = [lines[n : n + 1] for n in range(usual - 1)] + [lines[usual - 1 :]]
        steps = [[("cut_line", n) for n in cut] for cut in cuts] + [[("sum_line", None)]]
        return steps + [[("join_line", n) for n in reversed(cut)] for cut in reversed(cuts)]

    across = [[("cut_plane", 0)], [("cut_plane", 1)]]
    back = [[("join_plane", 1)], [("join_plane", 0)]]
    late_along = along(len(late.lines), 2 // AT_ONCE[0])
    joint_along = along(len(groups_of(AT_ONCE[1])[1]), 2 // AT_ONCE[1])
    steps = {"L": across + late_along + back, "M": across, "E": across[:1]}
    steps["J"] = joint_along + back

    parts = {
        "xb": cross_backward,
        "mg": middle_part,
        "sa": lambda: self_backward(0),
        "sb": lambda: self_backward(1),
        "eg": early_part,
        "E0": send_early,
        "T0": send_inputs,
        "T1": send_facing,
        "T2": inputs_done,
        "S1": send_first_row,
        "S2": slots_done,
    }

    def outputs(name):
        total = made[name]
        total.own[0] = later(total.own[0])
        if name == "L":
            made["late"] = late_outputs(total, d, ff)
            return made["late"][0]
        made["joint"] = joint_outputs(total, d, ff // d)
        return made["joint"][0]

    for name in ORDER:
        if name in parts:
            state["token"] = parts[name]()
        elif name[1] == "o":
            state["token"] = outputs(name[0])
        else:
            if name == "J1":
                made["J"] = Joint(made["M"], made["E"])
            total = made[name[0]]
            for step, n in steps[name[0]][int(name[1]) - 1]:
                total.tie(state["token"])
                state["token"] = getattr(total, step)(*([] if n is None else [n]))
    grad_cross_out, grad_cross_q, grad_cross_kv, grad_self_out, grad_self_qkv, *sums = made["joint"]
    grad_in_bias, grad_out_bias, grad_slot_bias, norm_gain_grad, norm_shift_grad = sums
    grad_slot_weight, grad_ffn_out, grad_ffn_in = made["late"]
    token_grad, memory_grad = made["token_grad"], made["memory_grad"]
    return (
        made["slots"][None],
        token_grad[None],
        memory_grad[None],
        grad_self_qkv,
        grad_self_out,
        grad_cross_q,
        grad_cross_kv,
        grad_cross_out,
        grad_ffn_in,
        grad_in_bias[0],
        grad_ffn_out,
        grad_out_bias[0],
        grad_slot_weight,
        grad_slot_bias[0],
        norm_gain_grad,
        norm_shift_grad,
    )


def solution(mesh):
    split = P("dp", "head", None)
    return jax.shard_map(
        shards,
        mesh=mesh,
        in_specs=(split, split, P("dp")) + (P(),) * 13 + (split,),
        out_specs=(split,) * 3 + (P(),) * 13,
        check_vma=False,
    )
```
